32 devices in a mesh: section: 4 (over y, x), dp: 8 (over z, core).
Axes of the slice: x: 2, y: 2, z: 4, core: 2. Of those that a mesh axis runs over, the one named last changes fastest.
Arguments:
- token_ids: int32 [64, 256], P('dp'), may hold values from 0 to 26
- timesteps: int32 [64], P('dp'), may hold values from 0 to 999
- token_table: bfloat16 [27, 768], replicated, may hold values from -6 to 6
- time_table: bfloat16 [1000, 768], replicated, may hold values from -3 to 3
- attn_gain: bfloat16 [4, 384], P('section'), may hold values from 0.5 to 1.5
- attn_shift: bfloat16 [4, 384], P('section'), may hold values from -1 to 1
- qkv_weight: bfloat16 [4, 384, 2304], P('section'), may hold values from -0.21875 to 0.21875
- query_bias: bfloat16 [4, 384], P('section'), may hold values from -2.5 to 2.5
- value_bias: bfloat16 [4, 384], P('section'), may hold values from -1.5 to 1.5
- proj_weight: bfloat16 [4, 384, 768], P('section'), may hold values from -1.75 to 1.75
- proj_bias: bfloat16 [4, 384], P('section'), may hold values from -1 to 1
- mlp_gain: bfloat16 [4, 384], P('section'), may hold values from 0.5 to 1.5
- mlp_shift: bfloat16 [4, 384], P('section'), may hold values from -1 to 1
- up_weight: bfloat16 [4, 384, 3072], P('section'), may hold values from -0.21875 to 0.21875
- up_bias: bfloat16 [4, 1536], P('section'), may hold values from -2.5 to 2.5
- down_weight: bfloat16 [4, 1536, 768], P('section'), may hold values from -0.109375 to 0.109375
- down_bias: bfloat16 [4, 384], P('section'), may hold values from -1 to 1
- cotangent: bfloat16 [64, 256, 768], P('dp'), may hold values from -6 to 6
Outputs:
- activations: float32 [64, 256, 768], P('dp', None, 'section')
- token_table_grad: float32 [27, 768], P(None, 'section')
- time_table_grad: float32 [1000, 768], P(None, 'section')
- attn_gain_grad: float32 [4, 384], P('section', 'dp')
- attn_shift_grad: float32 [4, 384], P('section', 'dp')
- qkv_weight_grad: float32 [4, 384, 2304], P('section', 'dp')
- query_bias_grad: float32 [4, 384], P('section', 'dp')
- value_bias_grad: float32 [4, 384], P('section', 'dp')
- proj_weight_grad: float32 [4, 384, 768], P('section', 'dp')
- proj_bias_grad: float32 [4, 384], P('section', 'dp')
- mlp_gain_grad: float32 [4, 384], P('section', 'dp')
- mlp_shift_grad: float32 [4, 384], P('section', 'dp')
- up_weight_grad: float32 [4, 384, 3072], P('section', 'dp')
- up_bias_grad: float32 [4, 1536], P('section', 'dp')
- down_weight_grad: float32 [4, 1536, 768], P('section', 'dp')
- down_bias_grad: float32 [4, 384], P('section', 'dp')
The draws below stay inside these ranges and needn't reach their ends.
Inputs may be any that keep to these rules, and one draw needn't show every extreme that they name: `timesteps`: a row of time_table for each sequence.
All inputs are finite; a program needn't handle non-finite values.
Results may differ from the reference program's by a relative error of at most 0.014.
Values may be sent and summed in bfloat16 or wider, within the bound.
A program may use at most 192 MiB of HBM per device.

```python
import math
import jax
import jax.numpy as jnp
import numpy as np
from jax import lax

D = 768
HEADS = 12
FF = 3072
VOCAB = 27
TSTEPS = 1000
SEQ = 256
HALF = 384
FF_HALF = 1536
LAYERS = 2
ROWS = 64
N_SECTION = 4


def touch_ends(values, key, least, high):
    dims = values.shape
    place = [jax.random.randint(jax.random.fold_in(key, axis), (), 0, dims[axis]) for axis in range(len(dims))]
    values = values.at[tuple(place)].set(least)
    longest = dims.index(max(dims))
    place[longest] = (place[longest] + 1) % dims[longest]
    return values.at[tuple(place)].set(high)


def shard_levels(stream_key, extent, split, least, high):
    def one(dim, blocks):
        draws = jax.random.uniform(jax.random.fold_in(jax.random.fold_in(stream_key, 6), dim), (blocks,), jnp.float32, least / len(split), high / len(split))
        return jnp.repeat(jnp.exp(draws), extent[dim] // blocks).reshape((-1,) + (1,) * (len(extent) - dim - 1))

    level = one(*split[0])
    for cut in split[1:]:
        level = level * one(*cut)
    return level


def cumulative_ranks(amount, slope):
    portions = [(1 << 20) // math.isqrt(grade ** slope) + 1 for grade in range(1, amount + 1)]
    scale = 1 + sum(portions) // (1 << 30)
    return np.cumsum(np.array([max(1, weight // scale) for weight in portions]))


def ranked_ids(key, extent, amount, slope):
    grid = cumulative_ranks(amount, slope)
    lot = jax.random.randint(jax.random.fold_in(key, 1), extent, 0, int(grid[amount - 1]))
    standing = jnp.searchsorted(jnp.asarray(grid, jnp.int32), lot, side="right")
    return jax.random.permutation(jax.random.fold_in(key, 2), amount)[standing].astype(jnp.int32)


def bell_draw(key, dims, scale, bound, cuts=(), dtype=jnp.bfloat16):
    entries = scale * jax.random.normal(key, dims, jnp.float32)
    if cuts:
        entries = entries * shard_levels(key, dims, cuts, -0.22, 0.18)
    return jnp.clip(entries, -bound, bound).astype(dtype)


def setup_inputs(seed: int = 0) -> dict:
    splits = jax.random.split(jax.random.key(seed), 19)
    return {
        "token_ids": touch_ends(ranked_ids(splits[0], (ROWS, SEQ), VOCAB, 1), jax.random.fold_in(splits[0], 3), 0, VOCAB - 1).astype(jnp.int32),
        "timesteps": touch_ends(jax.random.randint(splits[1], (ROWS,), 0, TSTEPS), jax.random.fold_in(splits[1], 1), 0, TSTEPS - 1).astype(jnp.int32),
        "token_table": bell_draw(splits[2], (VOCAB, D), 1.0, 6.0),
        "time_table": bell_draw(splits[3], (TSTEPS, D), 0.5, 3.0),
        "attn_gain": jnp.clip(1.0 + 0.1 * jax.random.normal(splits[4], (N_SECTION, HALF), jnp.float32), 0.5, 1.5).astype(jnp.bfloat16),
        "attn_shift": bell_draw(splits[5], (N_SECTION, HALF), 0.2, 1.0, ((0, 4),)),
        "qkv_weight": bell_draw(splits[6], (N_SECTION, HALF, 3 * D), D ** -0.5, 0.21875, ((0, 4),)),
        "query_bias": bell_draw(splits[7], (N_SECTION, HALF), 0.5, 2.5, ((0, 4),)),
        "value_bias": bell_draw(splits[8], (N_SECTION, HALF), 0.3, 1.5, ((0, 4),)),
        "proj_weight": bell_draw(splits[9], (N_SECTION, HALF, D), (max(D // 64, 1)) ** -0.5, 1.75, ((0, 4),)),
        "proj_bias": bell_draw(splits[10], (N_SECTION, HALF), 0.2, 1.0, ((0, 4),)),
        "mlp_gain": jnp.clip(1.0 + 0.1 * jax.random.normal(splits[11], (N_SECTION, HALF), jnp.float32), 0.5, 1.5).astype(jnp.bfloat16),
        "mlp_shift": bell_draw(splits[12], (N_SECTION, HALF), 0.2, 1.0, ((0, 4),)),
        "up_weight": bell_draw(splits[13], (N_SECTION, HALF, FF), D ** -0.5, 0.21875, ((0, 4),)),
        "up_bias": bell_draw(splits[14], (N_SECTION, FF_HALF), 0.5, 2.5, ((0, 4),)),
        "down_weight": bell_draw(splits[15], (N_SECTION, FF_HALF, D), FF ** -0.5, 0.109375, ((0, 4),)),
        "down_bias": bell_draw(splits[16], (N_SECTION, HALF), 0.2, 1.0, ((0, 4),)),
        "cotangent": bell_draw(splits[17], (ROWS, SEQ, D), 1.0, 6.0, ((0, 8),)),
    }


EPS = 1e-05
HIGHEST = lax.Precision.HIGHEST

@jax.custom_vjp
def low(v):
    return lax.optimization_barrier(v.astype(jnp.bfloat16)).astype(jnp.float32)

@jax.custom_vjp
def low_back(v):
    return v

def low_keep(v):
    return (low(v), None)

def low_pass(kept, grad):
    return (grad,)

def back_keep(v):
    return (v, None)

def back_low(kept, grad):
    return (low(grad),)
low.defvjp(low_keep, low_pass)
low_back.defvjp(back_keep, back_low)

def layer_norm(inputs, gain, shift):
    mean = lax.optimization_barrier(jnp.mean(inputs, axis=-1, keepdims=True))
    centered = inputs - mean
    spread = lax.optimization_barrier(jnp.mean(centered * centered, axis=-1, keepdims=True))
    return centered * lax.rsqrt(spread + EPS) * gain + shift

def attend(inputs, gain, shift, w_joint, b_query, b_value, w_proj, b_proj):
    batch, length, width = inputs.shape
    size = width // HEADS
    scale = 1.0 / math.sqrt(size)
    normal = low(layer_norm(inputs, gain, shift))
    joint = jnp.einsum('bld,de->ble', normal, w_joint, precision=HIGHEST)
    query = low_back(low(joint[..., :width] + b_query)).reshape(batch, length, HEADS, size)
    keys = low_back(low(joint[..., width:2 * width])).reshape(batch, length, HEADS, size)
    values = low_back(low(joint[..., 2 * width:] + b_value)).reshape(batch, length, HEADS, size)
    scores = low_back(jnp.einsum('bqhd,bkhd->bhqk', query, keys, precision=HIGHEST) * scale)
    largest = lax.optimization_barrier(jnp.max(scores, axis=-1, keepdims=True))
    expo = jnp.exp(scores - largest)
    probs = expo / lax.optimization_barrier(jnp.sum(expo, axis=-1, keepdims=True))
    mixed = jnp.einsum('bhqk,bkhd->bqhd', low(probs), values, precision=HIGHEST).reshape(batch, length, width)
    mixed = low_back(low(mixed))
    branch = low_back(jnp.einsum('bld,de->ble', mixed, w_proj, precision=HIGHEST) + b_proj)
    return inputs + branch

def feed(inputs, gain, shift, w_up, b_up, w_down, b_down):
    normal = low(layer_norm(inputs, gain, shift))
    before = low_back(jnp.einsum('bld,df->blf', normal, w_up, precision=HIGHEST) + b_up)
    after = low(jax.nn.gelu(before, approximate=True))
    branch = low_back(jnp.einsum('blf,fd->bld', after, w_down, precision=HIGHEST) + b_down)
    return inputs + branch

def network(token_rows, time_rows, token_table, time_table, attn, mlp):
    state = jnp.take(token_table, token_rows, axis=0) + jnp.take(time_table, time_rows, axis=0)[:, None, :]
    for layer in range(LAYERS):
        if layer > 0:
            state = low_back(low(state))
        state = attend(state, *[weight[layer] for weight in attn])
        state = low_back(low(state))
        state = feed(state, *[weight[layer] for weight in mlp])
    return state

def joined(piece):
    whole = piece.astype(jnp.float32)
    return whole.reshape((LAYERS, 2 * whole.shape[1]) + whole.shape[2:])

def parted(grad):
    return grad.reshape((2 * LAYERS, grad.shape[1] // 2) + grad.shape[2:])

def reference(token_ids, timesteps, token_table, time_table, attn_gain, attn_shift, qkv_weight, query_bias, value_bias, proj_weight, proj_bias, mlp_gain, mlp_shift, up_weight, up_bias, down_weight, down_bias, cotangent):
    attn = tuple((joined(weight) for weight in (attn_gain, attn_shift, qkv_weight, query_bias, value_bias, proj_weight, proj_bias)))
    mlp = tuple((joined(weight) for weight in (mlp_gain, mlp_shift, up_weight, up_bias, down_weight, down_bias)))
    token_float = token_table.astype(jnp.float32)
    time_float = time_table.astype(jnp.float32)
    rows, length = token_ids.shape
    width = cotangent.shape[2]
    group = math.gcd(rows, 16)
    count = rows // group
    id_groups = token_ids.reshape(count, group, length)
    time_groups = timesteps.reshape(count, group)
    seed_groups = cotangent.reshape(count, group, length, width)

    def visit(totals, pieces):
        id_rows, time_rows, seed_rows = pieces

        def forward(token_part, time_part, attn_part, mlp_part):
            return network(id_rows, time_rows, token_part, time_part, attn_part, mlp_part)
        result, pull = jax.vjp(forward, token_float, time_float, attn, mlp)
        grads = pull(seed_rows.astype(jnp.float32))
        return (jax.tree.map(jnp.add, totals, grads), result)
    start = jax.tree.map(jnp.zeros_like, (token_float, time_float, attn, mlp))
    totals, results = lax.scan(visit, start, (id_groups, time_groups, seed_groups))
    token_grad, time_grad, attn_grads, mlp_grads = totals
    activations = results.reshape(rows, length, width)
    return (activations, token_grad, time_grad, parted(attn_grads[0]), parted(attn_grads[1]), parted(attn_grads[2]), parted(attn_grads[3]), parted(attn_grads[4]), parted(attn_grads[5]), parted(attn_grads[6]), parted(mlp_grads[0]), parted(mlp_grads[1]), parted(mlp_grads[2]), parted(mlp_grads[3]), parted(mlp_grads[4]), parted(mlp_grads[5]))
```

```python
import functools
import math

import jax
import jax.numpy as jnp
from jax import lax
from jax.experimental import pallas as pl
from jax.experimental.pallas import tpu as pltpu
from jax.sharding import PartitionSpec as P

HEADS = 12
EPS = 1e-05
HIGHEST = lax.Precision.HIGHEST
MESH = pl.DeviceIdType.MESH
BF = jnp.bfloat16
F32 = jnp.float32
TILES = 12
QKV, PROJ, UP, DOWN = 0, 3, 4, 8
GELU_A = math.sqrt(2.0 / math.pi)
GELU_B = 0.044715


def flipped(value, bit):
    mask = 2**bit
    return value + mask - 2 * mask * lax.rem(lax.div(value, mask), 2)


def mul(a, b):
    return lax.dot_general(a, b, (((1,), (0,)), ((), ())), preferred_element_type=F32)


def mul_nt(a, b):
    return lax.dot_general(a, b, (((1,), (1,)), ((), ())), preferred_element_type=F32)


def mul_tn(a, b):
    return lax.dot_general(a, b, (((0,), (0,)), ((), ())), preferred_element_type=F32)


def normalize(x):
    mean = jnp.mean(x, axis=-1, keepdims=True)
    centered = x - mean
    spread = jnp.mean(centered * centered, axis=-1, keepdims=True)
    rate = lax.rsqrt(spread + EPS)
    return centered * rate, rate


def scaled_back(gh, gain, n, rate):
    gn = gh * gain
    inner = jnp.mean(gn * n, axis=-1, keepdims=True)
    return (gn - jnp.mean(gn, axis=-1, keepdims=True) - n * inner) * rate


def column(values):
    return jnp.sum(values, axis=0, keepdims=True)


def pipeline_kernel(
    seqs,
    length,
    width,
    qkv_in,
    proj_in,
    up_in,
    down_in,
    vec_in,
    ids_in,
    table_in,
    time_in,
    cot_in,
    act_out,
    small_out,
    table_out,
    fixed_out,
    moving_out,
    w,
    vecs,
    par,
    xs,
    n_a,
    n_f,
    r_a,
    r_f,
    qkv,
    probs,
    y1,
    slope,
    gate,
    h_s,
    o_s,
    hf_s,
    gq_s,
    g1,
    go_s,
    acc,
    ybuf,
    ysend,
    gsum,
    tsum,
    own_sem,
    x_send,
    x_recv,
    z_send,
    z_recv,
    c1_send,
    c1_recv,
    c2_send,
    c2_recv,
    y_send,
    y_recv,
    v_sem,
    cot_sem,
    act_sem,
    keep_sem,
    last_sem,
):
    s = lax.axis_index("section")
    d = lax.axis_index("dp")
    stage = lax.div(s, 2)
    part = lax.rem(s, 2)
    other = 1 - part
    x_dev = (flipped(s, 0), d)
    y_dev = (flipped(s, 1), d)
    z_dev = (s, flipped(d, 1))
    c_dev = (s, flipped(d, 0))
    half = width // 2
    quarter = half // 4
    hidden_half = up_in.shape[2] // 2
    mine = lax.rem(d, 4)
    across = flipped(mine, 1)
    scale = 1.0 / math.sqrt(width // HEADS)
    letters_count = table_in.shape[0]

    barrier = pltpu.get_barrier_semaphore()
    for device in (x_dev, y_dev, z_dev, c_dev):
        pl.semaphore_signal(barrier, inc=1, device_id=device, device_id_type=MESH)

    own_rows = pl.ds(pl.multiple_of(part * half, 16), half)

    def own_copies(tile):
        if tile < PROJ:
            pairs = [(qkv_in.at[0, :, pl.ds(tile * width, width)], w.at[tile, own_rows])]
        elif tile < UP:
            pairs = [(proj_in.at[0], w.at[tile, own_rows])]
        elif tile < DOWN:
            pairs = [
                (
                    up_in.at[0, :, pl.ds(side * hidden_half + (tile - UP) * half, half)],
                    w.at[tile, own_rows, pl.ds(side * half, half)],
                )
                for side in range(2)
            ]
        else:
            pairs = [(down_in.at[0, pl.ds((tile - DOWN) * half, half)], w.at[tile, own_rows])]
        return [
            pltpu.make_async_copy(src, dst, own_sem.at[2 * tile + k]) for k, (src, dst) in enumerate(pairs)
        ]

    def x_copy(tile):
        rows = pl.ds(pl.multiple_of(part * half + mine * quarter, 16), quarter)
        return pltpu.make_async_remote_copy(
            src_ref=w.at[tile, rows],
            dst_ref=w.at[tile, rows],
            send_sem=x_send.at[tile],
            recv_sem=x_recv.at[tile],
            device_id=x_dev,
            device_id_type=MESH,
        )

    def relay(tile, which, send, recv, device):
        rows = pl.ds(pl.multiple_of(other * half + which * quarter, 16), quarter)
        return pltpu.make_async_remote_copy(
            src_ref=w.at[tile, rows],
            dst_ref=w.at[tile, rows],
            send_sem=send.at[tile],
            recv_sem=recv.at[tile],
            device_id=device,
            device_id_type=MESH,
        )

    def z_copy(tile):
        return relay(tile, mine, z_send, z_recv, z_dev)

    def c1_copy(tile):
        return relay(tile, mine, c1_send, c1_recv, c_dev)

    def c2_copy(tile):
        return relay(tile, across, c2_send, c2_recv, c_dev)

    def x_arrival(tile):
        return relay(tile, mine, x_send, x_recv, x_dev)

    def z_arrival(tile):
        return relay(tile, across, z_send, z_recv, z_dev)

    def c1_arrival(tile):
        return relay(tile, flipped(mine, 0), c1_send, c1_recv, c_dev)

    def c2_arrival(tile):
        return relay(tile, flipped(across, 0), c2_send, c2_recv, c_dev)

    def vec_copy(which):
        return pltpu.make_async_remote_copy(
            src_ref=vecs.at[which],
            dst_ref=vecs.at[which],
            send_sem=v_sem.at[1],
            recv_sem=v_sem.at[2],
            device_id=x_dev,
            device_id_type=MESH,
        )

    def pass_first(tile):
        x_arrival(tile).wait_recv()
        z_copy(tile).start()
        c1_copy(tile).start()

    def pass_second(tile):
        z_arrival(tile).wait_recv()
        c2_copy(tile).start()

    def ready(tile):
        c1_arrival(tile).wait_recv()
        c2_arrival(tile).wait_recv()

    vec_own = pltpu.make_async_copy(vec_in, vecs.at[part], v_sem.at[0])
    vec_own.start()
    for tile in range(TILES):
        for copy in own_copies(tile):
            copy.start()
    gsum[...] = jnp.zeros_like(gsum)
    tsum[...] = jnp.zeros_like(tsum)
    vec_own.wait()
    pl.semaphore_wait(barrier, 4)
    vec_copy(part).start()
    for tile in range(TILES):
        for copy in own_copies(tile):
            copy.wait()
        x_copy(tile).start()

    pass_first(0)
    pass_first(1)
    pass_second(0)
    pass_first(2)
    pass_second(1)
    pass_first(3)
    pass_second(2)
    pass_first(4)
    pass_second(3)
    pass_first(5)

    @pl.when(stage == 1)
    def _():
        def step(tile, _):
            pass_second(tile - 2)
            pass_first(tile)
            return 0

        lax.fori_loop(6, TILES, step, 0)
        pass_second(TILES - 2)
        pass_second(TILES - 1)

    vec_copy(other).wait_recv()
    par[:, :half] = vecs[0].astype(F32)
    par[:, half:] = vecs[1].astype(F32)
    for tile in range(UP):
        ready(tile)

    def rows_of(i):
        return pl.ds(pl.multiple_of(i * length, 16), length)

    def kept(slot, source, target, place, i):
        return pltpu.make_async_copy(source, target.at[place, rows_of(i)], keep_sem.at[slot])

    def keep_hf(i):
        return [kept(0, hf_s, fixed_out, 0, i)]

    def keep_h(i):
        return [kept(1, h_s, fixed_out, 1, i)]

    def keep_o(i):
        return [kept(2, o_s, fixed_out, 2, i)]

    def keep_g1(i):
        return [kept(3, g1, moving_out, PROJ + 4, i)]

    def keep_gq(i):
        return [kept(4 + j, gq_s.at[j], moving_out, 4 + j, i) for j in range(3)]

    def keep_a(i):
        return [kept(7 + j, gate.at[j], moving_out, 8 + j, i) for j in range(4)]

    def last_gu(i):
        return [
            pltpu.make_async_copy(slope.at[i, j], moving_out.at[j, rows_of(i)], last_sem.at[i, j])
            for j in range(4)
        ]

    def last_gz(i):
        return [pltpu.make_async_copy(ybuf.at[i], fixed_out.at[3, rows_of(i)], last_sem.at[i, 4])]

    def start(copies):
        for copy in copies:
            copy.start()

    def wait(copies):
        for copy in copies:
            copy.wait()

    def act_copy(i):
        return pltpu.make_async_copy(y1.at[i], act_out.at[i], act_sem.at[i])

    def cot_copy(i):
        return pltpu.make_async_copy(cot_in.at[part * seqs + i], ybuf.at[i], cot_sem.at[i])

    def y_copy(i):
        return pltpu.make_async_remote_copy(
            src_ref=ysend.at[i],
            dst_ref=ybuf.at[i],
            send_sem=y_send.at[i],
            recv_sem=y_recv.at[i],
            device_id=y_dev,
            device_id_type=MESH,
        )

    def row(index):
        return par[index : index + 1, :]

    lane = lax.broadcasted_iota(jnp.int32, (length, 128), 1)
    low = lane < 64
    side_ones = [(lane < 64).astype(F32).astype(BF), (lane >= 64).astype(F32).astype(BF)]

    def letters(i):
        ids = ids_in[pl.ds(part * seqs + i, 1), :]
        place = lax.broadcasted_iota(jnp.int32, (letters_count, length), 0)
        return (place == ids).astype(F32).astype(BF)

    def attn_fwd(i):
        @pl.when(stage == 0)
        def _():
            xs[...] = mul_tn(letters(i), table_in[...]) + time_in[pl.ds(part * seqs + i, 1), :]

        @pl.when(stage == 1)
        def _():
            y_copy(i).wait_recv()
            xs[...] = ybuf[i].astype(F32)
            cot_copy(i).start()

        n, rate = normalize(xs[...])
        n_a[i] = n.astype(BF)
        r_a[i] = jnp.broadcast_to(rate, (length, 128))

        @pl.when(i > 0)
        def _():
            wait(keep_h(i))
            wait(keep_o(i))

        h_s[...] = (n * row(0) + row(1)).astype(BF)
        start(keep_h(i))
        for j in range(3):
            joint = mul(h_s[...], w[QKV + j])
            if j == 0:
                joint = joint + row(2)
            if j == 2:
                joint = joint + row(3)
            qkv[i, :, j * width : (j + 1) * width] = joint.astype(BF)

        def pair(hp, _):
            at = pl.multiple_of(hp * 128, 128)
            q2 = qkv[i, :, pl.ds(at, 128)]
            k2 = qkv[i, :, pl.ds(width + at, 128)]
            v2 = qkv[i, :, pl.ds(2 * width + at, 128)]
            outs = []
            for side in range(2):
                scores = mul_nt(q2 * side_ones[side], k2) * scale
                expo = jnp.exp(scores - jnp.max(scores, axis=-1, keepdims=True))
                total = jnp.sum(expo, axis=-1, keepdims=True)
                pb = (expo * (1.0 / total)).astype(BF)
                probs[i, 2 * hp + side] = pb
                outs.append(mul(pb, v2))
            o_s[:, pl.ds(at, 128)] = jnp.where(low, outs[0], outs[1]).astype(BF)
            return 0

        lax.fori_loop(0, HEADS // 2, pair, 0)
        start(keep_o(i))
        y1[i] = (xs[...] + (mul(o_s[...], w[PROJ]) + row(4))).astype(BF)

    def feed_fwd(i):
        @pl.when(i == 0)
        def _():
            def one(tile, _):
                ready(tile)
                return 0

            lax.fori_loop(UP, TILES, one, 0)

        x = y1[i].astype(F32)
        n, rate = normalize(x)
        n_f[i] = n.astype(BF)
        r_f[i] = jnp.broadcast_to(rate, (length, 128))

        @pl.when(i > 0)
        def _():
            wait(keep_hf(i))
            wait(keep_a(i))

        hf_s[...] = (n * row(5) + row(6)).astype(BF)
        start(keep_hf(i))
        acc[...] = x + row(7)

        def one(j, _):
            u = mul(hf_s[...], w[UP + j]) + par[pl.ds(8 + j, 1), :]
            square = u * u
            t = jnp.tanh(u * (GELU_A + GELU_A * GELU_B * square))
            both = 0.5 + 0.5 * t
            a = (u * both).astype(BF)
            gate[j] = a
            bend = (0.5 * GELU_A + 1.5 * GELU_A * GELU_B * square) * u
            slope[i, j] = (both + bend * (1.0 - t * t)).astype(BF)
            acc[...] += mul(a, w[DOWN + j])
            return 0

        lax.fori_loop(0, 4, one, 0)
        start(keep_a(i))

        @pl.when(stage == 0)
        def _():
            ysend[i] = acc[...].astype(BF)
            y_copy(i).start()

        @pl.when(stage == 1)
        def _():
            y1[i] = acc[...].astype(BF)
            act_copy(i).start()

    def feed_bwd(i):
        @pl.when(stage == 0)
        def _():
            y_copy(i).wait_recv()

        @pl.when(stage == 1)
        def _():
            cot_copy(i).wait()

        start(last_gz(i))
        gsum[7:8, :] += column(ybuf[i].astype(F32))
        acc[...] = jnp.zeros_like(acc)

        def one(j, _):
            ga = mul_nt(ybuf[i], w[DOWN + j])
            gu = (ga * slope[i, j].astype(F32)).astype(BF)
            slope[i, j] = gu
            gsum[pl.ds(8 + j, 1), :] += column(gu.astype(F32))
            acc[...] += mul_nt(gu, w[UP + j])
            return 0

        lax.fori_loop(0, 4, one, 0)
        start(last_gu(i))
        gh = acc[...]
        n = n_f[i].astype(F32)
        gsum[5:6, :] += column(gh * n)
        gsum[6:7, :] += column(gh)
        gx = ybuf[i].astype(F32) + scaled_back(gh, row(5), n, r_f[i][:, 0:1])

        @pl.when(i > 0)
        def _():
            wait(keep_g1(i))
            wait(keep_gq(i))

        g1[...] = gx.astype(BF)
        start(keep_g1(i))

    def attn_bwd(i):
        gsum[4:5, :] += column(g1[...].astype(F32))
        go_s[...] = mul_nt(g1[...], w[PROJ]).astype(BF)

        def pair(hp, _):
            at = pl.multiple_of(hp * 128, 128)
            q2 = qkv[i, :, pl.ds(at, 128)]
            k2 = qkv[i, :, pl.ds(width + at, 128)]
            v2 = qkv[i, :, pl.ds(2 * width + at, 128)]
            go2 = go_s[:, pl.ds(at, 128)]
            gq, gk, gv = [], [], []
            for side in range(2):
                pb = probs[i, 2 * hp + side]
                gp = mul_nt(go2 * side_ones[side], v2)
                p = pb.astype(F32)
                pg = p * gp
                gs = (pg - p * jnp.sum(pg, axis=-1, keepdims=True)).astype(BF)
                gv.append(mul_tn(pb, go2))
                gq.append(mul(gs, k2))
                gk.append(mul_tn(gs, q2))
            gq_s[0, :, pl.ds(at, 128)] = (jnp.where(low, gq[0], gq[1]) * scale).astype(BF)
            gq_s[1, :, pl.ds(at, 128)] = (jnp.where(low, gk[0], gk[1]) * scale).astype(BF)
            gq_s[2, :, pl.ds(at, 128)] = jnp.where(low, gv[0], gv[1]).astype(BF)
            return 0

        lax.fori_loop(0, HEADS // 2, pair, 0)
        start(keep_gq(i))
        gsum[2:3, :] += column(gq_s[0].astype(F32))
        gsum[3:4, :] += column(gq_s[2].astype(F32))
        gh = mul_nt(gq_s[0], w[QKV]) + mul_nt(gq_s[1], w[QKV + 1]) + mul_nt(gq_s[2], w[QKV + 2])
        n = n_a[i].astype(F32)
        gsum[0:1, :] += column(gh * n)
        gsum[1:2, :] += column(gh)
        gx = g1[...].astype(F32) + scaled_back(gh, row(0), n, r_a[i][:, 0:1])
        acc[...] = gx

        @pl.when(stage == 1)
        def _():
            ysend[i] = acc[...].astype(BF)
            y_copy(i).start()

        @pl.when(stage == 0)
        def _():
            high = acc[...].astype(BF)
            rest = (acc[...] - high.astype(F32)).astype(BF)
            hot = letters(i)
            tsum[:letters_count, :] += mul(hot, high) + mul(hot, rest)
            tsum[pl.ds(letters_count + part * seqs + i, 1), :] = column(acc[...])

    def unit(u, _):
        early = u < 2 * seqs
        kind0 = jnp.where(early, lax.div(u, seqs), 2 + lax.rem(u, 2))
        index0 = jnp.where(early, lax.rem(u, seqs), lax.div(u, 2) - seqs)
        kind = jnp.where(stage == 0, kind0, lax.rem(u, 4))
        i = jnp.where(stage == 0, index0, lax.div(u, 4))

        @pl.when(jnp.logical_and(stage == 0, jnp.logical_and(u >= 1, u <= 4)))
        def _():
            pass_second(2 + 2 * u)
            pass_second(3 + 2 * u)

        @pl.when(jnp.logical_and(stage == 0, jnp.logical_and(u >= 1, u <= 3)))
        def _():
            pass_first(4 + 2 * u)
            pass_first(5 + 2 * u)

        for index, run in enumerate((attn_fwd, feed_fwd, feed_bwd, attn_bwd)):

            @pl.when(kind == index)
            def _():
                run(i)

        return 0

    lax.fori_loop(0, 4 * seqs, unit, 0)

    small_out[...] = gsum[...]
    table_out[...] = tsum[...]

    vec_copy(part).wait_send()

    def settle(tile, _):
        x_copy(tile).wait_send()
        z_copy(tile).wait_send()
        c1_copy(tile).wait_send()
        c2_copy(tile).wait_send()
        return 0

    lax.fori_loop(0, TILES, settle, 0)
    for done in (keep_h, keep_o, keep_hf, keep_a, keep_gq, keep_g1):
        wait(done(seqs - 1))

    def finish(i, _):
        y_copy(i).wait_send()
        wait(last_gu(i))
        wait(last_gz(i))

        @pl.when(stage == 1)
        def _():
            act_copy(i).wait()

        return 0

    lax.fori_loop(0, seqs, finish, 0)


def run_pipeline(weights, vec, ids, table, times, cot):
    rows, length = ids.shape
    width = cot.shape[2]
    seqs = rows // 2
    tokens = seqs * length
    dma = pltpu.SemaphoreType.DMA
    anywhere = pl.BlockSpec(memory_space=pl.ANY)
    local = pl.BlockSpec(memory_space=pltpu.VMEM)
    vm = pltpu.VMEM
    return pl.pallas_call(
        functools.partial(pipeline_kernel, seqs, length, width),
        out_shape=(
            jax.ShapeDtypeStruct((seqs, length, width), BF),
            jax.ShapeDtypeStruct((16, width), F32),
            jax.ShapeDtypeStruct((table.shape[0] + rows, width), F32),
            jax.ShapeDtypeStruct((4, tokens, width), BF),
            jax.ShapeDtypeStruct((12, tokens, width), BF),
        ),
        in_specs=[anywhere] * 5 + [local] * 3 + [anywhere],
        out_specs=(anywhere, local, local, anywhere, anywhere),
        scratch_shapes=[
            vm((TILES, width, width), BF),
            vm((2, 16, width // 2), BF),
            vm((16, width), F32),
            vm((length, width), F32),
            vm((seqs, length, width), BF),
            vm((seqs, length, width), BF),
            vm((seqs, length, 128), F32),
            vm((seqs, length, 128), F32),
            vm((seqs, length, 3 * width), BF),
            vm((seqs, HEADS, length, length), BF),
            vm((seqs, length, width), BF),
            vm((seqs, 4, length, width), BF),
            vm((4, length, width), BF),
            vm((length, width), BF),
            vm((length, width), BF),
            vm((length, width), BF),
            vm((3, length, width), BF),
            vm((length, width), BF),
            vm((length, width), BF),
            vm((length, width), F32),
            vm((seqs, length, width), BF),
            vm((seqs, length, width), BF),
            vm((16, width), F32),
            vm((table.shape[0] + rows, width), F32),
            dma((2 * TILES,)),
        ]
        + [dma((TILES,))] * 8
        + [
            dma((seqs,)),
            dma((seqs,)),
            dma((3,)),
            dma((seqs,)),
            dma((seqs,)),
            dma((11,)),
            dma((seqs, 5)),
        ],
        compiler_params=pltpu.CompilerParams(
            collective_id=0, has_side_effects=True, vmem_limit_bytes=62 * 2**20
        ),
    )(*weights, vec, ids, table, times, cot)


def reduce_kernel(
    nz,
    half,
    rows,
    fixed_in,
    moving_in,
    qkv_out,
    proj_out,
    up_out,
    down_out,
    fixed,
    moving,
    parts,
    core_buf,
    x_buf,
    right_buf,
    left_buf,
    total,
    fixed_sem,
    moving_sem,
    core_send,
    core_recv,
    x_send,
    x_recv,
    right_send,
    right_recv,
    left_send,
    left_recv,
):
    s = lax.axis_index("section")
    d = lax.axis_index("dp")
    part = lax.rem(s, 2)
    other = 1 - part
    core = lax.rem(d, 2)
    z = lax.div(d, 2)
    x_dev = (flipped(s, 0), d)
    c_dev = (s, flipped(d, 0))
    ends = nz - 1
    slots = moving.shape[0]
    width = 2 * half

    barrier = pltpu.get_barrier_semaphore()
    for device in (x_dev, c_dev):
        pl.semaphore_signal(barrier, inc=1, device_id=device, device_id_type=MESH)

    @pl.when(z > 0)
    def _():
        pl.semaphore_signal(barrier, inc=1, device_id=(s, d - 2), device_id_type=MESH)

    @pl.when(z < ends)
    def _():
        pl.semaphore_signal(barrier, inc=1, device_id=(s, d + 2), device_id_type=MESH)

    def load_fixed(index):
        return pltpu.make_async_copy(fixed_in.at[index], fixed.at[index], fixed_sem.at[index])

    def tile_at(turn):
        pair = turn - 4
        return jnp.where(turn < 4, turn, 4 + lax.div(pair, 2) + 4 * lax.rem(pair, 2))

    def load_moving(turn):
        slot = lax.rem(turn, slots)
        return pltpu.make_async_copy(moving_in.at[tile_at(turn)], moving.at[slot], moving_sem.at[slot])

    for turn in range(slots):
        load_moving(jnp.int32(turn)).start()
        if turn == 0:
            load_fixed(0).start()
    for index in (1, 3, 2):
        load_fixed(index).start()

    neighbours = 2 + (z > 0).astype(jnp.int32) + (z < ends).astype(jnp.int32)
    pl.semaphore_wait(barrier, neighbours)

    def core_copy(k):
        return pltpu.make_async_remote_copy(
            src_ref=parts.at[k, :, :, 1 - core],
            dst_ref=core_buf.at[k],
            send_sem=core_send.at[k],
            recv_sem=core_recv.at[k],
            device_id=c_dev,
            device_id_type=MESH,
        )

    def x_copy(k):
        return pltpu.make_async_remote_copy(
            src_ref=parts.at[k, other, :, core],
            dst_ref=x_buf.at[k],
            send_sem=x_send.at[k],
            recv_sem=x_recv.at[k],
            device_id=x_dev,
            device_id_type=MESH,
        )

    def right_copy(k, j):
        return pltpu.make_async_remote_copy(
            src_ref=parts.at[k, part, j, core],
            dst_ref=right_buf.at[k, j],
            send_sem=right_send.at[k, j],
            recv_sem=right_recv.at[k, j],
            device_id=(s, d + 2),
            device_id_type=MESH,
        )

    def left_copy(k, j):
        return pltpu.make_async_remote_copy(
            src_ref=parts.at[k, part, j, core],
            dst_ref=left_buf.at[k, j],
            send_sem=left_send.at[k, j],
            recv_sem=left_recv.at[k, j],
            device_id=(s, d - 2),
            device_id_type=MESH,
        )

    def right_step(k):
        for j in range(ends, -1, -1):

            @pl.when(jnp.logical_and(z > 0, j >= z))
            def _():
                right_copy(k, j).wait_recv()

            @pl.when(jnp.logical_and(z > 0, j > z))
            def _():
                both = parts[k, part, j, core].astype(F32) + right_buf[k, j].astype(F32)
                parts[k, part, j, core] = both.astype(BF)

            @pl.when(j > z)
            def _():
                right_copy(k, j).start()

    def left_step(k):
        for j in range(nz):

            @pl.when(jnp.logical_and(z < ends, j <= z))
            def _():
                left_copy(k, j).wait_recv()

            @pl.when(jnp.logical_and(z < ends, j < z))
            def _():
                both = parts[k, part, j, core].astype(F32) + left_buf[k, j].astype(F32)
                parts[k, part, j, core] = both.astype(BF)

            @pl.when(j < z)
            def _():
                left_copy(k, j).start()

    def close_step(k):
        @pl.when(z == 0)
        def _():
            total[...] = parts[k, part, z, core].astype(F32) + left_buf[k, z].astype(F32)

        @pl.when(z == ends)
        def _():
            total[...] = parts[k, part, z, core].astype(F32) + right_buf[k, z].astype(F32)

        @pl.when(jnp.logical_and(z > 0, z < ends))
        def _():
            sides = left_buf[k, z].astype(F32) + right_buf[k, z].astype(F32)
            total[...] = parts[k, part, z, core].astype(F32) + sides

        @pl.when(k < 4)
        def _():
            for side in range(2):
                at = pl.multiple_of(side * 4 * half + k * half, 128)
                up_out[0, :, pl.ds(at, half)] = total[:, side * half : (side + 1) * half]

        @pl.when(jnp.logical_and(k >= 4, k < 7))
        def _():
            qkv_out[0, :, pl.ds(pl.multiple_of((k - 4) * width, 128), width)] = total[...]

        @pl.when(k == 7)
        def _():
            proj_out[0] = total[...]

        @pl.when(k >= 8)
        def _():
            down_out[0, pl.ds(pl.multiple_of((k - 8) * rows, 8), rows), :] = total[...]

    def product(turn):
        load_moving(turn).wait()
        m = tile_at(turn)
        slot = lax.rem(turn, slots)

        @pl.when(m == 0)
        def _():
            load_fixed(0).wait()

        @pl.when(m == 4)
        def _():
            load_fixed(1).wait()

        @pl.when(m == 7)
        def _():
            load_fixed(2).wait()

        @pl.when(m == 8)
        def _():
            load_fixed(3).wait()

        @pl.when(m < 8)
        def _():
            upper = (m >= 4).astype(jnp.int32) + (m >= 7).astype(jnp.int32)
            value = mul_tn(fixed[upper], moving[slot]).astype(BF)
            parts[m] = value.reshape(2, nz, 2, rows, width)

        @pl.when(m >= 8)
        def _():
            value = mul_tn(moving[slot], fixed[3]).astype(BF).reshape(2, 2, 4, rows, width)
            for block in range(4):
                parts[8 + block, :, m - 8] = value[:, :, block]

        @pl.when(turn + slots < TILES)
        def _():
            load_moving(turn + slots).start()

    def inside(k):
        return jnp.logical_and(k >= 0, k < TILES)

    def step(t, _):
        @pl.when(t < 4)
        def _():
            product(t)

        @pl.when(jnp.logical_and(t >= 4, t < 8))
        def _():
            product(4 + 2 * (t - 4))
            product(5 + 2 * (t - 4))

        @pl.when(t < TILES)
        def _():
            core_copy(t).start()

        k1 = t - 1

        @pl.when(inside(k1))
        def _():
            core_copy(k1).wait_recv()
            for side in range(2):
                both = parts[k1, side, :, core].astype(F32) + core_buf[k1, side].astype(F32)
                parts[k1, side, :, core] = both.astype(BF)
            x_copy(k1).start()

        k2 = t - 2

        @pl.when(inside(k2))
        def _():
            x_copy(k2).wait_recv()
            both = parts[k2, part, :, core].astype(F32) + x_buf[k2].astype(F32)
            parts[k2, part, :, core] = both.astype(BF)

        k3 = t - 2 - z

        @pl.when(inside(k3))
        def _():
            right_step(k3)

        k4 = t - 2 - (ends - z)

        @pl.when(inside(k4))
        def _():
            left_step(k4)

        k5 = jnp.minimum(k3, k4)

        @pl.when(inside(k5))
        def _():
            close_step(k5)

        return 0

    lax.fori_loop(0, TILES + 2 + ends, step, 0)

    def settle(k, _):
        core_copy(k).wait_send()
        x_copy(k).wait_send()
        for j in range(nz):

            @pl.when(j > z)
            def _():
                right_copy(k, j).wait_send()

            @pl.when(j < z)
            def _():
                left_copy(k, j).wait_send()

        return 0

    lax.fori_loop(0, TILES, settle, 0)


def run_reduce(fixed, moving, replicas):
    tokens, width = fixed.shape[1:]
    nz = replicas // 2
    half = width // 2
    rows = half // replicas
    dma = pltpu.SemaphoreType.DMA
    vm = pltpu.VMEM
    slots = 3
    return pl.pallas_call(
        functools.partial(reduce_kernel, nz, half, rows),
        out_shape=(
            jax.ShapeDtypeStruct((1, rows, 3 * width), F32),
            jax.ShapeDtypeStruct((1, rows, width), F32),
            jax.ShapeDtypeStruct((1, rows, 4 * width), F32),
            jax.ShapeDtypeStruct((1, 4 * rows, width), F32),
        ),
        in_specs=[pl.BlockSpec(memory_space=pl.ANY)] * 2,
        out_specs=(pl.BlockSpec(memory_space=pltpu.VMEM),) * 4,
        scratch_shapes=[
            vm((4, tokens, width), BF),
            vm((slots, tokens, width), BF),
            vm((TILES, 2, nz, 2, rows, width), BF),
            vm((TILES, 2, nz, rows, width), BF),
            vm((TILES, nz, rows, width), BF),
            vm((TILES, nz, rows, width), BF),
            vm((TILES, nz, rows, width), BF),
            vm((rows, width), F32),
            dma((4,)),
            dma((slots,)),
            dma((TILES,)),
            dma((TILES,)),
            dma((TILES,)),
            dma((TILES,)),
            dma((TILES, nz)),
            dma((TILES, nz)),
            dma((TILES, nz)),
            dma((TILES, nz)),
        ],
        compiler_params=pltpu.CompilerParams(
            collective_id=1, has_side_effects=True, vmem_limit_bytes=62 * 2**20
        ),
    )(fixed, moving)


def plain_reduce(fixed, moving, lower):
    def grad(left, right):
        return jnp.einsum("tk,tn->kn", left, right, preferred_element_type=F32)

    width = fixed.shape[2]
    half = width // 2
    hf, h, o, gz = (fixed[index] for index in range(4))
    ups = jnp.stack([grad(hf, moving[j]) for j in range(4)])
    up = ups.reshape(4, width, 2, half).transpose(1, 2, 0, 3).reshape(width, 4 * width)
    joint = jnp.concatenate([grad(h, moving[4 + j]) for j in range(3)], axis=1)
    proj = grad(o, moving[7])
    downs = jnp.stack([grad(moving[8 + j], gz) for j in range(4)])
    down = downs.reshape(4, 2, half, width).transpose(1, 0, 2, 3).reshape(4 * width, width)
    results = []
    for total in (joint, proj, up, down):
        halves = total.reshape((2, total.shape[0] // 2) + total.shape[1:])
        summed = lax.psum_scatter(halves, "dp", scatter_dimension=1, tiled=True)
        ours = jnp.where(lower, summed[0], summed[1])
        theirs = jnp.where(lower, summed[1], summed[0]).astype(BF)
        pairs = [(i, i ^ 1) for i in range(lax.axis_size("section"))]
        results.append((ours + lax.ppermute(theirs, "section", pairs).astype(F32))[None])
    return results


def spread_activations(act, section, width):
    quarter = width // 4
    part = lax.rem(section, 2)

    def piece(index):
        return lax.dynamic_slice_in_dim(act, index * quarter, quarter, axis=2)

    straight = lax.ppermute(piece(part), "section", [(2, 0), (3, 1)])
    crossed = lax.ppermute(piece(1 - part), "section", [(2, 1), (3, 0)])
    beside = lax.ppermute(piece(3 - part), "section", [(2, 3), (3, 2)])
    upper = section >= 2
    same = jnp.where(upper, piece(2 + part), straight)
    far = jnp.where(upper, beside, crossed)
    lower = part == 0
    first = jnp.where(lower, same, far)
    second = jnp.where(lower, far, same)
    return jnp.concatenate([first, second], axis=0).astype(F32)


def per_device(
    token_ids,
    timesteps,
    token_table,
    time_table,
    attn_gain,
    attn_shift,
    qkv_weight,
    query_bias,
    value_bias,
    proj_weight,
    proj_bias,
    mlp_gain,
    mlp_shift,
    up_weight,
    up_bias,
    down_weight,
    down_bias,
    cotangent,
):
    section = lax.axis_index("section")
    replica = lax.axis_index("dp")
    replicas = lax.axis_size("dp")
    rows, length = token_ids.shape
    width = cotangent.shape[2]
    half = width // 2
    layer = section // 2
    part = section % 2
    letters_count = token_table.shape[0]
    times_count = time_table.shape[0]
    padded = -(-letters_count // 16) * 16
    vec = jnp.concatenate(
        [
            attn_gain,
            attn_shift,
            query_bias,
            value_bias,
            proj_bias,
            mlp_gain,
            mlp_shift,
            down_bias,
            up_bias.reshape(4, half),
            jnp.zeros((4, half), BF),
        ],
        axis=0,
    )
    table = jnp.pad(token_table, ((0, padded - letters_count), (0, 0)))
    times = jnp.take(time_table, timesteps, axis=0).astype(F32)
    moments = lax.all_gather(timesteps, "dp", tiled=True)
    weights = (qkv_weight, proj_weight, up_weight, down_weight)
    act, small, tables, fixed, moving = run_pipeline(weights, vec, token_ids, table, times, cotangent)
    activations = spread_activations(act, section, width)
    total_rows = rows * replicas
    mine = jnp.zeros((2, 16, width), F32)
    mine = lax.dynamic_update_slice_in_dim(mine, small[None], layer, 0)
    placed = jnp.zeros((total_rows, width), F32)
    placed = lax.dynamic_update_slice_in_dim(placed, tables[padded:], replica * rows, 0)
    joined = jnp.concatenate([tables[:padded], mine.reshape(32, width), placed], axis=0)
    joined = lax.psum(joined, ("section", "dp"))
    if half % (16 * replicas) == 0:
        qkv_grad, proj_grad, up_grad, down_grad = run_reduce(fixed, moving, replicas)
    else:
        qkv_grad, proj_grad, up_grad, down_grad = plain_reduce(fixed, moving, part == 0)
    quarter = width // 4
    columns = lax.dynamic_slice_in_dim(joined, section * quarter, quarter, axis=1)
    token_grad = columns[:letters_count]
    steps = jnp.arange(times_count, dtype=jnp.int32)
    hot = (steps[:, None] == moments[None, :]).astype(F32)
    time_grad = jnp.einsum("tb,bd->td", hot, columns[padded + 32 :], precision=HIGHEST)
    ours = lax.dynamic_slice(joined, (padded + 16 * layer, part * half), (16, half))
    each = half // replicas
    vectors = lax.dynamic_slice_in_dim(ours[:8], replica * each, each, axis=1)
    ups = lax.dynamic_slice_in_dim(ours[8:12].reshape(1, 4 * half), replica * 4 * each, 4 * each, axis=1)
    return (
        activations,
        token_grad,
        time_grad,
        vectors[0:1],
        vectors[1:2],
        qkv_grad,
        vectors[2:3],
        vectors[3:4],
        proj_grad,
        vectors[4:5],
        vectors[5:6],
        vectors[6:7],
        up_grad,
        ups,
        down_grad,
        vectors[7:8],
    )


def solution(mesh):
    return jax.shard_map(
        per_device,
        mesh=mesh,
        in_specs=(
            P("dp", None),
            P("dp"),
            P(),
            P(),
            P("section", None),
            P("section", None),
            P("section", None, None),
            P("section", None),
            P("section", None),
            P("section", None, None),
            P("section", None),
            P("section", None),
            P("section", None),
            P("section", None, None),
            P("section", None),
            P("section", None, None),
            P("section", None),
            P("dp", None, None),
        ),
        out_specs=(
            P("dp", None, "section"),
            P(None, "section"),
            P(None, "section"),
            P("section", "dp"),
            P("section", "dp"),
            P("section", "dp", None),
            P("section", "dp"),
            P("section", "dp"),
            P("section", "dp", None),
            P("section", "dp"),
            P("section", "dp"),
            P("section", "dp"),
            P("section", "dp", None),
            P("section", "dp"),
            P("section", "dp", None),
            P("section", "dp"),
        ),
        check_vma=False,
    )
```

```python
import functools
import math

import jax
import jax.numpy as jnp
from jax import lax
from jax.experimental import pallas as pl
from jax.experimental.pallas import tpu as pltpu
from jax.sharding import PartitionSpec as P

HEADS = 12
EPS = 1e-05
HIGHEST = lax.Precision.HIGHEST
MESH = pl.DeviceIdType.MESH
BF = jnp.bfloat16
F32 = jnp.float32
TILES = 12
QKV, PROJ, UP, DOWN = 0, 3, 4, 8
GELU_A = math.sqrt(2.0 / math.pi)
GELU_B = 0.044715


def flipped(value, bit):
    mask = 2**bit
    return value + mask - 2 * mask * lax.rem(lax.div(value, mask), 2)


def mul(a, b):
    return lax.dot_general(a, b, (((1,), (0,)), ((), ())), preferred_element_type=F32)


def mul_nt(a, b):
    return lax.dot_general(a, b, (((1,), (1,)), ((), ())), preferred_element_type=F32)


def mul_tn(a, b):
    return lax.dot_general(a, b, (((0,), (0,)), ((), ())), preferred_element_type=F32)


def normalize(x):
    mean = jnp.mean(x, axis=-1, keepdims=True)
    centered = x - mean
    spread = jnp.mean(centered * centered, axis=-1, keepdims=True)
    rate = lax.rsqrt(spread + EPS)
    return centered * rate, rate


def scaled_back(gh, gain, n, rate):
    gn = gh * gain
    inner = jnp.mean(gn * n, axis=-1, keepdims=True)
    return (gn - jnp.mean(gn, axis=-1, keepdims=True) - n * inner) * rate


def column(values):
    return jnp.sum(values, axis=0, keepdims=True)


def pipeline_kernel(
    seqs,
    length,
    width,
    qkv_in,
    proj_in,
    up_in,
    down_in,
    ga_in,
    sa_in,
    bq_in,
    bv_in,
    bo_in,
    gm_in,
    sm_in,
    bdown_in,
    bup_in,
    ids_in,
    table_in,
    time_in,
    cot_in,
    act_out,
    sums_out,
    fixed_out,
    moving_out,
    w,
    vecs,
    table,
    par,
    xs,
    n_a,
    n_f,
    r_a,
    r_f,
    qkv,
    probs,
    y1,
    slope,
    gate,
    h_s,
    o_s,
    hf_s,
    gq_s,
    g1,
    go_s,
    acc,
    ybuf,
    ysend,
    act,
    gsum,
    own_sem,
    x_send,
    x_recv,
    z_send,
    z_recv,
    c1_send,
    c1_recv,
    c2_send,
    c2_recv,
    y_send,
    y_recv,
    v_sem,
    cot_sem,
    act_send,
    act_recv,
    keep_sem,
    last_sem,
):
    s = lax.axis_index("section")
    d = lax.axis_index("dp")
    stage = lax.div(s, 2)
    part = lax.rem(s, 2)
    other = 1 - part
    x_dev = (flipped(s, 0), d)
    y_dev = (flipped(s, 1), d)
    z_dev = (s, flipped(d, 1))
    c_dev = (s, flipped(d, 0))
    far_dev = (flipped(flipped(s, 0), 1), d)
    half = width // 2
    quarter = half // 4
    hidden_half = up_in.shape[2] // 2
    mine = lax.rem(d, 4)
    across = flipped(mine, 1)
    scale = 1.0 / math.sqrt(width // HEADS)
    letters_count = table_in.shape[0]
    padded = table.shape[0]
    vectors = 16

    barrier = pltpu.get_barrier_semaphore()
    for device in (x_dev, y_dev, z_dev, c_dev, far_dev):
        pl.semaphore_signal(barrier, inc=1, device_id=device, device_id_type=MESH)

    own_rows = pl.ds(pl.multiple_of(part * half, 16), half)

    def own_copies(tile):
        if tile < PROJ:
            pairs = [(qkv_in.at[0, :, pl.ds(tile * width, width)], w.at[tile, own_rows])]
        elif tile < UP:
            pairs = [(proj_in.at[0], w.at[tile, own_rows])]
        elif tile < DOWN:
            pairs = [
                (
                    up_in.at[0, :, pl.ds(side * hidden_half + (tile - UP) * half, half)],
                    w.at[tile, own_rows, pl.ds(side * half, half)],
                )
                for side in range(2)
            ]
        else:
            pairs = [(down_in.at[0, pl.ds((tile - DOWN) * half, half)], w.at[tile, own_rows])]
        return [
            pltpu.make_async_copy(src, dst, own_sem.at[2 * tile + k]) for k, (src, dst) in enumerate(pairs)
        ]

    def x_copy(tile):
        rows = pl.ds(pl.multiple_of(part * half + mine * quarter, 16), quarter)
        return pltpu.make_async_remote_copy(
            src_ref=w.at[tile, rows],
            dst_ref=w.at[tile, rows],
            send_sem=x_send.at[tile],
            recv_sem=x_recv.at[tile],
            device_id=x_dev,
            device_id_type=MESH,
        )

    def relay(tile, which, send, recv, device):
        rows = pl.ds(pl.multiple_of(other * half + which * quarter, 16), quarter)
        return pltpu.make_async_remote_copy(
            src_ref=w.at[tile, rows],
            dst_ref=w.at[tile, rows],
            send_sem=send.at[tile],
            recv_sem=recv.at[tile],
            device_id=device,
            device_id_type=MESH,
        )

    def z_copy(tile):
        return relay(tile, mine, z_send, z_recv, z_dev)

    def c1_copy(tile):
        return relay(tile, mine, c1_send, c1_recv, c_dev)

    def c2_copy(tile):
        return relay(tile, across, c2_send, c2_recv, c_dev)

    def x_arrival(tile):
        return relay(tile, mine, x_send, x_recv, x_dev)

    def z_arrival(tile):
        return relay(tile, across, z_send, z_recv, z_dev)

    def c1_arrival(tile):
        return relay(tile, flipped(mine, 0), c1_send, c1_recv, c_dev)

    def c2_arrival(tile):
        return relay(tile, flipped(across, 0), c2_send, c2_recv, c_dev)

    def vec_copy(which):
        return pltpu.make_async_remote_copy(
            src_ref=vecs.at[which],
            dst_ref=vecs.at[which],
            send_sem=v_sem.at[1],
            recv_sem=v_sem.at[2],
            device_id=x_dev,
            device_id_type=MESH,
        )

    def pass_first(tile):
        x_arrival(tile).wait_recv()
        z_copy(tile).start()
        c1_copy(tile).start()

    def pass_second(tile):
        z_arrival(tile).wait_recv()
        c2_copy(tile).start()

    def ready(tile):
        c1_arrival(tile).wait_recv()
        c2_arrival(tile).wait_recv()

    for tile in range(TILES):
        for copy in own_copies(tile):
            copy.start()
    singles = (ga_in, sa_in, bq_in, bv_in, bo_in, gm_in, sm_in, bdown_in)
    for index, single in enumerate(singles):
        vecs[part, index : index + 1, :] = single[...].astype(F32)
    for j in range(4):
        vecs[part, 8 + j : 9 + j, :] = bup_in[:, j * half : (j + 1) * half].astype(F32)
    vecs[part, 12:16, :] = jnp.zeros((4, half), F32)
    table[...] = jnp.zeros_like(table)
    table[:letters_count, :] = table_in[...]
    gsum[...] = jnp.zeros_like(gsum)
    pl.semaphore_wait(barrier, 5)
    vec_copy(part).start()
    for tile in range(TILES):
        for copy in own_copies(tile):
            copy.wait()
        x_copy(tile).start()

    pass_first(0)
    pass_first(1)
    pass_second(0)
    pass_first(2)
    pass_second(1)
    pass_first(3)
    pass_second(2)
    pass_first(4)
    pass_second(3)
    pass_first(5)

    @pl.when(stage == 1)
    def _():
        def step(tile, _):
            pass_second(tile - 2)
            pass_first(tile)
            return 0

        lax.fori_loop(6, TILES, step, 0)
        pass_second(TILES - 2)
        pass_second(TILES - 1)

    vec_copy(other).wait_recv()
    par[:, :half] = vecs[0]
    par[:, half:] = vecs[1]
    for tile in range(UP):
        ready(tile)

    def rows_of(i):
        return pl.ds(pl.multiple_of(i * length, 16), length)

    def kept(slot, source, target, place, i):
        return pltpu.make_async_copy(source, target.at[place, rows_of(i)], keep_sem.at[slot])

    def keep_hf(i):
        return [kept(0, hf_s, fixed_out, 0, i)]

    def keep_h(i):
        return [kept(1, h_s, fixed_out, 1, i)]

    def keep_o(i):
        return [kept(2, o_s, fixed_out, 2, i)]

    def keep_g1(i):
        return [kept(3, g1, moving_out, PROJ + 4, i)]

    def keep_gq(i):
        return [kept(4 + j, gq_s.at[j], moving_out, 4 + j, i) for j in range(3)]

    def keep_a(i):
        return [kept(7 + j, gate.at[j], moving_out, 8 + j, i) for j in range(4)]

    def last_gu(i):
        return [
            pltpu.make_async_copy(slope.at[i, j], moving_out.at[j, rows_of(i)], last_sem.at[i, j])
            for j in range(4)
        ]

    def last_gz(i):
        return [pltpu.make_async_copy(ybuf.at[i], fixed_out.at[3, rows_of(i)], last_sem.at[i, 4])]

    def start(copies):
        for copy in copies:
            copy.start()

    def wait(copies):
        for copy in copies:
            copy.wait()

    def act_copies(i):
        copies = []
        for index, device in enumerate((y_dev, x_dev, far_dev)):
            copies.append(
                pltpu.make_async_remote_copy(
                    src_ref=act.at[i, device[0]],
                    dst_ref=act_out.at[part, i],
                    send_sem=act_send.at[i, index],
                    recv_sem=act_recv.at[part, i],
                    device_id=device,
                    device_id_type=MESH,
                )
            )
        return copies

    def act_own(i):
        return pltpu.make_async_copy(act.at[i, s], act_out.at[part, i], act_send.at[i, 3])

    def act_arrival(side, i):
        return pltpu.make_async_remote_copy(
            src_ref=act.at[i, 0],
            dst_ref=act_out.at[side, i],
            send_sem=act_send.at[i, 0],
            recv_sem=act_recv.at[side, i],
            device_id=y_dev,
            device_id_type=MESH,
        )

    def cot_copy(i):
        return pltpu.make_async_copy(cot_in.at[part * seqs + i], ybuf.at[i], cot_sem.at[i])

    def y_copy(i):
        return pltpu.make_async_remote_copy(
            src_ref=ysend.at[i],
            dst_ref=ybuf.at[i],
            send_sem=y_send.at[i],
            recv_sem=y_recv.at[i],
            device_id=y_dev,
            device_id_type=MESH,
        )

    def row(index):
        return par[index : index + 1, :]

    lane = lax.broadcasted_iota(jnp.int32, (length, 128), 1)
    low = lane < 64
    side_scaled = [((lane < 64).astype(F32) * scale).astype(BF), ((lane >= 64).astype(F32) * scale).astype(BF)]
    side_ones = [(lane < 64).astype(F32).astype(BF), (lane >= 64).astype(F32).astype(BF)]

    def letters(i):
        ids = ids_in[pl.ds(part * seqs + i, 1), :]
        place = lax.broadcasted_iota(jnp.int32, (padded, length), 0)
        return (place == ids).astype(F32).astype(BF)

    def attn_fwd(i):
        @pl.when(stage == 0)
        def _():
            xs[...] = mul_tn(letters(i), table[...]) + time_in[pl.ds(part * seqs + i, 1), :width]

        @pl.when(stage == 1)
        def _():
            y_copy(i).wait_recv()
            xs[...] = ybuf[i].astype(F32)
            cot_copy(i).start()

        n, rate = normalize(xs[...])
        n_a[i] = n.astype(BF)
        r_a[i] = jnp.broadcast_to(rate, (length, 128))

        @pl.when(i > 0)
        def _():
            wait(keep_h(i))
            wait(keep_o(i))

        h_s[...] = (n * row(0) + row(1)).astype(BF)
        start(keep_h(i))
        for j in range(3):
            joint = mul(h_s[...], w[QKV + j])
            if j == 0:
                joint = joint + row(2)
            if j == 2:
                joint = joint + row(3)
            qkv[i, :, j * width : (j + 1) * width] = joint.astype(BF)

        def first(hp, _):
            at = pl.multiple_of(hp * 128, 128)
            q2 = qkv[i, :, pl.ds(at, 128)]
            k2 = qkv[i, :, pl.ds(width + at, 128)]
            for side in range(2):
                scores = mul_nt(q2 * side_scaled[side], k2)
                expo = jnp.exp(scores - jnp.max(scores, axis=-1, keepdims=True))
                total = jnp.sum(expo, axis=-1, keepdims=True)
                probs[i, 2 * hp + side] = (expo * (1.0 / total)).astype(BF)
            return 0

        def second(hp, _):
            at = pl.multiple_of(hp * 128, 128)
            v2 = qkv[i, :, pl.ds(2 * width + at, 128)]
            outs = [mul(probs[i, 2 * hp + side], v2) for side in range(2)]
            o_s[:, pl.ds(at, 128)] = jnp.where(low, outs[0], outs[1]).astype(BF)
            return 0

        lax.fori_loop(0, HEADS // 2, first, 0, unroll=6)
        lax.fori_loop(0, HEADS // 2, second, 0, unroll=6)
        start(keep_o(i))
        y1[i] = (xs[...] + (mul(o_s[...], w[PROJ]) + row(4))).astype(BF)

    def feed_fwd(i):
        def arrived(first, last):
            @pl.when(i == 0)
            def _():
                def one(tile, _):
                    ready(tile)
                    return 0

                lax.fori_loop(first, last, one, 0)

        arrived(UP, DOWN)
        x = y1[i].astype(F32)
        n, rate = normalize(x)
        n_f[i] = n.astype(BF)
        r_f[i] = jnp.broadcast_to(rate, (length, 128))

        @pl.when(i > 0)
        def _():
            wait(keep_hf(i))
            wait(keep_a(i))

        hf_s[...] = (n * row(5) + row(6)).astype(BF)
        start(keep_hf(i))
        acc[...] = x + row(7)

        def one(j, _):
            u = mul(hf_s[...], w[UP + j]) + par[pl.ds(8 + j, 1), :]
            square = u * u
            t = jnp.tanh(u * (GELU_A + GELU_A * GELU_B * square))
            both = 0.5 + 0.5 * t
            a = (u * both).astype(BF)
            gate[j] = a
            bend = (0.5 * GELU_A + 1.5 * GELU_A * GELU_B * square) * u
            slope[i, j] = (both + bend * (1.0 - t * t)).astype(BF)
            return 0

        lax.fori_loop(0, 4, one, 0, unroll=4)
        start(keep_a(i))
        arrived(DOWN, TILES)
        down = mul(gate[0], w[DOWN])
        for j in range(1, 4):
            down = down + mul(gate[j], w[DOWN + j])
        acc[...] += down

        @pl.when(stage == 0)
        def _():
            ysend[i] = acc[...].astype(BF)
            y_copy(i).start()

        @pl.when(stage == 1)
        def _():
            for q in range(4):
                act[i, q] = acc[:, q * (width // 4) : (q + 1) * (width // 4)].astype(BF)
            start(act_copies(i))
            act_own(i).start()

    def feed_bwd(i):
        @pl.when(stage == 0)
        def _():
            y_copy(i).wait_recv()

        @pl.when(stage == 1)
        def _():
            cot_copy(i).wait()

        start(last_gz(i))
        gsum[7:8, :width] += column(ybuf[i].astype(F32))
        acc[...] = jnp.zeros_like(acc)

        def one(j, _):
            ga = mul_nt(ybuf[i], w[DOWN + j])
            gu = (ga * slope[i, j].astype(F32)).astype(BF)
            slope[i, j] = gu
            gsum[pl.ds(8 + j, 1), :width] += column(gu.astype(F32))
            return 0

        lax.fori_loop(0, 4, one, 0, unroll=4)
        start(last_gu(i))
        gh = mul_nt(slope[i, 0], w[UP])
        for j in range(1, 4):
            gh = gh + mul_nt(slope[i, j], w[UP + j])
        n = n_f[i].astype(F32)
        gsum[5:6, :width] += column(gh * n)
        gsum[6:7, :width] += column(gh)
        gx = ybuf[i].astype(F32) + scaled_back(gh, row(5), n, r_f[i][:, 0:1])

        @pl.when(i > 0)
        def _():
            wait(keep_g1(i))
            wait(keep_gq(i))

        g1[...] = gx.astype(BF)
        start(keep_g1(i))

    def attn_bwd(i):
        gsum[4:5, :width] += column(g1[...].astype(F32))
        go_s[...] = mul_nt(g1[...], w[PROJ]).astype(BF)

        def first(hp, _):
            at = pl.multiple_of(hp * 128, 128)
            v2 = qkv[i, :, pl.ds(2 * width + at, 128)]
            go2 = go_s[:, pl.ds(at, 128)]
            gv = []
            for side in range(2):
                pb = probs[i, 2 * hp + side]
                gp = mul_nt(go2 * side_ones[side], v2)
                p = pb.astype(F32)
                pg = p * gp
                gs = (pg - p * jnp.sum(pg, axis=-1, keepdims=True)).astype(BF)
                gv.append(mul_tn(pb, go2))
                probs[i, 2 * hp + side] = gs
            gq_s[2, :, pl.ds(at, 128)] = jnp.where(low, gv[0], gv[1]).astype(BF)
            return 0

        def second(hp, _):
            at = pl.multiple_of(hp * 128, 128)
            q2 = qkv[i, :, pl.ds(at, 128)]
            k2 = qkv[i, :, pl.ds(width + at, 128)]
            gq, gk = [], []
            for side in range(2):
                gs = probs[i, 2 * hp + side]
                gq.append(mul(gs, k2))
                gk.append(mul_tn(gs, q2))
            gq_s[0, :, pl.ds(at, 128)] = (jnp.where(low, gq[0], gq[1]) * scale).astype(BF)
            gq_s[1, :, pl.ds(at, 128)] = (jnp.where(low, gk[0], gk[1]) * scale).astype(BF)
            return 0

        lax.fori_loop(0, HEADS // 2, first, 0, unroll=6)
        lax.fori_loop(0, HEADS // 2, second, 0, unroll=6)
        start(keep_gq(i))
        gsum[2:3, :width] += column(gq_s[0].astype(F32))
        gsum[3:4, :width] += column(gq_s[2].astype(F32))
        gh = mul_nt(gq_s[0], w[QKV]) + mul_nt(gq_s[1], w[QKV + 1]) + mul_nt(gq_s[2], w[QKV + 2])
        n = n_a[i].astype(F32)
        gsum[0:1, :width] += column(gh * n)
        gsum[1:2, :width] += column(gh)
        gx = g1[...].astype(F32) + scaled_back(gh, row(0), n, r_a[i][:, 0:1])
        acc[...] = gx

        @pl.when(stage == 1)
        def _():
            ysend[i] = acc[...].astype(BF)
            y_copy(i).start()

        @pl.when(stage == 0)
        def _():
            high = acc[...].astype(BF)
            rest = (acc[...] - high.astype(F32)).astype(BF)
            hot = letters(i)
            gsum[vectors : vectors + padded, :width] += mul(hot, high) + mul(hot, rest)
            mark = part * seqs + i
            stamp = time_in[pl.ds(mark, 1), :]
            gsum[pl.ds(vectors + padded + mark, 1), :] = jnp.concatenate(
                [column(acc[...]), stamp[:, width:]], axis=1
            )

    def unit(u, _):
        early = u < 2 * seqs
        kind0 = jnp.where(early, lax.div(u, seqs), 2 + lax.rem(u, 2))
        index0 = jnp.where(early, lax.rem(u, seqs), lax.div(u, 2) - seqs)
        kind = jnp.where(stage == 0, kind0, lax.rem(u, 4))
        i = jnp.where(stage == 0, index0, lax.div(u, 4))

        @pl.when(jnp.logical_and(stage == 0, jnp.logical_and(u >= 1, u <= 4)))
        def _():
            pass_second(2 + 2 * u)
            pass_second(3 + 2 * u)

        @pl.when(jnp.logical_and(stage == 0, jnp.logical_and(u >= 1, u <= 3)))
        def _():
            pass_first(4 + 2 * u)
            pass_first(5 + 2 * u)

        for index, run in enumerate((attn_fwd, feed_fwd, feed_bwd, attn_bwd)):

            @pl.when(kind == index)
            def _():
                run(i)

        return 0

    lax.fori_loop(0, 4 * seqs, unit, 0)

    sums_out[...] = gsum[...]

    vec_copy(part).wait_send()

    def settle(tile, _):
        x_copy(tile).wait_send()
        z_copy(tile).wait_send()
        c1_copy(tile).wait_send()
        c2_copy(tile).wait_send()
        return 0

    lax.fori_loop(0, TILES, settle, 0)
    for done in (keep_h, keep_o, keep_hf, keep_a, keep_gq, keep_g1):
        wait(done(seqs - 1))

    def finish(i, _):
        y_copy(i).wait_send()
        wait(last_gu(i))
        wait(last_gz(i))

        @pl.when(stage == 1)
        def _():
            for copy in act_copies(i):
                copy.wait_send()
            act_own(i).wait()
            act_arrival(other, i).wait_recv()

        @pl.when(stage == 0)
        def _():
            act_arrival(0, i).wait_recv()
            act_arrival(1, i).wait_recv()

        return 0

    lax.fori_loop(0, seqs, finish, 0)


def run_pipeline(weights, singles, ids, table, times, cot):
    rows, length = ids.shape
    width = cot.shape[2]
    seqs = rows // 2
    tokens = seqs * length
    padded = -(-table.shape[0] // 16) * 16
    dma = pltpu.SemaphoreType.DMA
    anywhere = pl.BlockSpec(memory_space=pl.ANY)
    local = pl.BlockSpec(memory_space=pltpu.VMEM)
    vm = pltpu.VMEM
    return pl.pallas_call(
        functools.partial(pipeline_kernel, seqs, length, width),
        out_shape=(
            jax.ShapeDtypeStruct((2, seqs, length, width // 4), BF),
            jax.ShapeDtypeStruct((16 + padded + rows, width + 128), F32),
            jax.ShapeDtypeStruct((4, tokens, width), BF),
            jax.ShapeDtypeStruct((12, tokens, width), BF),
        ),
        in_specs=[anywhere] * 4 + [local] * 12 + [anywhere],
        out_specs=(anywhere, local, anywhere, anywhere),
        scratch_shapes=[
            vm((TILES, width, width), BF),
            vm((2, 16, width // 2), F32),
            vm((padded, width), BF),
            vm((16, width), F32),
            vm((length, width), F32),
            vm((seqs, length, width), BF),
            vm((seqs, length, width), BF),
            vm((seqs, length, 128), F32),
            vm((seqs, length, 128), F32),
            vm((seqs, length, 3 * width), BF),
            vm((seqs, HEADS, length, length), BF),
            vm((seqs, length, width), BF),
            vm((seqs, 4, length, width), BF),
            vm((4, length, width), BF),
            vm((length, width), BF),
            vm((length, width), BF),
            vm((length, width), BF),
            vm((3, length, width), BF),
            vm((length, width), BF),
            vm((length, width), BF),
            vm((length, width), F32),
            vm((seqs, length, width), BF),
            vm((seqs, length, width), BF),
            vm((seqs, 4, length, width // 4), BF),
            vm((16 + padded + rows, width + 128), F32),
            dma((2 * TILES,)),
        ]
        + [dma((TILES,))] * 8
        + [
            dma((seqs,)),
            dma((seqs,)),
            dma((3,)),
            dma((seqs,)),
            dma((seqs, 4)),
            dma((2, seqs)),
            dma((11,)),
            dma((seqs, 5)),
        ],
        compiler_params=pltpu.CompilerParams(
            collective_id=0, has_side_effects=True, vmem_limit_bytes=62 * 2**20
        ),
    )(*weights, *singles, ids, table, times, cot)


def reduce_kernel(
    nz,
    half,
    rows,
    bits,
    fixed_in,
    moving_in,
    sums_in,
    grads_out,
    small_out,
    token_out,
    stamp_out,
    fixed,
    moving,
    parts,
    core_buf,
    x_buf,
    right_buf,
    left_buf,
    sums_buf,
    adds,
    adds_buf,
    stamps,
    fixed_sem,
    moving_sem,
    core_send,
    core_recv,
    x_send,
    x_recv,
    right_send,
    right_recv,
    left_send,
    left_recv,
    sums_send,
    sums_recv,
    adds_send,
    adds_recv,
    stamps_send,
    stamps_recv,
    final_send,
    final_recv,
):
    s = lax.axis_index("section")
    d = lax.axis_index("dp")
    part = lax.rem(s, 2)
    other = 1 - part
    core = lax.rem(d, 2)
    z = lax.div(d, 2)
    stage = lax.div(s, 2)
    x_dev = (flipped(s, 0), d)
    y_dev = (flipped(s, 1), d)
    c_dev = (s, flipped(d, 0))
    bit_devs = [(s, flipped(d, bit)) for bit in range(bits)]
    ends = nz - 1
    slots = moving.shape[0]
    width = 2 * half

    barrier = pltpu.get_barrier_semaphore()
    for device in [x_dev, y_dev] + bit_devs:
        pl.semaphore_signal(barrier, inc=1, device_id=device, device_id_type=MESH)

    middle_left = jnp.logical_and(z > 0, lax.rem(z, 2) == 0)
    middle_right = jnp.logical_and(z < ends, lax.rem(z, 2) == 1)

    @pl.when(middle_left)
    def _():
        pl.semaphore_signal(barrier, inc=1, device_id=(s, d - 2), device_id_type=MESH)

    @pl.when(middle_right)
    def _():
        pl.semaphore_signal(barrier, inc=1, device_id=(s, d + 2), device_id_type=MESH)

    def load_fixed(index):
        return pltpu.make_async_copy(fixed_in.at[index], fixed.at[index], fixed_sem.at[index])

    def tile_at(turn):
        pair = turn - 4
        return jnp.where(turn < 4, turn, 4 + lax.div(pair, 2) + 4 * lax.rem(pair, 2))

    def load_moving(turn):
        slot = lax.rem(turn, slots)
        return pltpu.make_async_copy(moving_in.at[tile_at(turn)], moving.at[slot], moving_sem.at[slot])

    for turn in range(slots):
        load_moving(jnp.int32(turn)).start()
        if turn == 0:
            load_fixed(0).start()
    for index in (1, 3, 2):
        load_fixed(index).start()

    neighbours = 2 + bits + middle_left.astype(jnp.int32) + middle_right.astype(jnp.int32)
    pl.semaphore_wait(barrier, neighbours)

    def core_copy(k):
        return pltpu.make_async_remote_copy(
            src_ref=parts.at[k, :, :, 1 - core],
            dst_ref=core_buf.at[k],
            send_sem=core_send.at[k],
            recv_sem=core_recv.at[k],
            device_id=c_dev,
            device_id_type=MESH,
        )

    def x_copy(k):
        return pltpu.make_async_remote_copy(
            src_ref=parts.at[k, other, :, core],
            dst_ref=x_buf.at[k],
            send_sem=x_send.at[k],
            recv_sem=x_recv.at[k],
            device_id=x_dev,
            device_id_type=MESH,
        )

    def right_copy(k, j):
        return pltpu.make_async_remote_copy(
            src_ref=parts.at[k, part, j, core],
            dst_ref=right_buf.at[k, j],
            send_sem=right_send.at[k, j],
            recv_sem=right_recv.at[k, j],
            device_id=(s, d + 2),
            device_id_type=MESH,
        )

    def left_copy(k, j):
        return pltpu.make_async_remote_copy(
            src_ref=parts.at[k, part, j, core],
            dst_ref=left_buf.at[k, j],
            send_sem=left_send.at[k, j],
            recv_sem=left_recv.at[k, j],
            device_id=(s, d - 2),
            device_id_type=MESH,
        )

    def right_step(k):
        for j in range(ends, -1, -1):

            @pl.when(jnp.logical_and(z > 0, j >= z))
            def _():
                right_copy(k, j).wait_recv()

            @pl.when(jnp.logical_and(z > 0, j > z))
            def _():
                both = parts[k, part, j, core].astype(F32) + right_buf[k, j].astype(F32)
                parts[k, part, j, core] = both.astype(BF)

            @pl.when(j > z)
            def _():
                right_copy(k, j).start()

    def left_step(k):
        for j in range(nz):

            @pl.when(jnp.logical_and(z < ends, j <= z))
            def _():
                left_copy(k, j).wait_recv()

            @pl.when(jnp.logical_and(z < ends, j < z))
            def _():
                both = parts[k, part, j, core].astype(F32) + left_buf[k, j].astype(F32)
                parts[k, part, j, core] = both.astype(BF)

            @pl.when(j < z)
            def _():
                left_copy(k, j).start()

    def close_step(k):
        @pl.when(z == 0)
        def _():
            grads_out[k] = parts[k, part, z, core].astype(F32) + left_buf[k, z].astype(F32)

        @pl.when(z == ends)
        def _():
            grads_out[k] = parts[k, part, z, core].astype(F32) + right_buf[k, z].astype(F32)

        @pl.when(jnp.logical_and(z > 0, z < ends))
        def _():
            sides = left_buf[k, z].astype(F32) + right_buf[k, z].astype(F32)
            grads_out[k] = parts[k, part, z, core].astype(F32) + sides

    vectors = small_out.shape[0]
    count = adds.shape[1]
    own_stamps = sums_in.shape[0] - count

    def sums_copy():
        return pltpu.make_async_remote_copy(
            src_ref=sums_in,
            dst_ref=sums_buf,
            send_sem=sums_send,
            recv_sem=sums_recv,
            device_id=x_dev,
            device_id_type=MESH,
        )

    def adds_copy(bit):
        return pltpu.make_async_remote_copy(
            src_ref=adds.at[bit],
            dst_ref=adds_buf.at[bit],
            send_sem=adds_send.at[bit],
            recv_sem=adds_recv.at[bit],
            device_id=bit_devs[bit],
            device_id_type=MESH,
        )

    def block(bit, place):
        size = own_stamps * 2**bit
        return pl.ds(pl.multiple_of(lax.div(place, 2**bit) * size, 8), size)

    def stamps_copy(bit):
        return pltpu.make_async_remote_copy(
            src_ref=stamps.at[block(bit, d)],
            dst_ref=stamps.at[block(bit, d)],
            send_sem=stamps_send.at[bit],
            recv_sem=stamps_recv.at[bit],
            device_id=bit_devs[bit],
            device_id_type=MESH,
        )

    def stamps_arrival(bit):
        place = block(bit, bit_devs[bit][1])
        return pltpu.make_async_remote_copy(
            src_ref=stamps.at[place],
            dst_ref=stamps.at[place],
            send_sem=stamps_send.at[bit],
            recv_sem=stamps_recv.at[bit],
            device_id=bit_devs[bit],
            device_id_type=MESH,
        )

    def final_copies():
        pairs = ((adds.at[bits, pl.ds(vectors, count - vectors)], token_out), (stamps, stamp_out))
        return [
            pltpu.make_async_remote_copy(
                src_ref=src,
                dst_ref=dst,
                send_sem=final_send.at[index],
                recv_sem=final_recv.at[index],
                device_id=y_dev,
                device_id_type=MESH,
            )
            for index, (src, dst) in enumerate(pairs)
        ]

    def small_step(t):
        @pl.when(t == 2)
        def _():
            sums_copy().wait_recv()
            adds[0] = sums_in[:count, : 2 * half] + sums_buf[:count, : 2 * half]
            stamps[block(0, d), :] = sums_in[count:, :] + sums_buf[count:, :]
            adds_copy(0).start()
            stamps_copy(0).start()

        for bit in range(bits):

            @pl.when(t == 4 + 2 * bit)
            def _():
                adds_copy(bit).wait_recv()
                stamps_arrival(bit).wait_recv()
                adds[bit + 1] = adds[bit] + adds_buf[bit]
                if bit + 1 < bits:
                    adds_copy(bit + 1).start()
                    stamps_copy(bit + 1).start()

        @pl.when(t == 5 + 2 * bits)
        def _():
            small_out[...] = adds[bits, :vectors]

            @pl.when(stage == 0)
            def _():
                for copy in final_copies():
                    copy.start()
                token_out[...] = adds[bits, vectors:]
                stamp_out[...] = stamps[...]

    sums_copy().start()

    def product(turn):
        load_moving(turn).wait()
        m = tile_at(turn)
        slot = lax.rem(turn, slots)

        @pl.when(m == 0)
        def _():
            load_fixed(0).wait()

        @pl.when(m == 4)
        def _():
            load_fixed(1).wait()

        @pl.when(m == 7)
        def _():
            load_fixed(2).wait()

        @pl.when(m == 8)
        def _():
            load_fixed(3).wait()

        @pl.when(m < 8)
        def _():
            upper = (m >= 4).astype(jnp.int32) + (m >= 7).astype(jnp.int32)
            value = mul_tn(fixed[upper], moving[slot]).astype(BF)
            parts[m] = value.reshape(2, nz, 2, rows, width)

        @pl.when(m >= 8)
        def _():
            value = mul_tn(moving[slot], fixed[3]).astype(BF).reshape(2, 2, 4, rows, width)
            for block in range(4):
                parts[8 + block, :, m - 8] = value[:, :, block]

        @pl.when(turn + slots < TILES)
        def _():
            load_moving(turn + slots).start()

    def inside(k):
        return jnp.logical_and(k >= 0, k < TILES)

    def step(t, _):
        @pl.when(t < 4)
        def _():
            product(t)

        @pl.when(jnp.logical_and(t >= 4, t < 8))
        def _():
            product(4 + 2 * (t - 4))
            product(5 + 2 * (t - 4))

        @pl.when(t < TILES)
        def _():
            core_copy(t).start()

        small_step(t)

        k1 = t - 1

        @pl.when(inside(k1))
        def _():
            core_copy(k1).wait_recv()
            for side in range(2):
                both = parts[k1, side, :, core].astype(F32) + core_buf[k1, side].astype(F32)
                parts[k1, side, :, core] = both.astype(BF)
            x_copy(k1).start()

        k2 = t - 2

        @pl.when(inside(k2))
        def _():
            x_copy(k2).wait_recv()
            both = parts[k2, part, :, core].astype(F32) + x_buf[k2].astype(F32)
            parts[k2, part, :, core] = both.astype(BF)

        k3 = t - 2 - z

        @pl.when(inside(k3))
        def _():
            right_step(k3)

        k4 = t - 2 - (ends - z)

        @pl.when(inside(k4))
        def _():
            left_step(k4)

        k5 = jnp.minimum(k3, k4)

        @pl.when(inside(k5))
        def _():
            close_step(k5)

        return 0

    lax.fori_loop(0, TILES + 2 + ends, step, 0)

    def settle(k, _):
        core_copy(k).wait_send()
        x_copy(k).wait_send()
        for j in range(nz):

            @pl.when(j > z)
            def _():
                right_copy(k, j).wait_send()

            @pl.when(j < z)
            def _():
                left_copy(k, j).wait_send()

        return 0

    lax.fori_loop(0, TILES, settle, 0)
    sums_copy().wait_send()
    for bit in range(bits):
        adds_copy(bit).wait_send()
        stamps_copy(bit).wait_send()

    @pl.when(stage == 0)
    def _():
        for copy in final_copies():
            copy.wait_send()

    @pl.when(stage == 1)
    def _():
        for copy in final_copies():
            copy.wait_recv()


def run_reduce(fixed, moving, sums, vectors, stamp_rows, replicas):
    tokens, width = fixed.shape[1:]
    nz = replicas // 2
    half = width // 2
    rows = half // replicas
    dma = pltpu.SemaphoreType.DMA
    vm = pltpu.VMEM
    slots = 3
    bits = replicas.bit_length() - 1
    count = sums.shape[0] - stamp_rows
    local = pl.BlockSpec(memory_space=pltpu.VMEM)
    return pl.pallas_call(
        functools.partial(reduce_kernel, nz, half, rows, bits),
        out_shape=(
            jax.ShapeDtypeStruct((TILES, rows, width), F32),
            jax.ShapeDtypeStruct((vectors, width), F32),
            jax.ShapeDtypeStruct((count - vectors, width), F32),
            jax.ShapeDtypeStruct((stamp_rows * replicas, sums.shape[1]), F32),
        ),
        in_specs=[pl.BlockSpec(memory_space=pl.ANY)] * 2 + [local],
        out_specs=(local,) * 4,
        scratch_shapes=[
            vm((4, tokens, width), BF),
            vm((slots, tokens, width), BF),
            vm((TILES, 2, nz, 2, rows, width), BF),
            vm((TILES, 2, nz, rows, width), BF),
            vm((TILES, nz, rows, width), BF),
            vm((TILES, nz, rows, width), BF),
            vm((TILES, nz, rows, width), BF),
            vm(sums.shape, F32),
            vm((bits + 1, count, width), F32),
            vm((bits, count, width), F32),
            vm((stamp_rows * replicas, sums.shape[1]), F32),
            dma((4,)),
            dma((slots,)),
            dma((TILES,)),
            dma((TILES,)),
            dma((TILES,)),
            dma((TILES,)),
            dma((TILES, nz)),
            dma((TILES, nz)),
            dma((TILES, nz)),
            dma((TILES, nz)),
            dma,
            dma,
            dma((bits,)),
            dma((bits,)),
            dma((bits,)),
            dma((bits,)),
            dma((2,)),
            dma((2,)),
        ],
        compiler_params=pltpu.CompilerParams(
            collective_id=1, has_side_effects=True, vmem_limit_bytes=62 * 2**20
        ),
    )(fixed, moving, sums)


def three_parts(value):
    first = value.astype(BF)
    rest = value - first.astype(F32)
    second = rest.astype(BF)
    return first, second, (rest - second.astype(F32)).astype(BF)


def finish_kernel(
    replicas,
    act,
    grads,
    small,
    token,
    stamp,
    act_out,
    token_out,
    time_out,
    ga_out,
    sa_out,
    qkv_out,
    bq_out,
    bv_out,
    proj_out,
    bo_out,
    gm_out,
    sm_out,
    up_out,
    bup_out,
    down_out,
    bdown_out,
):
    s = lax.axis_index("section")
    d = lax.axis_index("dp")
    part = lax.rem(s, 2)
    rows, width = grads.shape[1:]
    half = width // 2
    quarter = width // 4
    seqs = act.shape[1]
    for side in range(2):
        act_out[side * seqs : (side + 1) * seqs] = act[side].astype(F32)
    for j in range(4):
        for side in range(2):
            first = side * 4 * half + j * half
            up_out[0, :, first : first + half] = grads[j, :, side * half : (side + 1) * half]
    for j in range(3):
        qkv_out[0, :, j * width : (j + 1) * width] = grads[4 + j]
    proj_out[0] = grads[7]
    for j in range(4):
        down_out[0, j * rows : (j + 1) * rows, :] = grads[8 + j]
    halves = small[:, pl.ds(pl.multiple_of(part * half, 128), half)]
    turned = pltpu.roll(halves, lax.rem(half - d * rows, half), 1)
    outs = (ga_out, sa_out, bq_out, bv_out, bo_out, gm_out, sm_out, bdown_out)
    for index, out in enumerate(outs):
        out[...] = turned[index : index + 1, :rows]
    per_row = half // (4 * rows)
    ups = small[pl.ds(8 + lax.div(d, per_row), 1), pl.ds(pl.multiple_of(part * half, 128), half)]
    ups = pltpu.roll(jnp.broadcast_to(ups, (8, half)), lax.rem(half - lax.rem(d, per_row) * 4 * rows, half), 1)
    bup_out[...] = ups[0:1, : 4 * rows]
    times_count = time_out.shape[0]
    spread = -(-times_count // 128) * 128
    place = lax.broadcasted_iota(jnp.int32, (stamp.shape[0], spread), 1).astype(F32)
    hot = (place == stamp[:, width : width + 1]).astype(F32).astype(BF)
    for q in range(4):

        @pl.when(s == q)
        def _():
            at = slice(q * quarter, (q + 1) * quarter)
            token_out[...] = token[: token_out.shape[0], at]
            sums = jnp.zeros((spread, quarter), F32)
            for piece in three_parts(stamp[:, at]):
                sums = sums + mul_tn(hot, piece)
            time_out[...] = sums[:times_count]


def run_finish(act, grads, small, token, stamp, letters_count, times_count, replicas):
    rows, width = grads.shape[1:]
    length = act.shape[2]
    quarter = width // 4
    local = pl.BlockSpec(memory_space=pltpu.VMEM)
    single = (1, rows)
    shapes = [
        (2 * act.shape[1], length, quarter),
        (letters_count, quarter),
        (times_count, quarter),
        single,
        single,
        (1, rows, 3 * width),
        single,
        single,
        (1, rows, width),
        single,
        single,
        single,
        (1, rows, 4 * width),
        (1, 4 * rows),
        (1, 4 * rows, width),
        single,
    ]
    return pl.pallas_call(
        functools.partial(finish_kernel, replicas),
        out_shape=tuple(jax.ShapeDtypeStruct(shape, F32) for shape in shapes),
        in_specs=[local] * 5,
        out_specs=(local,) * len(shapes),
        compiler_params=pltpu.CompilerParams(vmem_limit_bytes=60 * 2**20),
    )(act, grads, small, token, stamp)


def plain_reduce(fixed, moving, lower):
    def grad(left, right):
        return jnp.einsum("tk,tn->kn", left, right, preferred_element_type=F32)

    width = fixed.shape[2]
    half = width // 2
    hf, h, o, gz = (fixed[index] for index in range(4))
    ups = jnp.stack([grad(hf, moving[j]) for j in range(4)])
    up = ups.reshape(4, width, 2, half).transpose(1, 2, 0, 3).reshape(width, 4 * width)
    joint = jnp.concatenate([grad(h, moving[4 + j]) for j in range(3)], axis=1)
    proj = grad(o, moving[7])
    downs = jnp.stack([grad(moving[8 + j], gz) for j in range(4)])
    down = downs.reshape(4, 2, half, width).transpose(1, 0, 2, 3).reshape(4 * width, width)
    results = []
    for total in (joint, proj, up, down):
        halves = total.reshape((2, total.shape[0] // 2) + total.shape[1:])
        summed = lax.psum_scatter(halves, "dp", scatter_dimension=1, tiled=True)
        ours = jnp.where(lower, summed[0], summed[1])
        theirs = jnp.where(lower, summed[1], summed[0]).astype(BF)
        pairs = [(i, i ^ 1) for i in range(lax.axis_size("section"))]
        results.append((ours + lax.ppermute(theirs, "section", pairs).astype(F32))[None])
    return results


def per_device(
    token_ids,
    timesteps,
    token_table,
    time_table,
    attn_gain,
    attn_shift,
    qkv_weight,
    query_bias,
    value_bias,
    proj_weight,
    proj_bias,
    mlp_gain,
    mlp_shift,
    up_weight,
    up_bias,
    down_weight,
    down_bias,
    cotangent,
):
    section = lax.axis_index("section")
    replica = lax.axis_index("dp")
    replicas = lax.axis_size("dp")
    rows, length = token_ids.shape
    width = cotangent.shape[2]
    half = width // 2
    layer = section // 2
    part = section % 2
    letters_count = token_table.shape[0]
    times_count = time_table.shape[0]
    padded = -(-letters_count // 16) * 16
    singles = (
        attn_gain,
        attn_shift,
        query_bias,
        value_bias,
        proj_bias,
        mlp_gain,
        mlp_shift,
        down_bias,
        up_bias,
    )
    marks = jnp.broadcast_to(timesteps.astype(F32)[:, None], (rows, 128))
    times = time_table.at[timesteps].get(mode="promise_in_bounds").astype(F32)
    times = jnp.concatenate([times, marks], axis=1)
    weights = (qkv_weight, proj_weight, up_weight, down_weight)
    act, sums, fixed, moving = run_pipeline(weights, singles, token_ids, token_table, times, cotangent)
    vectors = 16
    if half % (16 * replicas) == 0 and replicas & (replicas - 1) == 0:
        grads, small, token, stamp = run_reduce(fixed, moving, sums, vectors, rows, replicas)
        return run_finish(act, grads, small, token, stamp, letters_count, times_count, replicas)
    qkv_grad, proj_grad, up_grad, down_grad = plain_reduce(fixed, moving, part == 0)
    activations = act.reshape(rows, length, width // 4).astype(F32)
    mine = jnp.zeros((2, vectors, width + 128), F32)
    mine = lax.dynamic_update_slice_in_dim(mine, sums[None, :vectors], layer, 0)
    placed = jnp.zeros((rows * replicas, width + 128), F32)
    placed = lax.dynamic_update_slice_in_dim(placed, sums[vectors + padded :], replica * rows, 0)
    joined = jnp.concatenate(
        [sums[vectors : vectors + padded], mine.reshape(2 * vectors, width + 128), placed], axis=0
    )
    joined = lax.psum(joined, ("section", "dp"))
    quarter = width // 4
    columns = lax.dynamic_slice_in_dim(joined, section * quarter, quarter, axis=1)
    token_grad = columns[:letters_count]
    first = padded + 2 * vectors
    steps = jnp.arange(times_count, dtype=jnp.int32).astype(F32)
    hot = (steps[:, None] == joined[first:, width][None, :]).astype(F32)
    time_grad = jnp.einsum("tb,bd->td", hot, columns[first:], precision=HIGHEST)
    ours = lax.dynamic_slice(joined, (padded + vectors * layer, part * half), (vectors, half))
    each = half // replicas
    flat = lax.dynamic_slice_in_dim(ours[:8], replica * each, each, axis=1)
    ups = lax.dynamic_slice_in_dim(ours[8:12].reshape(1, 4 * half), replica * 4 * each, 4 * each, axis=1)
    return (
        activations,
        token_grad,
        time_grad,
        flat[0:1],
        flat[1:2],
        qkv_grad,
        flat[2:3],
        flat[3:4],
        proj_grad,
        flat[4:5],
        flat[5:6],
        flat[6:7],
        up_grad,
        ups,
        down_grad,
        flat[7:8],
    )


def solution(mesh):
    return jax.shard_map(
        per_device,
        mesh=mesh,
        in_specs=(
            P("dp", None),
            P("dp"),
            P(),
            P(),
            P("section", None),
            P("section", None),
            P("section", None, None),
            P("section", None),
            P("section", None),
            P("section", None, None),
            P("section", None),
            P("section", None),
            P("section", None),
            P("section", None, None),
            P("section", None),
            P("section", None, None),
            P("section", None),
            P("dp", None, None),
        ),
        out_specs=(
            P("dp", None, "section"),
            P(None, "section"),
            P(None, "section"),
            P("section", "dp"),
            P("section", "dp"),
            P("section", "dp", None),
            P("section", "dp"),
            P("section", "dp"),
            P("section", "dp", None),
            P("section", "dp"),
            P("section", "dp"),
            P("section", "dp"),
            P("section", "dp", None),
            P("section", "dp"),
            P("section", "dp", None),
            P("section", "dp"),
        ),
        check_vma=False,
    )
```

```python
import functools
import math

import jax
import jax.numpy as jnp
from jax import lax
from jax.experimental import pallas as pl
from jax.experimental.pallas import tpu as pltpu
from jax.sharding import PartitionSpec as P

HEADS = 12
EPS = 1e-05
HIGHEST = lax.Precision.HIGHEST
MESH = pl.DeviceIdType.MESH
BF = jnp.bfloat16
F32 = jnp.float32
TILES = 12
QKV, PROJ, UP, DOWN = 0, 3, 4, 8
GELU_A = math.sqrt(2.0 / math.pi)
GELU_B = 0.044715


def flipped(value, bit):
    mask = 2**bit
    return value + mask - 2 * mask * lax.rem(lax.div(value, mask), 2)


def mul(a, b):
    return lax.dot_general(a, b, (((1,), (0,)), ((), ())), preferred_element_type=F32)


def mul_nt(a, b):
    return lax.dot_general(a, b, (((1,), (1,)), ((), ())), preferred_element_type=F32)


def mul_tn(a, b):
    return lax.dot_general(a, b, (((0,), (0,)), ((), ())), preferred_element_type=F32)


def normalize(x):
    mean = jnp.mean(x, axis=-1, keepdims=True)
    centered = x - mean
    spread = jnp.mean(centered * centered, axis=-1, keepdims=True)
    rate = lax.rsqrt(spread + EPS)
    return centered * rate, rate


def scaled_back(gh, gain, n, rate):
    gn = gh * gain
    inner = jnp.mean(gn * n, axis=-1, keepdims=True)
    return (gn - jnp.mean(gn, axis=-1, keepdims=True) - n * inner) * rate


def column(values):
    return jnp.sum(values, axis=0, keepdims=True)


class Refs:
    def __init__(self, names, refs):
        for name, ref in zip(names, refs, strict=True):
            setattr(self, name, ref)


INPUTS = (
    "qkv_in proj_in up_in down_in ga_in sa_in bq_in bv_in bo_in gm_in sm_in bdown_in bup_in "
    "ids_in table_in time_in cot_in"
).split()


def layer_kernel(seqs, length, width, fused, names, *all_refs):
    refs = Refs(names, all_refs)
    w, par, qkv, probs = refs.w, refs.par, refs.qkv, refs.probs
    xs, acc, ybuf, ysend, y1 = refs.xs, refs.acc, refs.ybuf, refs.ysend, refs.y1
    slope, gate, h_s, o_s, hf_s, go_s = refs.slope, refs.gate, refs.h_s, refs.o_s, refs.hf_s, refs.go_s
    act, landed, gsum = refs.act, refs.landed, refs.gsum
    s = lax.axis_index("section")
    d = lax.axis_index("dp")
    stage = lax.div(s, 2)
    part = lax.rem(s, 2)
    other = 1 - part
    core = lax.rem(d, 2)
    z = lax.div(d, 2)
    x_dev = (flipped(s, 0), d)
    y_dev = (flipped(s, 1), d)
    far_dev = (flipped(flipped(s, 0), 1), d)
    z_dev = (s, flipped(d, 1))
    c_dev = (s, flipped(d, 0))
    half = width // 2
    wide = width // 4
    hidden_half = 4 * half
    rows = w.shape[4]
    mine = lax.rem(d, 4)
    across = flipped(mine, 1)
    scale = 1.0 / math.sqrt(width // HEADS)
    letters_count = refs.table_in.shape[0]
    padded = refs.table.shape[0]
    vectors = 16
    count = vectors + padded
    nz = lax.axis_size("dp") // 2
    zbits = nz.bit_length() - 1
    ends = nz - 1

    def send(src, dst, send_sem, recv_sem, device):
        return pltpu.make_async_remote_copy(
            src_ref=src,
            dst_ref=dst,
            send_sem=send_sem,
            recv_sem=recv_sem,
            device_id=device,
            device_id_type=MESH,
        )

    def start(copies):
        for copy in copies:
            copy.start()

    def wait(copies):
        for copy in copies:
            copy.wait()

    def signal(sem, device):
        pl.semaphore_signal(sem, inc=1, device_id=device, device_id_type=MESH)

    barrier = pltpu.get_barrier_semaphore()
    greeted = [x_dev, y_dev, far_dev, c_dev, z_dev]
    if fused:
        greeted += [(s, flipped(d, 1 + bit)) for bit in range(1, zbits)]
    for device in greeted:
        signal(barrier, device)
    expected = len(greeted)
    if fused:
        middle_left = jnp.logical_and(z > 0, lax.rem(z, 2) == 0)
        middle_right = jnp.logical_and(z < ends, lax.rem(z, 2) == 1)

        @pl.when(middle_left)
        def _():
            signal(barrier, (s, d - 2))

        @pl.when(middle_right)
        def _():
            signal(barrier, (s, d + 2))

        expected = expected + middle_left.astype(jnp.int32) + middle_right.astype(jnp.int32)

    def tile(index):
        return w[index].reshape(width, width)

    def own_copies(index):
        if index < PROJ:
            pairs = [(refs.qkv_in.at[:, :, :, pl.ds(index * width, width)], w.at[index, part])]
        elif index < UP:
            pairs = [(refs.proj_in, w.at[index, part])]
        elif index < DOWN:
            pairs = [
                (
                    refs.up_in.at[:, :, :, pl.ds(side * hidden_half + (index - UP) * half, half)],
                    w.at[index, part, :, :, :, pl.ds(side * half, half)],
                )
                for side in range(2)
            ]
        else:
            pairs = [(refs.down_in.at[index - DOWN], w.at[index, part])]
        return [
            pltpu.make_async_copy(src, dst, refs.own_sem.at[2 * index + k])
            for k, (src, dst) in enumerate(pairs)
        ]

    def x_weight(index):
        place = w.at[index, part, mine]
        return send(place, place, refs.wx_send.at[index], refs.wx_recv.at[index], x_dev)

    def relay(index, which, send_sem, recv_sem, device):
        place = w.at[index, other, which]
        return send(place, place, send_sem.at[index], recv_sem.at[index], device)

    def z_weight(index):
        return relay(index, mine, refs.wz_send, refs.wz_recv, z_dev)

    def c1_weight(index):
        return relay(index, mine, refs.c1_send, refs.c1_recv, c_dev)

    def c2_weight(index):
        return relay(index, across, refs.c2_send, refs.c2_recv, c_dev)

    def pass_first(index):
        relay(index, mine, refs.wx_send, refs.wx_recv, x_dev).wait_recv()
        z_weight(index).start()
        c1_weight(index).start()

    def pass_second(index):
        relay(index, across, refs.wz_send, refs.wz_recv, z_dev).wait_recv()
        c2_weight(index).start()

    def ready(index):
        relay(index, flipped(mine, 0), refs.c1_send, refs.c1_recv, c_dev).wait_recv()
        relay(index, flipped(across, 0), refs.c2_send, refs.c2_recv, c_dev).wait_recv()

    def settle_weights():
        def settle(index, _):
            x_weight(index).wait_send()
            z_weight(index).wait_send()
            c1_weight(index).wait_send()
            c2_weight(index).wait_send()
            return 0

        lax.fori_loop(0, TILES, settle, 0)

    def vec_copy(which):
        place = refs.vecs.at[which]
        return send(place, place, refs.vec_sem.at[0], refs.vec_sem.at[1], x_dev)

    for index in range(TILES):
        start(own_copies(index))
    singles = ("ga", "sa", "bq", "bv", "bo", "gm", "sm", "bdown")
    for index, name in enumerate(singles):
        refs.vecs[part, index : index + 1, :] = getattr(refs, name + "_in")[...].astype(F32)
    for j in range(4):
        refs.vecs[part, 8 + j : 9 + j, :] = refs.bup_in[:, j * half : (j + 1) * half].astype(F32)
    refs.vecs[part, 12:16, :] = jnp.zeros((4, half), F32)
    refs.table[...] = jnp.zeros_like(refs.table)
    refs.table[:letters_count, :] = refs.table_in[...]
    gsum[...] = jnp.zeros_like(gsum)
    pl.semaphore_wait(barrier, expected)
    for index in range(TILES):
        wait(own_copies(index))
        x_weight(index).start()
        if index == 3:
            vec_copy(part).start()

    pass_first(0)
    pass_first(1)
    pass_second(0)
    pass_first(2)
    pass_second(1)
    pass_first(3)
    pass_second(2)
    pass_first(4)
    pass_second(3)
    pass_first(5)

    @pl.when(stage == 1)
    def _():
        def step(index, _):
            pass_second(index - 2)
            pass_first(index)
            return 0

        lax.fori_loop(6, TILES, step, 0)
        pass_second(TILES - 2)
        pass_second(TILES - 1)

    vec_copy(other).wait_recv()
    par[:, :half] = refs.vecs[0]
    par[:, half:] = refs.vecs[1]
    for index in range(UP):
        ready(index)

    def act_copies(i):
        slot = lax.rem(i, 2)
        return [
            send(
                act.at[slot, device[0]],
                landed.at[part, i],
                refs.act_send.at[i, index],
                refs.act_recv.at[part, i],
                device,
            )
            for index, device in enumerate((y_dev, x_dev, far_dev))
        ]

    def act_own(i):
        return pltpu.make_async_copy(act.at[lax.rem(i, 2), s], landed.at[part, i], refs.act_send.at[i, 3])

    def act_arrival(side, i):
        return send(act.at[0, 0], landed.at[side, i], refs.act_send.at[i, 0], refs.act_recv.at[side, i], y_dev)

    def act_settle(i):
        for copy in act_copies(i):
            copy.wait_send()

    def cot_copy(i):
        return pltpu.make_async_copy(refs.cot_in.at[part * seqs + i], ybuf.at[i], refs.cot_sem.at[i])

    def y_copy(i):
        return send(ysend.at[i], ybuf.at[i], refs.y_send.at[i], refs.y_recv.at[i], y_dev)

    def row(index):
        return par[index : index + 1, :]

    def add_row(index, values):
        gsum[index : index + 1, :width] += column(values)

    lane = lax.broadcasted_iota(jnp.int32, (length, 128), 1)
    low = lane < 64
    side_ones = [(lane < 64).astype(F32).astype(BF), (lane >= 64).astype(F32).astype(BF)]
    side_scaled = [
        ((lane < 64).astype(F32) * scale).astype(BF),
        ((lane >= 64).astype(F32) * scale).astype(BF),
    ]
    pairs = HEADS // 2

    def letters(i):
        ids = refs.ids_in[pl.ds(part * seqs + i, 1), :]
        place = lax.broadcasted_iota(jnp.int32, (padded, length), 0)
        return (place == ids).astype(F32).astype(BF)

    def attn_fwd(i):
        @pl.when(stage == 0)
        def _():
            xs[...] = mul_tn(letters(i), refs.table[...]) + refs.time_in[pl.ds(part * seqs + i, 1), :width]

        @pl.when(stage == 1)
        def _():
            y_copy(i).wait_recv()
            xs[...] = ybuf[i].astype(F32)
            cot_copy(i).start()

        n, rate = normalize(xs[...])
        refs.n_a[i] = n.astype(BF)
        refs.r_a[i] = jnp.broadcast_to(rate, (length, 128))
        h_s[i] = (n * row(0) + row(1)).astype(BF)
        for j in range(3):
            joint = mul(h_s[i], tile(QKV + j))
            if j == 0:
                joint = joint + row(2)
            if j == 2:
                joint = joint + row(3)
            qkv[i, :, j * width : (j + 1) * width] = joint.astype(BF)

        for hp in range(pairs):
            at = hp * 128
            q2 = qkv[i, :, at : at + 128]
            k2 = qkv[i, :, width + at : width + at + 128]
            for side in range(2):
                scores = mul_nt(q2 * side_scaled[side], k2)
                expo = jnp.exp(scores - jnp.max(scores, axis=-1, keepdims=True))
                total = jnp.sum(expo, axis=-1, keepdims=True)
                probs[i, 2 * hp + side] = (expo * (1.0 / total)).astype(BF)
        for hp in range(pairs):
            at = hp * 128
            v2 = qkv[i, :, 2 * width + at : 2 * width + at + 128]
            outs = [mul(probs[i, 2 * hp + side], v2) for side in range(2)]
            o_s[i, :, at : at + 128] = jnp.where(low, outs[0], outs[1]).astype(BF)
        y1[i] = (xs[...] + (mul(o_s[i], tile(PROJ)) + row(4))).astype(BF)

    def feed_fwd(i):
        def arrived(first, last):
            @pl.when(i == 0)
            def _():
                def one(index, _):
                    ready(index)
                    return 0

                lax.fori_loop(first, last, one, 0)

        arrived(UP, DOWN)
        x = y1[i].astype(F32)
        n, rate = normalize(x)
        refs.n_f[i] = n.astype(BF)
        refs.r_f[i] = jnp.broadcast_to(rate, (length, 128))
        hf_s[i] = (n * row(5) + row(6)).astype(BF)
        acc[...] = x + row(7)
        for j in range(4):
            u = mul(hf_s[i], tile(UP + j)) + row(8 + j)
            square = u * u
            t = jnp.tanh(u * (GELU_A + GELU_A * GELU_B * square))
            both = 0.5 + 0.5 * t
            gate[i, j] = (u * both).astype(BF)
            bend = (0.5 * GELU_A + 1.5 * GELU_A * GELU_B * square) * u
            slope[i, j] = (both + bend * (1.0 - t * t)).astype(BF)
        arrived(DOWN, TILES)
        down = mul(gate[i, 0], tile(DOWN))
        for j in range(1, 4):
            down = down + mul(gate[i, j], tile(DOWN + j))
        acc[...] += down

        @pl.when(stage == 0)
        def _():
            ysend[i] = acc[...].astype(BF)
            y_copy(i).start()

        @pl.when(stage == 1)
        def _():
            @pl.when(i >= 2)
            def _():
                act_settle(i - 2)
                act_own(i - 2).wait()

            for q in range(4):
                act[lax.rem(i, 2), q] = acc[:, q * wide : (q + 1) * wide].astype(BF)
            start(act_copies(i))
            act_own(i).start()

    def feed_bwd(i):
        @pl.when(stage == 0)
        def _():
            y_copy(i).wait_recv()

        @pl.when(stage == 1)
        def _():
            cot_copy(i).wait()

        add_row(7, ybuf[i].astype(F32))
        for j in range(4):
            ga = mul_nt(ybuf[i], tile(DOWN + j))
            gu = (ga * slope[i, j].astype(F32)).astype(BF)
            slope[i, j] = gu
            add_row(8 + j, gu.astype(F32))
        gh = mul_nt(slope[i, 0], tile(UP))
        for j in range(1, 4):
            gh = gh + mul_nt(slope[i, j], tile(UP + j))
        n = refs.n_f[i].astype(F32)
        add_row(5, gh * n)
        add_row(6, gh)
        gx = ybuf[i].astype(F32) + scaled_back(gh, row(5), n, refs.r_f[i][:, 0:1])
        y1[i] = gx.astype(BF)

    def attn_bwd(i):
        add_row(4, y1[i].astype(F32))
        go_s[...] = mul_nt(y1[i], tile(PROJ)).astype(BF)
        for hp in range(pairs):
            at = hp * 128
            v2 = qkv[i, :, 2 * width + at : 2 * width + at + 128]
            go2 = go_s[:, at : at + 128]
            gv = []
            for side in range(2):
                pb = probs[i, 2 * hp + side]
                gp = mul_nt(go2 * side_ones[side], v2)
                p = pb.astype(F32)
                pg = p * gp
                gs = (pg - p * jnp.sum(pg, axis=-1, keepdims=True)).astype(BF)
                gv.append(mul_tn(pb, go2))
                probs[i, 2 * hp + side] = gs
            qkv[i, :, 2 * width + at : 2 * width + at + 128] = jnp.where(low, gv[0], gv[1]).astype(BF)
        for hp in range(pairs):
            at = hp * 128
            q2 = qkv[i, :, at : at + 128]
            k2 = qkv[i, :, width + at : width + at + 128]
            gq, gk = [], []
            for side in range(2):
                gs = probs[i, 2 * hp + side]
                gq.append(mul(gs, k2))
                gk.append(mul_tn(gs, q2))
            qkv[i, :, at : at + 128] = (jnp.where(low, gq[0], gq[1]) * scale).astype(BF)
            qkv[i, :, width + at : width + at + 128] = (jnp.where(low, gk[0], gk[1]) * scale).astype(BF)
        pieces = [qkv[i, :, j * width : (j + 1) * width] for j in range(3)]
        add_row(2, pieces[0].astype(F32))
        add_row(3, pieces[2].astype(F32))
        gh = mul_nt(pieces[0], tile(QKV)) + mul_nt(pieces[1], tile(QKV + 1)) + mul_nt(pieces[2], tile(QKV + 2))
        n = refs.n_a[i].astype(F32)
        add_row(0, gh * n)
        add_row(1, gh)
        acc[...] = y1[i].astype(F32) + scaled_back(gh, row(0), n, refs.r_a[i][:, 0:1])

        @pl.when(stage == 1)
        def _():
            ysend[i] = acc[...].astype(BF)
            y_copy(i).start()

        @pl.when(stage == 0)
        def _():
            high = acc[...].astype(BF)
            rest = (acc[...] - high.astype(F32)).astype(BF)
            hot = letters(i)
            gsum[vectors:count, :width] += mul(hot, high) + mul(hot, rest)
            mark = part * seqs + i
            stamp = refs.time_in[pl.ds(mark, 1), :]
            gsum[pl.ds(count + mark, 1), :] = jnp.concatenate([column(acc[...]), stamp[:, width:]], axis=1)

    units = (attn_fwd, feed_fwd, feed_bwd, attn_bwd)
    steps = 0
    if fused:
        step = reduce_steps(refs, seqs, length, width, send, signal, act_arrival, act_own, settle_weights)
        units = units + (step,)
        steps = TILES + 2 + ends

    def unit(u, _):
        early = u < 2 * seqs
        kind0 = jnp.where(early, lax.div(u, seqs), 2 + lax.rem(u, 2))
        index0 = jnp.where(early, lax.rem(u, seqs), lax.div(u, 2) - seqs)
        kind1 = lax.rem(u, 4)
        index1 = lax.div(u, 4)
        if fused:
            last = 4 * seqs - 1
            ahead = 2
            kind0 = jnp.where(u >= last, 4, kind0)
            index0 = jnp.where(u >= last, jnp.where(u < last + ahead, u - last, u - last - 1), index0)
            kind0 = jnp.where(u == last + ahead, 3, kind0)
            index0 = jnp.where(u == last + ahead, seqs - 1, index0)
            kind1 = jnp.where(u > last, 4, kind1)
            index1 = jnp.where(u > last, u - last - 1, index1)
        kind = jnp.where(stage == 0, kind0, kind1)
        i = jnp.where(stage == 0, index0, index1)

        @pl.when(jnp.logical_and(stage == 0, jnp.logical_and(u >= 1, u <= 4)))
        def _():
            pass_second(2 + 2 * u)
            pass_second(3 + 2 * u)

        @pl.when(jnp.logical_and(stage == 0, jnp.logical_and(u >= 1, u <= 3)))
        def _():
            pass_first(4 + 2 * u)
            pass_first(5 + 2 * u)

        for index, run in enumerate(units):

            @pl.when(kind == index)
            def _():
                run(i)

        return 0

    lax.fori_loop(0, 4 * seqs + steps, unit, 0)

    vec_copy(part).wait_send()
    if not fused:
        settle_weights()

    def finish(i, _):
        y_copy(i).wait_send()

        @pl.when(jnp.logical_and(stage == 1, i >= 2))
        def _():
            act_settle(i)

        return 0

    lax.fori_loop(0, seqs, finish, 0)
    if not fused:

        @pl.when(stage == 1)
        def _():
            for i in range(2, seqs):
                act_own(i).wait()

        for i in range(seqs):
            for side in range(2):

                @pl.when(jnp.logical_or(stage == 0, part != side))
                def _():
                    act_arrival(side, i).wait_recv()

        refs.sums_out[...] = gsum[...]
        copies = []
        for i in range(seqs):
            place = pl.ds(i * length, length)
            for index, ref in enumerate((hf_s, h_s, o_s, ybuf)):
                copies.append((ref.at[i], refs.fixed_out.at[index, place]))
            for j in range(4):
                copies.append((slope.at[i, j], refs.moving_out.at[j, place]))
                copies.append((gate.at[i, j], refs.moving_out.at[8 + j, place]))
            for j in range(3):
                copies.append((qkv.at[i, :, pl.ds(j * width, width)], refs.moving_out.at[4 + j, place]))
            copies.append((y1.at[i], refs.moving_out.at[7, place]))
        copies.append((landed, refs.act_out))
        copies = [
            pltpu.make_async_copy(src, dst, refs.keep_sem.at[index]) for index, (src, dst) in enumerate(copies)
        ]
        start(copies)
        wait(copies)


def reduce_steps(refs, seqs, length, width, send, signal, act_arrival, act_own, settle_weights):
    s = lax.axis_index("section")
    d = lax.axis_index("dp")
    stage = lax.div(s, 2)
    part = lax.rem(s, 2)
    other = 1 - part
    core = lax.rem(d, 2)
    z = lax.div(d, 2)
    x_dev = (flipped(s, 0), d)
    y_dev = (flipped(s, 1), d)
    c_dev = (s, flipped(d, 0))
    right_dev = (s, d + 2)
    left_dev = (s, d - 2)
    w, gsum = refs.w, refs.gsum
    nz = w.shape[2]
    rows = w.shape[4]
    ends = nz - 1
    slots = refs.x_buf.shape[0]
    tokens = seqs * length
    core_buf, x_buf, right_buf, left_buf = refs.core_buf, refs.x_buf, refs.right_buf, refs.left_buf
    vectors = 16
    count = vectors + refs.table.shape[0]
    split = count // 2
    zbits = nz.bit_length() - 1
    own = gsum.shape[0] - count

    def where(k):
        return jnp.where(k < 4, k + 4, jnp.where(k < 8, k - 4, k))

    def slot(k):
        return lax.rem(k, slots)

    def core_copy(k):
        return send(
            w.at[where(k), :, :, 1 - core],
            core_buf.at[slot(k)],
            refs.core_send.at[k],
            refs.core_recv.at[k],
            c_dev,
        )

    def x_copy(k):
        return send(
            w.at[where(k), other, :, core], x_buf.at[slot(k)], refs.x_send.at[k], refs.x_recv.at[k], x_dev
        )

    def right_copy(k, j):
        return send(
            w.at[where(k), part, j, core],
            right_buf.at[slot(k), j],
            refs.right_send.at[k, j],
            refs.right_recv.at[k, j],
            right_dev,
        )

    def left_copy(k, j):
        return send(
            w.at[where(k), part, j, core],
            left_buf.at[slot(k), j],
            refs.left_send.at[k, j],
            refs.left_recv.at[k, j],
            left_dev,
        )

    def add_to(k, j, buffer):
        both = w[where(k), part, j, core].astype(F32) + buffer[slot(k), j].astype(F32)
        w[where(k), part, j, core] = both.astype(BF)

    def spend(k, credit):
        @pl.when(k >= slots)
        def _():
            pl.semaphore_wait(credit, 1)

    def grant(k, credit, device):
        @pl.when(k + slots < TILES)
        def _():
            signal(credit, device)

    def right_step(k):
        @pl.when(z < ends)
        def _():
            spend(k, refs.right_credit)

        for j in range(ends, -1, -1):

            @pl.when(jnp.logical_and(z > 0, j >= z))
            def _():
                right_copy(k, j).wait_recv()

            @pl.when(jnp.logical_and(z > 0, j > z))
            def _():
                add_to(k, j, right_buf)

            @pl.when(j > z)
            def _():
                right_copy(k, j).start()

    def left_step(k):
        @pl.when(z > 0)
        def _():
            spend(k, refs.left_credit)

        for j in range(nz):

            @pl.when(jnp.logical_and(z < ends, j <= z))
            def _():
                left_copy(k, j).wait_recv()

            @pl.when(jnp.logical_and(z < ends, j < z))
            def _():
                add_to(k, j, left_buf)

            @pl.when(j < z)
            def _():
                left_copy(k, j).start()

    def grads_copy(k):
        return pltpu.make_async_copy(refs.grad_stage, refs.grads_out.at[k], refs.out_sem.at[0])

    def act_copy(turn):
        return pltpu.make_async_copy(refs.act_stage, refs.act_out.at[turn], refs.out_sem.at[1])

    def close_step(k):
        base = w[where(k), part, z, core].astype(F32)

        @pl.when(k > 0)
        def _():
            grads_copy(k - 1).wait()

        @pl.when(z == 0)
        def _():
            refs.grad_stage[...] = base + left_buf[slot(k), z].astype(F32)

        @pl.when(z == ends)
        def _():
            refs.grad_stage[...] = base + right_buf[slot(k), z].astype(F32)

        @pl.when(jnp.logical_and(z > 0, z < ends))
        def _():
            sides = left_buf[slot(k), z].astype(F32) + right_buf[slot(k), z].astype(F32)
            refs.grad_stage[...] = base + sides

        grads_copy(k).start()

        @pl.when(z > 0)
        def _():
            grant(k, refs.right_credit, left_dev)

        @pl.when(z < ends)
        def _():
            grant(k, refs.left_credit, right_dev)

    def flat(value):
        return value.reshape(tokens, width)

    def store(k, value):
        w[where(k)] = value.astype(BF).reshape(2, nz, 2, rows, width)

    def products(t):
        @pl.when(t < 4)
        def _():
            store(t, mul_tn(flat(refs.hf_s[...]), flat(refs.slope[:, t])))

        for j in range(3):

            @pl.when(t == 4 + j)
            def _():
                store(t, mul_tn(flat(refs.h_s[...]), flat(refs.qkv[:, :, j * width : (j + 1) * width])))

        @pl.when(t == 7)
        def _():
            store(t, mul_tn(flat(refs.o_s[...]), flat(refs.y1[...])))

        @pl.when(jnp.logical_and(t >= 4, t < 8))
        def _():
            value = mul_tn(flat(refs.gate[:, t - 4]), flat(refs.ybuf[...])).astype(BF)
            value = value.reshape(2, 2, 4, rows, width)
            for block in range(4):
                w[8 + block, :, t - 4] = value[:, :, block]

    def inside(k):
        return jnp.logical_and(k >= 0, k < TILES)

    def core_sums():
        return send(
            gsum.at[pl.ds(0, count)], refs.sums_buf, refs.sums_sem.at[0], refs.sums_sem.at[1], c_dev
        )

    def x_sums():
        return [
            send(refs.adds.at[0], refs.adds_buf.at[0], refs.adds_send.at[0], refs.adds_recv.at[0], x_dev),
            send(
                gsum.at[pl.ds(count, own)],
                refs.stamp_buf,
                refs.stamp_send.at[0],
                refs.stamp_recv.at[0],
                x_dev,
            ),
        ]

    def block(bit, place_core, place_z):
        size = own * 2**bit
        first = place_core * nz * own + lax.div(place_z, 2**bit) * size
        return pl.ds(pl.multiple_of(first, 8), size)

    def z_sums(bit, arriving):
        there = flipped(z, bit)
        place = refs.stamps.at[block(bit, core, there if arriving else z)]
        device = (s, flipped(d, 1 + bit))
        return [
            send(
                refs.adds.at[1 + bit],
                refs.adds_buf.at[1 + bit],
                refs.adds_send.at[1 + bit],
                refs.adds_recv.at[1 + bit],
                device,
            ),
            send(place, place, refs.stamp_send.at[1 + bit], refs.stamp_recv.at[1 + bit], device),
        ]

    def last_sums(arriving):
        side = 1 - core if arriving else core
        place = refs.stamps.at[block(zbits, side, z)]
        half_sums = refs.whole.at[side]
        return [
            send(half_sums, half_sums, refs.sums_sem.at[2], refs.sums_sem.at[3], c_dev),
            send(place, place, refs.stamp_send.at[1 + zbits], refs.stamp_recv.at[1 + zbits], c_dev),
        ]

    def final_copies():
        return [
            send(src, dst, refs.final_send.at[index], refs.final_recv.at[index], y_dev)
            for index, (src, dst) in enumerate(((refs.whole, refs.token_out), (refs.stamps, refs.stamp_out)))
        ]

    def arrive(copies):
        for copy in copies:
            copy.wait_recv()

    def begin(copies):
        for copy in copies:
            copy.start()

    def small_step(t):
        @pl.when(t == 2)
        def _():
            core_sums().start()

        @pl.when(t == 4)
        def _():
            core_sums().wait_recv()
            sums = gsum[:count, :width] + refs.sums_buf[:, :width]

            @pl.when(core == 0)
            def _():
                refs.adds[0] = sums[:split]

            @pl.when(core == 1)
            def _():
                refs.adds[0] = sums[split:]

            begin(x_sums())

        @pl.when(t == 6)
        def _():
            arrive(x_sums())
            refs.adds[1] = refs.adds[0] + refs.adds_buf[0]
            refs.stamps[block(0, core, z), :] = gsum[count:, :] + refs.stamp_buf[...]
            begin(z_sums(0, False))

        for bit in range(zbits):

            @pl.when(t == 8 + 2 * bit)
            def _():
                arrive(z_sums(bit, True))
                total = refs.adds[1 + bit] + refs.adds_buf[1 + bit]
                if bit + 1 < zbits:
                    refs.adds[2 + bit] = total
                    begin(z_sums(bit + 1, False))
                else:
                    refs.whole[core] = total
                    begin(last_sums(False))

        @pl.when(t == 8 + 2 * zbits)
        def _():
            arrive(last_sums(True))
            refs.small_out[...] = refs.whole[...]

            @pl.when(stage == 0)
            def _():
                begin(final_copies())
                refs.token_out[...] = refs.whole[...]
                refs.stamp_out[...] = refs.stamps[...]

    def act_step(t):
        turn = t - 3

        @pl.when(jnp.logical_and(turn >= 0, turn < 2 * seqs))
        def _():
            side = lax.div(turn, seqs)
            i = lax.rem(turn, seqs)
            ours = jnp.logical_and(stage == 1, side == part)

            @pl.when(jnp.logical_not(ours))
            def _():
                act_arrival(side, i).wait_recv()

            @pl.when(jnp.logical_and(ours, i >= 2))
            def _():
                act_own(i).wait()

            @pl.when(turn > 0)
            def _():
                act_copy(turn - 1).wait()

            refs.act_stage[...] = refs.landed[side, i].astype(F32).T
            act_copy(turn).start()

    def step(t):
        @pl.when(t == 0)
        def _():
            settle_weights()

        products(t)

        @pl.when(t < TILES)
        def _():
            spend(t, refs.core_credit)
            core_copy(t).start()

        k1 = t - 1

        @pl.when(inside(k1))
        def _():
            core_copy(k1).wait_recv()
            for side in range(2):
                both = w[where(k1), side, :, core].astype(F32) + core_buf[slot(k1), side].astype(F32)
                w[where(k1), side, :, core] = both.astype(BF)
            grant(k1, refs.core_credit, c_dev)
            spend(k1, refs.x_credit)
            x_copy(k1).start()

        small_step(t)
        act_step(t)
        k2 = t - 2

        @pl.when(inside(k2))
        def _():
            x_copy(k2).wait_recv()
            both = w[where(k2), part, :, core].astype(F32) + x_buf[slot(k2)].astype(F32)
            w[where(k2), part, :, core] = both.astype(BF)
            grant(k2, refs.x_credit, x_dev)

        k3 = t - 2 - z

        @pl.when(inside(k3))
        def _():
            right_step(k3)

        k4 = t - 2 - (ends - z)

        @pl.when(inside(k4))
        def _():
            left_step(k4)

        k5 = jnp.minimum(k3, k4)

        @pl.when(inside(k5))
        def _():
            close_step(k5)

        @pl.when(t == TILES + 1 + ends)
        def _():
            finish()

    def finish():
        def settle(k, _):
            core_copy(k).wait_send()
            x_copy(k).wait_send()
            for j in range(nz):

                @pl.when(j > z)
                def _():
                    right_copy(k, j).wait_send()

                @pl.when(j < z)
                def _():
                    left_copy(k, j).wait_send()

            return 0

        lax.fori_loop(0, TILES, settle, 0)
        grads_copy(TILES - 1).wait()
        act_copy(2 * seqs - 1).wait()
        sends = [core_sums()] + x_sums() + last_sums(False)
        for bit in range(zbits):
            sends += z_sums(bit, False)
        for copy in sends:
            copy.wait_send()

        @pl.when(stage == 0)
        def _():
            for copy in final_copies():
                copy.wait_send()

        @pl.when(stage == 1)
        def _():
            arrive(final_copies())

    return step


def run_layers(weights, singles, ids, table, times, cot, replicas, fused):
    rows, length = ids.shape
    width = cot.shape[2]
    half = width // 2
    seqs = rows // 2
    tokens = seqs * length
    padded = -(-table.shape[0] // 16) * 16
    count = 16 + padded
    nz = replicas // 2
    lane = width + 128
    cut = half // 8
    slots = 3
    dma = pltpu.SemaphoreType.DMA
    credit = pltpu.SemaphoreType.REGULAR
    anywhere = pl.BlockSpec(memory_space=pl.ANY)
    local = pl.BlockSpec(memory_space=pltpu.VMEM)
    vm = pltpu.VMEM
    shape = jax.ShapeDtypeStruct
    if fused:
        outs = {
            "act_out": (shape((2 * seqs, width // 4, length), F32), anywhere),
            "grads_out": (shape((TILES, cut, width), F32), anywhere),
            "small_out": (shape((2, count // 2, width), F32), local),
            "token_out": (shape((2, count // 2, width), F32), local),
            "stamp_out": (shape((rows * replicas, lane), F32), local),
        }
    else:
        outs = {
            "act_out": (shape((2, seqs, length, width // 4), BF), anywhere),
            "sums_out": (shape((count + rows, lane), F32), local),
            "fixed_out": (shape((4, tokens, width), BF), anywhere),
            "moving_out": (shape((12, tokens, width), BF), anywhere),
        }
    scratch = {
        "w": vm((TILES, 2, 4, 2, cut, width), BF),
        "vecs": vm((2, 16, half), F32),
        "table": vm((padded, width), BF),
        "par": vm((16, width), F32),
        "xs": vm((length, width), F32),
        "acc": vm((length, width), F32),
        "n_a": vm((seqs, length, width), BF),
        "n_f": vm((seqs, length, width), BF),
        "r_a": vm((seqs, length, 128), F32),
        "r_f": vm((seqs, length, 128), F32),
        "qkv": vm((seqs, length, 3 * width), BF),
        "probs": vm((seqs, HEADS, length, length), BF),
        "y1": vm((seqs, length, width), BF),
        "slope": vm((seqs, 4, length, width), BF),
        "gate": vm((seqs, 4, length, width), BF),
        "h_s": vm((seqs, length, width), BF),
        "o_s": vm((seqs, length, width), BF),
        "hf_s": vm((seqs, length, width), BF),
        "go_s": vm((length, width), BF),
        "ybuf": vm((seqs, length, width), BF),
        "ysend": vm((seqs, length, width), BF),
        "act": vm((2, 4, length, width // 4), BF),
        "landed": vm((2, seqs, length, width // 4), BF),
        "gsum": vm((count + rows, lane), F32),
        "own_sem": dma((2 * TILES,)),
        "vec_sem": dma((2,)),
        "cot_sem": dma((seqs,)),
        "y_send": dma((seqs,)),
        "y_recv": dma((seqs,)),
        "act_send": dma((seqs, 4)),
        "act_recv": dma((2, seqs)),
    }
    for name in ("wx", "wz", "c1", "c2"):
        scratch[name + "_send"] = dma((TILES,))
        scratch[name + "_recv"] = dma((TILES,))
    if fused:
        zbits = nz.bit_length() - 1
        scratch |= {
            "core_buf": vm((slots, 2, nz, cut, width), BF),
            "x_buf": vm((slots, nz, cut, width), BF),
            "right_buf": vm((slots, nz, cut, width), BF),
            "left_buf": vm((slots, nz, cut, width), BF),
            "sums_buf": vm((count, lane), F32),
            "adds": vm((1 + zbits, count // 2, width), F32),
            "adds_buf": vm((1 + zbits, count // 2, width), F32),
            "whole": vm((2, count // 2, width), F32),
            "stamp_buf": vm((rows, lane), F32),
            "stamps": vm((rows * replicas, lane), F32),
            "grad_stage": vm((cut, width), F32),
            "act_stage": vm((width // 4, length), F32),
            "out_sem": dma((2,)),
            "sums_sem": dma((4,)),
            "adds_send": dma((1 + zbits,)),
            "adds_recv": dma((1 + zbits,)),
            "stamp_send": dma((2 + zbits,)),
            "stamp_recv": dma((2 + zbits,)),
            "final_send": dma((2,)),
            "final_recv": dma((2,)),
            "core_credit": credit,
            "x_credit": credit,
            "right_credit": credit,
            "left_credit": credit,
        }
        for name in ("core", "x"):
            scratch[name + "_send"] = dma((TILES,))
            scratch[name + "_recv"] = dma((TILES,))
        for name in ("right", "left"):
            scratch[name + "_send"] = dma((TILES, nz))
            scratch[name + "_recv"] = dma((TILES, nz))
    else:
        scratch["keep_sem"] = dma((16 * seqs + 1,))
    names = INPUTS + list(outs) + list(scratch)
    return pl.pallas_call(
        functools.partial(layer_kernel, seqs, length, width, fused, names),
        out_shape=tuple(out[0] for out in outs.values()),
        in_specs=[anywhere] * 4 + [local] * 12 + [anywhere],
        out_specs=tuple(out[1] for out in outs.values()),
        scratch_shapes=list(scratch.values()),
        compiler_params=pltpu.CompilerParams(
            collective_id=0, has_side_effects=True, vmem_limit_bytes=64 * 2**20 - 2**17
        ),
    )(*weights, *singles, ids, table, times, cot)


def three_parts(value):
    first = value.astype(BF)
    rest = value - first.astype(F32)
    second = rest.astype(BF)
    return first, second, (rest - second.astype(F32)).astype(BF)


def finish_kernel(
    act,
    grads,
    small,
    token,
    stamp,
    act_out,
    token_out,
    time_out,
    ga_out,
    sa_out,
    qkv_out,
    bq_out,
    bv_out,
    proj_out,
    bo_out,
    gm_out,
    sm_out,
    up_out,
    bup_out,
    down_out,
    bdown_out,
    sem,
):
    s = lax.axis_index("section")
    d = lax.axis_index("dp")
    part = lax.rem(s, 2)
    rows, width = grads.shape[1:]
    half = width // 2
    quarter = width // 4
    pairs = [(act, act_out)]
    for j in range(4):
        for side in range(2):
            first = side * 4 * half + j * half
            pairs.append((grads.at[j, :, pl.ds(side * half, half)], up_out.at[0, :, pl.ds(first, half)]))
    for j in range(3):
        pairs.append((grads.at[4 + j], qkv_out.at[0, :, pl.ds(j * width, width)]))
    pairs.append((grads.at[7], proj_out.at[0]))
    for j in range(4):
        pairs.append((grads.at[8 + j], down_out.at[0, pl.ds(j * rows, rows)]))
    copies = [pltpu.make_async_copy(src, dst, sem.at[index]) for index, (src, dst) in enumerate(pairs)]
    for copy in copies:
        copy.start()
    vectors = small[0, :16, :]
    lower = jnp.where(part == 0, vectors[:, :half], vectors[:, half:])
    turned = pltpu.roll(lower, lax.rem(half - d * rows, half), 1)
    outs = (ga_out, sa_out, bq_out, bv_out, bo_out, gm_out, sm_out, bdown_out)
    for index, out in enumerate(outs):
        out[...] = turned[index : index + 1, :rows]
    per_row = half // (4 * rows)
    shifted = pltpu.roll(lower, lax.rem(half - lax.rem(d, per_row) * 4 * rows, half), 1)
    for j in range(4):

        @pl.when(lax.div(d, per_row) == j)
        def _():
            bup_out[...] = shifted[8 + j : 9 + j, : 4 * rows]

    times_count = time_out.shape[1]
    spread = -(-times_count // 128) * 128
    place = lax.broadcasted_iota(jnp.int32, (stamp.shape[0], spread), 1).astype(F32)
    hot = (place == stamp[:, width : width + 1]).astype(F32).astype(BF)
    letters = token_out.shape[0]
    split = token.shape[1]
    for q in range(4):

        @pl.when(s == q)
        def _():
            at = slice(q * quarter, (q + 1) * quarter)
            token_out[: split - 16, :] = token[0, 16:, at]
            token_out[split - 16 :, :] = token[1, : letters + 16 - split, at]
            sums = jnp.zeros((quarter, spread), F32)
            for piece in three_parts(stamp[:, at]):
                sums = sums + mul_tn(piece, hot)
            time_out[...] = sums[:, :times_count]

    for copy in copies:
        copy.wait()


def run_finish(act, grads, small, token, stamp, letters_count, times_count):
    rows, width = grads.shape[1:]
    quarter = width // 4
    local = pl.BlockSpec(memory_space=pltpu.VMEM)
    anywhere = pl.BlockSpec(memory_space=pl.ANY)
    single = (1, rows)
    shapes = [
        (act.shape, anywhere),
        ((letters_count, quarter), local),
        ((quarter, times_count), local),
        (single, local),
        (single, local),
        ((1, rows, 3 * width), anywhere),
        (single, local),
        (single, local),
        ((1, rows, width), anywhere),
        (single, local),
        (single, local),
        (single, local),
        ((1, rows, 4 * width), anywhere),
        ((1, 4 * rows), local),
        ((1, 4 * rows, width), anywhere),
        (single, local),
    ]
    outs = pl.pallas_call(
        finish_kernel,
        out_shape=tuple(jax.ShapeDtypeStruct(shape, F32) for shape, _ in shapes),
        in_specs=[anywhere] * 2 + [local] * 3,
        out_specs=tuple(spec for _, spec in shapes),
        scratch_shapes=[pltpu.SemaphoreType.DMA((17,))],
        compiler_params=pltpu.CompilerParams(vmem_limit_bytes=32 * 2**20),
    )(act, grads, small, token, stamp)
    return (jnp.swapaxes(outs[0], 1, 2), outs[1], jnp.swapaxes(outs[2], 0, 1)) + tuple(outs[3:])


def plain_reduce(fixed, moving, lower):
    def grad(left, right):
        return jnp.einsum("tk,tn->kn", left, right, preferred_element_type=F32)

    width = fixed.shape[2]
    half = width // 2
    hf, h, o, gz = (fixed[index] for index in range(4))
    ups = jnp.stack([grad(hf, moving[j]) for j in range(4)])
    up = ups.reshape(4, width, 2, half).transpose(1, 2, 0, 3).reshape(width, 4 * width)
    joint = jnp.concatenate([grad(h, moving[4 + j]) for j in range(3)], axis=1)
    proj = grad(o, moving[7])
    downs = jnp.stack([grad(moving[8 + j], gz) for j in range(4)])
    down = downs.reshape(4, 2, half, width).transpose(1, 0, 2, 3).reshape(4 * width, width)
    results = []
    for total in (joint, proj, up, down):
        halves = total.reshape((2, total.shape[0] // 2) + total.shape[1:])
        summed = lax.psum_scatter(halves, "dp", scatter_dimension=1, tiled=True)
        ours = jnp.where(lower, summed[0], summed[1])
        theirs = jnp.where(lower, summed[1], summed[0]).astype(BF)
        pairs = [(i, i ^ 1) for i in range(lax.axis_size("section"))]
        results.append((ours + lax.ppermute(theirs, "section", pairs).astype(F32))[None])
    return results


def per_device(
    token_ids,
    timesteps,
    token_table,
    time_table,
    attn_gain,
    attn_shift,
    qkv_weight,
    query_bias,
    value_bias,
    proj_weight,
    proj_bias,
    mlp_gain,
    mlp_shift,
    up_weight,
    up_bias,
    down_weight,
    down_bias,
    cotangent,
):
    section = lax.axis_index("section")
    replica = lax.axis_index("dp")
    replicas = lax.axis_size("dp")
    rows, length = token_ids.shape
    width = cotangent.shape[2]
    half = width // 2
    layer = section // 2
    part = section % 2
    letters_count = token_table.shape[0]
    times_count = time_table.shape[0]
    padded = -(-letters_count // 16) * 16
    singles = (
        attn_gain,
        attn_shift,
        query_bias,
        value_bias,
        proj_bias,
        mlp_gain,
        mlp_shift,
        down_bias,
        up_bias,
    )
    marks = jnp.broadcast_to(timesteps.astype(F32)[:, None], (rows, 128))
    times = time_table.at[timesteps].get(mode="promise_in_bounds").astype(F32)
    times = jnp.concatenate([times, marks], axis=1)
    cut = half // 8
    weights = (
        qkv_weight.reshape(4, 2, cut, 3 * width),
        proj_weight.reshape(4, 2, cut, width),
        up_weight.reshape(4, 2, cut, 4 * width),
        down_weight.reshape(4, 4, 2, cut, width),
    )
    vectors = 16
    fused = replicas == 8
    layers = run_layers(weights, singles, token_ids, token_table, times, cotangent, replicas, fused)
    if fused:
        return run_finish(*layers, letters_count, times_count)
    act, sums, fixed, moving = layers
    qkv_grad, proj_grad, up_grad, down_grad = plain_reduce(fixed, moving, part == 0)
    activations = act.reshape(rows, length, width // 4).astype(F32)
    mine = jnp.zeros((2, vectors, width + 128), F32)
    mine = lax.dynamic_update_slice_in_dim(mine, sums[None, :vectors], layer, 0)
    placed = jnp.zeros((rows * replicas, width + 128), F32)
    placed = lax.dynamic_update_slice_in_dim(placed, sums[vectors + padded :], replica * rows, 0)
    joined = jnp.concatenate(
        [sums[vectors : vectors + padded], mine.reshape(2 * vectors, width + 128), placed], axis=0
    )
    joined = lax.psum(joined, ("section", "dp"))
    quarter = width // 4
    columns = lax.dynamic_slice_in_dim(joined, section * quarter, quarter, axis=1)
    token_grad = columns[:letters_count]
    first = padded + 2 * vectors
    steps = jnp.arange(times_count, dtype=jnp.int32).astype(F32)
    hot = (steps[:, None] == joined[first:, width][None, :]).astype(F32)
    time_grad = jnp.einsum("tb,bd->td", hot, columns[first:], precision=HIGHEST)
    ours = lax.dynamic_slice(joined, (padded + vectors * layer, part * half), (vectors, half))
    each = half // replicas
    flat = lax.dynamic_slice_in_dim(ours[:8], replica * each, each, axis=1)
    ups = lax.dynamic_slice_in_dim(ours[8:12].reshape(1, 4 * half), replica * 4 * each, 4 * each, axis=1)
    return (
        activations,
        token_grad,
        time_grad,
        flat[0:1],
        flat[1:2],
        qkv_grad,
        flat[2:3],
        flat[3:4],
        proj_grad,
        flat[4:5],
        flat[5:6],
        flat[6:7],
        up_grad,
        ups,
        down_grad,
        flat[7:8],
    )


def solution(mesh):
    return jax.shard_map(
        per_device,
        mesh=mesh,
        in_specs=(
            P("dp", None),
            P("dp"),
            P(),
            P(),
            P("section", None),
            P("section", None),
            P("section", None, None),
            P("section", None),
            P("section", None),
            P("section", None, None),
            P("section", None),
            P("section", None),
            P("section", None),
            P("section", None, None),
            P("section", None),
            P("section", None, None),
            P("section", None),
            P("dp", None, None),
        ),
        out_specs=(
            P("dp", None, "section"),
            P(None, "section"),
            P(None, "section"),
            P("section", "dp"),
            P("section", "dp"),
            P("section", "dp", None),
            P("section", "dp"),
            P("section", "dp"),
            P("section", "dp", None),
            P("section", "dp"),
            P("section", "dp"),
            P("section", "dp"),
            P("section", "dp", None),
            P("section", "dp"),
            P("section", "dp", None),
            P("section", "dp"),
        ),
        check_vma=False,
    )
```

```python
import functools
import math

import jax
import jax.numpy as jnp
from jax import lax
from jax.experimental import pallas as pl
from jax.experimental.pallas import tpu as pltpu
from jax.sharding import PartitionSpec as P

HEADS = 12
EPS = 1e-05
HIGHEST = lax.Precision.HIGHEST
MESH = pl.DeviceIdType.MESH
BF = jnp.bfloat16
F32 = jnp.float32
TILES = 12
QKV, PROJ, UP, DOWN = 0, 3, 4, 8
CHUNKS = 2 * TILES
LINE_FIRST = (1, 4, 7, 11)
CORE_LAG, X_LAG, Z_LAG, LINE_START, LINE_LAST = 2, 6, 2, 3, 28
GELU_A = math.sqrt(2.0 / math.pi)
GELU_B = 0.044715


def flipped(value, bit):
    mask = 2**bit
    return value + mask - 2 * mask * lax.rem(lax.div(value, mask), 2)


def mul(a, b):
    return lax.dot_general(a, b, (((1,), (0,)), ((), ())), preferred_element_type=F32)


def mul_nt(a, b):
    return lax.dot_general(a, b, (((1,), (1,)), ((), ())), preferred_element_type=F32)


def mul_tn(a, b):
    return lax.dot_general(a, b, (((0,), (0,)), ((), ())), preferred_element_type=F32)


def normalize(x):
    mean = jnp.mean(x, axis=-1, keepdims=True)
    centered = x - mean
    spread = jnp.mean(centered * centered, axis=-1, keepdims=True)
    rate = lax.rsqrt(spread + EPS)
    return centered * rate, rate


def scaled_back(gh, gain, n, rate):
    gn = gh * gain
    inner = jnp.mean(gn * n, axis=-1, keepdims=True)
    return (gn - jnp.mean(gn, axis=-1, keepdims=True) - n * inner) * rate


def column(values):
    return jnp.sum(values, axis=0, keepdims=True)


class Refs:
    def __init__(self, names, refs):
        for name, ref in zip(names, refs, strict=True):
            setattr(self, name, ref)


INPUTS = (
    "qkv_in proj_in up_in down_in ga_in sa_in bq_in bv_in bo_in gm_in sm_in bdown_in bup_in "
    "ids_in table_in time_in cot_in"
).split()


def layer_kernel(seqs, length, width, fused, names, *all_refs):
    refs = Refs(names, all_refs)
    w, par, qkv, probs = refs.w, refs.par, refs.qkv, refs.probs
    xs, acc, ybuf, ysend, y1 = refs.xs, refs.acc, refs.ybuf, refs.ysend, refs.y1
    slope, gate, h_s, o_s, hf_s, go_s = refs.slope, refs.gate, refs.h_s, refs.o_s, refs.hf_s, refs.go_s
    act, landed, gsum = refs.act, refs.landed, refs.gsum
    s = lax.axis_index("section")
    d = lax.axis_index("dp")
    stage = lax.div(s, 2)
    part = lax.rem(s, 2)
    other = 1 - part
    core = lax.rem(d, 2)
    z = lax.div(d, 2)
    x_dev = (flipped(s, 0), d)
    y_dev = (flipped(s, 1), d)
    far_dev = (flipped(flipped(s, 0), 1), d)
    z_dev = (s, flipped(d, 1))
    c_dev = (s, flipped(d, 0))
    half = width // 2
    wide = width // 4
    hidden_half = 4 * half
    rows = w.shape[4]
    mine = lax.rem(d, 4)
    across = flipped(mine, 1)
    scale = 1.0 / math.sqrt(width // HEADS)
    letters_count = refs.table_in.shape[0]
    padded = refs.table.shape[0]
    vectors = 16
    count = vectors + padded
    nz = lax.axis_size("dp") // 2
    zbits = nz.bit_length() - 1
    ends = nz - 1

    def send(src, dst, send_sem, recv_sem, device):
        return pltpu.make_async_remote_copy(
            src_ref=src,
            dst_ref=dst,
            send_sem=send_sem,
            recv_sem=recv_sem,
            device_id=device,
            device_id_type=MESH,
        )

    def start(copies):
        for copy in copies:
            copy.start()

    def wait(copies):
        for copy in copies:
            copy.wait()

    def signal(sem, device):
        pl.semaphore_signal(sem, inc=1, device_id=device, device_id_type=MESH)

    barrier = pltpu.get_barrier_semaphore()
    greeted = [x_dev, y_dev, far_dev, c_dev, z_dev]
    if fused:
        greeted += [(s, flipped(d, 1 + bit)) for bit in range(1, zbits)]
    for device in greeted:
        signal(barrier, device)
    expected = len(greeted)
    if fused:
        middle_left = jnp.logical_and(z > 0, lax.rem(z, 2) == 0)
        middle_right = jnp.logical_and(z < ends, lax.rem(z, 2) == 1)

        @pl.when(middle_left)
        def _():
            signal(barrier, (s, d - 2))

        @pl.when(middle_right)
        def _():
            signal(barrier, (s, d + 2))

        expected = expected + middle_left.astype(jnp.int32) + middle_right.astype(jnp.int32)

    def tile(index):
        return w[index].reshape(width, width)

    def own_copies(index):
        if index < PROJ:
            pairs = [(refs.qkv_in.at[:, :, :, pl.ds(index * width, width)], w.at[index, part])]
        elif index < UP:
            pairs = [(refs.proj_in, w.at[index, part])]
        elif index < DOWN:
            pairs = [
                (
                    refs.up_in.at[:, :, :, pl.ds(side * hidden_half + (index - UP) * half, half)],
                    w.at[index, part, :, :, :, pl.ds(side * half, half)],
                )
                for side in range(2)
            ]
        else:
            pairs = [(refs.down_in.at[index - DOWN], w.at[index, part])]
        return [
            pltpu.make_async_copy(src, dst, refs.own_sem.at[2 * index + k])
            for k, (src, dst) in enumerate(pairs)
        ]

    def x_weight(index):
        place = w.at[index, part, mine]
        return send(place, place, refs.wx_send.at[index], refs.wx_recv.at[index], x_dev)

    def relay(index, which, send_sem, recv_sem, device):
        place = w.at[index, other, which]
        return send(place, place, send_sem.at[index], recv_sem.at[index], device)

    def z_weight(index):
        return relay(index, mine, refs.wz_send, refs.wz_recv, z_dev)

    def c1_weight(index):
        return relay(index, mine, refs.c1_send, refs.c1_recv, c_dev)

    def c2_weight(index):
        return relay(index, across, refs.c2_send, refs.c2_recv, c_dev)

    def pass_first(index):
        relay(index, mine, refs.wx_send, refs.wx_recv, x_dev).wait_recv()
        z_weight(index).start()
        c1_weight(index).start()

    def pass_second(index):
        relay(index, across, refs.wz_send, refs.wz_recv, z_dev).wait_recv()
        c2_weight(index).start()

    def ready(index):
        relay(index, flipped(mine, 0), refs.c1_send, refs.c1_recv, c_dev).wait_recv()
        relay(index, flipped(across, 0), refs.c2_send, refs.c2_recv, c_dev).wait_recv()

    def settle_weights():
        def settle(index, _):
            x_weight(index).wait_send()
            z_weight(index).wait_send()
            c1_weight(index).wait_send()
            c2_weight(index).wait_send()
            return 0

        lax.fori_loop(0, TILES, settle, 0)

    def vec_copy(which):
        place = refs.vecs.at[which]
        return send(place, place, refs.vec_sem.at[0], refs.vec_sem.at[1], x_dev)

    for index in range(TILES):
        start(own_copies(index))
    singles = ("ga", "sa", "bq", "bv", "bo", "gm", "sm", "bdown")
    for index, name in enumerate(singles):
        refs.vecs[part, index : index + 1, :] = getattr(refs, name + "_in")[...].astype(F32)
    for j in range(4):
        refs.vecs[part, 8 + j : 9 + j, :] = refs.bup_in[:, j * half : (j + 1) * half].astype(F32)
    refs.vecs[part, 12:16, :] = jnp.zeros((4, half), F32)
    refs.table[...] = jnp.zeros_like(refs.table)
    refs.table[:letters_count, :] = refs.table_in[...]
    gsum[...] = jnp.zeros_like(gsum)
    pl.semaphore_wait(barrier, expected)
    for index in range(TILES):
        wait(own_copies(index))
        x_weight(index).start()
        if index == 3:
            vec_copy(part).start()

    pass_first(0)
    pass_first(1)
    pass_second(0)
    pass_first(2)
    pass_second(1)
    pass_first(3)
    pass_second(2)
    pass_first(4)
    pass_second(3)
    pass_first(5)

    @pl.when(stage == 1)
    def _():
        def step(index, _):
            pass_second(index - 2)
            pass_first(index)
            return 0

        lax.fori_loop(6, TILES, step, 0)
        pass_second(TILES - 2)
        pass_second(TILES - 1)

    vec_copy(other).wait_recv()
    par[:, :half] = refs.vecs[0]
    par[:, half:] = refs.vecs[1]
    for index in range(UP):
        ready(index)

    def act_copies(i):
        slot = lax.rem(i, 2)
        return [
            send(
                act.at[slot, device[0]],
                landed.at[part, i],
                refs.act_send.at[i, index],
                refs.act_recv.at[part, i],
                device,
            )
            for index, device in enumerate((y_dev, x_dev, far_dev))
        ]

    def act_own(i):
        return pltpu.make_async_copy(act.at[lax.rem(i, 2), s], landed.at[part, i], refs.act_send.at[i, 3])

    def act_arrival(side, i):
        return send(act.at[0, 0], landed.at[side, i], refs.act_send.at[i, 0], refs.act_recv.at[side, i], y_dev)

    def act_settle(i):
        for copy in act_copies(i):
            copy.wait_send()

    def cot_copy(i):
        return pltpu.make_async_copy(refs.cot_in.at[part * seqs + i], ybuf.at[i], refs.cot_sem.at[i])

    def y_copy(i):
        return send(ysend.at[i], ybuf.at[i], refs.y_send.at[i], refs.y_recv.at[i], y_dev)

    def row(index):
        return par[index : index + 1, :]

    def add_row(index, values):
        gsum[index : index + 1, :width] += column(values)

    lane = lax.broadcasted_iota(jnp.int32, (length, 128), 1)
    low = lane < 64
    side_ones = [(lane < 64).astype(F32).astype(BF), (lane >= 64).astype(F32).astype(BF)]
    side_scaled = [
        ((lane < 64).astype(F32) * scale).astype(BF),
        ((lane >= 64).astype(F32) * scale).astype(BF),
    ]
    pairs = HEADS // 2

    def letters(i):
        ids = refs.ids_in[pl.ds(part * seqs + i, 1), :]
        place = lax.broadcasted_iota(jnp.int32, (padded, length), 0)
        return (place == ids).astype(F32).astype(BF)

    def attn_fwd(i):
        @pl.when(stage == 0)
        def _():
            xs[...] = mul_tn(letters(i), refs.table[...]) + refs.time_in[pl.ds(part * seqs + i, 1), :width]

        @pl.when(stage == 1)
        def _():
            y_copy(i).wait_recv()
            xs[...] = ybuf[i].astype(F32)
            cot_copy(i).start()

        n, rate = normalize(xs[...])
        refs.n_a[i] = n.astype(BF)
        refs.r_a[i] = jnp.broadcast_to(rate, (length, 128))
        h_s[i] = (n * row(0) + row(1)).astype(BF)
        for j in range(3):
            joint = mul(h_s[i], tile(QKV + j))
            if j == 0:
                joint = joint + row(2)
            if j == 2:
                joint = joint + row(3)
            qkv[i, :, j * width : (j + 1) * width] = joint.astype(BF)

        for hp in range(pairs):
            at = hp * 128
            q2 = qkv[i, :, at : at + 128]
            k2 = qkv[i, :, width + at : width + at + 128]
            for side in range(2):
                scores = mul_nt(q2 * side_scaled[side], k2)
                expo = jnp.exp(scores - jnp.max(scores, axis=-1, keepdims=True))
                total = jnp.sum(expo, axis=-1, keepdims=True)
                probs[i, 2 * hp + side] = (expo * (1.0 / total)).astype(BF)
        for hp in range(pairs):
            at = hp * 128
            v2 = qkv[i, :, 2 * width + at : 2 * width + at + 128]
            outs = [mul(probs[i, 2 * hp + side], v2) for side in range(2)]
            o_s[i, :, at : at + 128] = jnp.where(low, outs[0], outs[1]).astype(BF)
        y1[i] = (xs[...] + (mul(o_s[i], tile(PROJ)) + row(4))).astype(BF)

    def feed_fwd(i):
        def arrived(first, last):
            @pl.when(i == 0)
            def _():
                def one(index, _):
                    ready(index)
                    return 0

                lax.fori_loop(first, last, one, 0)

        arrived(UP, DOWN)
        x = y1[i].astype(F32)
        n, rate = normalize(x)
        refs.n_f[i] = n.astype(BF)
        refs.r_f[i] = jnp.broadcast_to(rate, (length, 128))
        hf_s[i] = (n * row(5) + row(6)).astype(BF)
        acc[...] = x + row(7)
        for j in range(4):
            u = mul(hf_s[i], tile(UP + j)) + row(8 + j)
            square = u * u
            t = jnp.tanh(u * (GELU_A + GELU_A * GELU_B * square))
            both = 0.5 + 0.5 * t
            gate[i, j] = (u * both).astype(BF)
            bend = (0.5 * GELU_A + 1.5 * GELU_A * GELU_B * square) * u
            slope[i, j] = (both + bend * (1.0 - t * t)).astype(BF)
        arrived(DOWN, TILES)
        down = mul(gate[i, 0], tile(DOWN))
        for j in range(1, 4):
            down = down + mul(gate[i, j], tile(DOWN + j))
        acc[...] += down

        @pl.when(stage == 0)
        def _():
            ysend[i] = acc[...].astype(BF)
            y_copy(i).start()

        @pl.when(stage == 1)
        def _():
            @pl.when(i >= 2)
            def _():
                act_settle(i - 2)
                act_own(i - 2).wait()

            for q in range(4):
                act[lax.rem(i, 2), q] = acc[:, q * wide : (q + 1) * wide].astype(BF)
            start(act_copies(i))
            act_own(i).start()

    def feed_bwd(i):
        @pl.when(stage == 0)
        def _():
            y_copy(i).wait_recv()

        @pl.when(stage == 1)
        def _():
            cot_copy(i).wait()

        add_row(7, ybuf[i].astype(F32))
        for j in range(4):
            ga = mul_nt(ybuf[i], tile(DOWN + j))
            gu = (ga * slope[i, j].astype(F32)).astype(BF)
            slope[i, j] = gu
            add_row(8 + j, gu.astype(F32))
        gh = mul_nt(slope[i, 0], tile(UP))
        for j in range(1, 4):
            gh = gh + mul_nt(slope[i, j], tile(UP + j))
        n = refs.n_f[i].astype(F32)
        add_row(5, gh * n)
        add_row(6, gh)
        gx = ybuf[i].astype(F32) + scaled_back(gh, row(5), n, refs.r_f[i][:, 0:1])
        y1[i] = gx.astype(BF)

    def attn_bwd(i):
        add_row(4, y1[i].astype(F32))
        go_s[...] = mul_nt(y1[i], tile(PROJ)).astype(BF)
        for hp in range(pairs):
            at = hp * 128
            v2 = qkv[i, :, 2 * width + at : 2 * width + at + 128]
            go2 = go_s[:, at : at + 128]
            gv = []
            for side in range(2):
                pb = probs[i, 2 * hp + side]
                gp = mul_nt(go2 * side_ones[side], v2)
                p = pb.astype(F32)
                pg = p * gp
                gs = (pg - p * jnp.sum(pg, axis=-1, keepdims=True)).astype(BF)
                gv.append(mul_tn(pb, go2))
                probs[i, 2 * hp + side] = gs
            qkv[i, :, 2 * width + at : 2 * width + at + 128] = jnp.where(low, gv[0], gv[1]).astype(BF)
        for hp in range(pairs):
            at = hp * 128
            q2 = qkv[i, :, at : at + 128]
            k2 = qkv[i, :, width + at : width + at + 128]
            gq, gk = [], []
            for side in range(2):
                gs = probs[i, 2 * hp + side]
                gq.append(mul(gs, k2))
                gk.append(mul_tn(gs, q2))
            qkv[i, :, at : at + 128] = (jnp.where(low, gq[0], gq[1]) * scale).astype(BF)
            qkv[i, :, width + at : width + at + 128] = (jnp.where(low, gk[0], gk[1]) * scale).astype(BF)
        pieces = [qkv[i, :, j * width : (j + 1) * width] for j in range(3)]
        add_row(2, pieces[0].astype(F32))
        add_row(3, pieces[2].astype(F32))
        gh = mul_nt(pieces[0], tile(QKV)) + mul_nt(pieces[1], tile(QKV + 1)) + mul_nt(pieces[2], tile(QKV + 2))
        n = refs.n_a[i].astype(F32)
        add_row(0, gh * n)
        add_row(1, gh)
        acc[...] = y1[i].astype(F32) + scaled_back(gh, row(0), n, refs.r_a[i][:, 0:1])

        @pl.when(stage == 1)
        def _():
            ysend[i] = acc[...].astype(BF)
            y_copy(i).start()

        @pl.when(stage == 0)
        def _():
            high = acc[...].astype(BF)
            rest = (acc[...] - high.astype(F32)).astype(BF)
            hot = letters(i)
            gsum[vectors:count, :width] += mul(hot, high) + mul(hot, rest)
            mark = part * seqs + i
            stamp = refs.time_in[pl.ds(mark, 1), :]
            gsum[pl.ds(count + mark, 1), :] = jnp.concatenate([column(acc[...]), stamp[:, width:]], axis=1)

    units = (attn_fwd, feed_fwd, feed_bwd, attn_bwd)
    steps = 0
    if fused:
        step = reduce_steps(refs, seqs, length, width, send, signal, act_arrival, act_own, settle_weights)
        units = units + (step,)
        steps = CHUNKS + X_LAG + Z_LAG * ends

    def unit(u, _):
        early = u < 2 * seqs
        kind0 = jnp.where(early, lax.div(u, seqs), 2 + lax.rem(u, 2))
        index0 = jnp.where(early, lax.rem(u, seqs), lax.div(u, 2) - seqs)
        kind1 = lax.rem(u, 4)
        index1 = lax.div(u, 4)
        if fused:
            last = 4 * seqs - 1
            ahead = 4
            kind0 = jnp.where(u >= last, 4, kind0)
            index0 = jnp.where(u >= last, jnp.where(u < last + ahead, u - last, u - last - 1), index0)
            kind0 = jnp.where(u == last + ahead, 3, kind0)
            index0 = jnp.where(u == last + ahead, seqs - 1, index0)
            kind1 = jnp.where(u > last, 4, kind1)
            index1 = jnp.where(u > last, u - last - 1, index1)
        kind = jnp.where(stage == 0, kind0, kind1)
        i = jnp.where(stage == 0, index0, index1)

        @pl.when(jnp.logical_and(stage == 0, jnp.logical_and(u >= 1, u <= 4)))
        def _():
            pass_second(2 + 2 * u)
            pass_second(3 + 2 * u)

        @pl.when(jnp.logical_and(stage == 0, jnp.logical_and(u >= 1, u <= 3)))
        def _():
            pass_first(4 + 2 * u)
            pass_first(5 + 2 * u)

        for index, run in enumerate(units):

            @pl.when(kind == index)
            def _():
                run(i)

        return 0

    lax.fori_loop(0, 4 * seqs + steps, unit, 0)

    vec_copy(part).wait_send()
    if not fused:
        settle_weights()

    def finish(i, _):
        y_copy(i).wait_send()

        @pl.when(jnp.logical_and(stage == 1, i >= 2))
        def _():
            act_settle(i)

        return 0

    lax.fori_loop(0, seqs, finish, 0)
    if not fused:

        @pl.when(stage == 1)
        def _():
            for i in range(2, seqs):
                act_own(i).wait()

        for i in range(seqs):
            for side in range(2):

                @pl.when(jnp.logical_or(stage == 0, part != side))
                def _():
                    act_arrival(side, i).wait_recv()

        refs.sums_out[...] = gsum[...]
        copies = []
        for i in range(seqs):
            place = pl.ds(i * length, length)
            for index, ref in enumerate((hf_s, h_s, o_s, ybuf)):
                copies.append((ref.at[i], refs.fixed_out.at[index, place]))
            for j in range(4):
                copies.append((slope.at[i, j], refs.moving_out.at[j, place]))
                copies.append((gate.at[i, j], refs.moving_out.at[8 + j, place]))
            for j in range(3):
                copies.append((qkv.at[i, :, pl.ds(j * width, width)], refs.moving_out.at[4 + j, place]))
            copies.append((y1.at[i], refs.moving_out.at[7, place]))
        copies.append((landed, refs.act_out))
        copies = [
            pltpu.make_async_copy(src, dst, refs.keep_sem.at[index]) for index, (src, dst) in enumerate(copies)
        ]
        start(copies)
        wait(copies)


def reduce_steps(refs, seqs, length, width, send, signal, act_arrival, act_own, settle_weights):
    s = lax.axis_index("section")
    d = lax.axis_index("dp")
    stage = lax.div(s, 2)
    part = lax.rem(s, 2)
    other = 1 - part
    core = lax.rem(d, 2)
    z = lax.div(d, 2)
    x_dev = (flipped(s, 0), d)
    y_dev = (flipped(s, 1), d)
    c_dev = (s, flipped(d, 0))
    right_dev = (s, d + 2)
    left_dev = (s, d - 2)
    w, gsum = refs.w, refs.gsum
    nz = w.shape[2]
    rows = w.shape[4]
    ends = nz - 1
    slots = refs.x_buf.shape[0]
    core_slots = refs.core_buf.shape[0]
    directs = CHUNKS - len(LINE_FIRST)
    half = width // 2
    tokens = seqs * length
    core_buf, x_buf, right_buf, left_buf = refs.core_buf, refs.x_buf, refs.right_buf, refs.left_buf
    vectors = 16
    count = vectors + refs.table.shape[0]
    split = count // 2
    zbits = nz.bit_length() - 1
    own = gsum.shape[0] - count

    def where(tile):
        return jnp.where(tile < 4, tile + 4, jnp.where(tile < 8, tile - 4, tile))

    def at(k, *index):
        columns = pl.ds(pl.multiple_of(lax.rem(k, 2) * half, 128), half)
        return (where(lax.div(k, 2)),) + index + (slice(None), columns)

    everything = slice(None)

    def turned(k):
        return functools.reduce(jnp.logical_or, [k == chunk for chunk in LINE_FIRST])

    def direct(k):
        return jnp.logical_and(jnp.logical_and(k >= 0, k < CHUNKS), jnp.logical_not(turned(k)))

    def order(k):
        return k - sum((k > chunk).astype(jnp.int32) for chunk in LINE_FIRST)

    def slot(k):
        return lax.rem(order(k), slots)

    def core_slot(k):
        return lax.rem(k, core_slots)

    def core_copy(k):
        return send(
            w.at[at(k, everything, everything, 1 - core)],
            core_buf.at[core_slot(k)],
            refs.core_send.at[core_slot(k)],
            refs.core_recv.at[core_slot(k)],
            c_dev,
        )

    def x_copy(k):
        return send(
            w.at[at(k, other, everything, core)],
            x_buf.at[slot(k)],
            refs.x_send.at[slot(k)],
            refs.x_recv.at[slot(k)],
            x_dev,
        )

    class Line:
        def __init__(self, name, slot, side, spend_from, grant_to):
            self.right_buf = getattr(refs, name + "right_buf")
            self.left_buf = getattr(refs, name + "left_buf")
            self.right_sems = getattr(refs, name + "right_send"), getattr(refs, name + "right_recv")
            self.left_sems = getattr(refs, name + "left_send"), getattr(refs, name + "left_recv")
            self.right_credit = getattr(refs, name + "right_credit")
            self.left_credit = getattr(refs, name + "left_credit")
            self.slots = self.right_buf.shape[0]
            self.slot = lambda job: lax.rem(slot(job), self.slots)
            self.side = side
            self.spend_from = spend_from
            self.grant_to = grant_to

        def place(self, job, j):
            k, side = self.side(job)
            return at(k, side, j, core)

        def right_copy(self, job, j):
            sends, recvs = self.right_sems
            slot = self.slot(job)
            target = self.right_buf.at[slot, j]
            return send(w.at[self.place(job, j)], target, sends.at[slot, j], recvs.at[slot, j], right_dev)

        def left_copy(self, job, j):
            sends, recvs = self.left_sems
            slot = self.slot(job)
            target = self.left_buf.at[slot, j]
            return send(w.at[self.place(job, j)], target, sends.at[slot, j], recvs.at[slot, j], left_dev)

        def add(self, job, j, buffer):
            both = w[self.place(job, j)].astype(F32) + buffer[self.slot(job), j].astype(F32)
            w[self.place(job, j)] = both.astype(BF)

        def right_step(self, job):
            @pl.when(jnp.logical_and(z < ends, self.spend_from(job)))
            def _():
                pl.semaphore_wait(self.right_credit, 1)

            for j in range(ends, -1, -1):

                @pl.when(jnp.logical_and(z > 0, j >= z))
                def _():
                    self.right_copy(job, j).wait_recv()
                    self.add(job, j, self.right_buf)

                @pl.when(jnp.logical_and(j > z, self.spend_from(job)))
                def _():
                    self.right_copy(job, j).wait_send()

                @pl.when(j > z)
                def _():
                    self.right_copy(job, j).start()

            @pl.when(jnp.logical_and(z > 0, self.grant_to(job)))
            def _():
                signal(self.right_credit, left_dev)

        def left_step(self, job):
            @pl.when(jnp.logical_and(z > 0, self.spend_from(job)))
            def _():
                pl.semaphore_wait(self.left_credit, 1)

            for j in range(nz):

                @pl.when(jnp.logical_and(z < ends, j <= z))
                def _():
                    self.left_copy(job, j).wait_recv()
                    self.add(job, j, self.left_buf)

                @pl.when(jnp.logical_and(j < z, self.spend_from(job)))
                def _():
                    self.left_copy(job, j).wait_send()

                @pl.when(j < z)
                def _():
                    self.left_copy(job, j).start()

            @pl.when(jnp.logical_and(z < ends, self.grant_to(job)))
            def _():
                signal(self.left_credit, right_dev)

        def settle(self, job):
            for j in range(nz):

                @pl.when(j > z)
                def _():
                    self.right_copy(job, j).wait_send()

                @pl.when(j < z)
                def _():
                    self.left_copy(job, j).wait_send()

    line_slots = refs.right_buf.shape[0]
    main = Line(
        "",
        order,
        lambda k: (k, part),
        lambda k: order(k) >= line_slots,
        lambda k: order(k) + line_slots < directs,
    )
    side_jobs = 2 * len(LINE_FIRST)
    side_slots = refs.b_right_buf.shape[0]

    def side_place(job):
        chunk = jnp.int32(LINE_FIRST[-1])
        for index in range(len(LINE_FIRST) - 1, -1, -1):
            chunk = jnp.where(job < 2 * (index + 1), LINE_FIRST[index], chunk)
        return chunk, lax.rem(job, 2)

    beside = Line(
        "b_",
        lambda job: job,
        side_place,
        lambda job: job >= side_slots,
        lambda job: job + side_slots < side_jobs,
    )

    def grads_copy(k):
        return pltpu.make_async_copy(refs.grad_stage, refs.grads_out.at[k], refs.out_sem.at[0])

    def act_copy(turn):
        return pltpu.make_async_copy(refs.act_stage, refs.act_out.at[turn], refs.out_sem.at[1])

    def put_grads(k, value):
        @pl.when(k > 0)
        def _():
            grads_copy(k).wait()

        refs.grad_stage[...] = value
        grads_copy(k).start()

    def last_copy(index):
        k = jnp.int32(LINE_FIRST[index])
        return send(
            w.at[at(k, other, z, core)],
            refs.last_buf.at[index],
            refs.last_send.at[index],
            refs.last_recv.at[index],
            x_dev,
        )

    def put_last(index):
        k = jnp.int32(LINE_FIRST[index])
        last_copy(index).wait_recv()
        put_grads(k, w[at(k, part, z, core)].astype(F32) + refs.last_buf[index].astype(F32))

    def flat(value):
        return value.reshape(tokens, width)

    def store(k, value):
        w[where(k)] = value.astype(BF).reshape(2, nz, 2, rows, width)

    def products(tile):
        @pl.when(tile < 4)
        def _():
            store(tile, mul_tn(flat(refs.hf_s[...]), flat(refs.slope[:, tile])))

        for j in range(3):

            @pl.when(tile == 4 + j)
            def _():
                store(tile, mul_tn(flat(refs.h_s[...]), flat(refs.qkv[:, :, j * width : (j + 1) * width])))

        @pl.when(tile == 7)
        def _():
            store(tile, mul_tn(flat(refs.o_s[...]), flat(refs.y1[...])))

        @pl.when(jnp.logical_and(tile >= 4, tile < 8))
        def _():
            value = mul_tn(flat(refs.gate[:, tile - 4]), flat(refs.ybuf[...])).astype(BF)
            value = value.reshape(2, 2, 4, rows, width)
            for block in range(4):
                w[8 + block, :, tile - 4] = value[:, :, block]

    def inside(k):
        return jnp.logical_and(k >= 0, k < CHUNKS)

    def core_sums():
        return send(
            gsum.at[pl.ds(0, count)], refs.sums_buf, refs.sums_sem.at[0], refs.sums_sem.at[1], c_dev
        )

    def x_sums():
        return [
            send(refs.adds.at[0], refs.adds_buf.at[0], refs.adds_send.at[0], refs.adds_recv.at[0], x_dev),
            send(
                gsum.at[pl.ds(count, own)],
                refs.stamp_buf,
                refs.stamp_send.at[0],
                refs.stamp_recv.at[0],
                x_dev,
            ),
        ]

    def block(bit, place_core, place_z):
        size = own * 2**bit
        first = place_core * nz * own + lax.div(place_z, 2**bit) * size
        return pl.ds(pl.multiple_of(first, 8), size)

    def z_sums(bit, arriving):
        there = flipped(z, bit)
        place = refs.stamps.at[block(bit, core, there if arriving else z)]
        device = (s, flipped(d, 1 + bit))
        return [
            send(
                refs.adds.at[1 + bit],
                refs.adds_buf.at[1 + bit],
                refs.adds_send.at[1 + bit],
                refs.adds_recv.at[1 + bit],
                device,
            ),
            send(place, place, refs.stamp_send.at[1 + bit], refs.stamp_recv.at[1 + bit], device),
        ]

    def last_sums(arriving):
        side = 1 - core if arriving else core
        place = refs.stamps.at[block(zbits, side, z)]
        half_sums = refs.whole.at[side]
        return [
            send(half_sums, half_sums, refs.sums_sem.at[2], refs.sums_sem.at[3], c_dev),
            send(place, place, refs.stamp_send.at[1 + zbits], refs.stamp_recv.at[1 + zbits], c_dev),
        ]

    def final_copies():
        return [
            send(src, dst, refs.final_send.at[index], refs.final_recv.at[index], y_dev)
            for index, (src, dst) in enumerate(((refs.whole, refs.token_out), (refs.stamps, refs.stamp_out)))
        ]

    def arrive(copies):
        for copy in copies:
            copy.wait_recv()

    def begin(copies):
        for copy in copies:
            copy.start()

    def small_step(t):
        @pl.when(t == 5)
        def _():
            core_sums().start()

        @pl.when(t == 8)
        def _():
            core_sums().wait_recv()
            sums = gsum[:count, :width] + refs.sums_buf[:, :width]

            @pl.when(core == 0)
            def _():
                refs.adds[0] = sums[:split]

            @pl.when(core == 1)
            def _():
                refs.adds[0] = sums[split:]

            begin(x_sums())

        @pl.when(t == 12)
        def _():
            arrive(x_sums())
            refs.adds[1] = refs.adds[0] + refs.adds_buf[0]
            refs.stamps[block(0, core, z), :] = gsum[count:, :] + refs.stamp_buf[...]
            begin(z_sums(0, False))

        for bit in range(zbits):

            @pl.when(t == 16 + 4 * bit)
            def _():
                arrive(z_sums(bit, True))
                total = refs.adds[1 + bit] + refs.adds_buf[1 + bit]
                if bit + 1 < zbits:
                    refs.adds[2 + bit] = total
                    begin(z_sums(bit + 1, False))
                else:
                    refs.whole[core] = total
                    begin(last_sums(False))

        @pl.when(t == 16 + 4 * zbits)
        def _():
            arrive(last_sums(True))
            refs.small_out[...] = refs.whole[...]

            @pl.when(stage == 0)
            def _():
                begin(final_copies())
                refs.token_out[...] = refs.whole[...]
                refs.stamp_out[...] = refs.stamps[...]

    def act_step(t):
        turn = t - 6

        @pl.when(jnp.logical_and(turn >= 0, turn < 2 * seqs))
        def _():
            side = lax.div(turn, seqs)
            i = lax.rem(turn, seqs)
            ours = jnp.logical_and(stage == 1, side == part)

            @pl.when(jnp.logical_not(ours))
            def _():
                act_arrival(side, i).wait_recv()

            @pl.when(jnp.logical_and(ours, i >= 2))
            def _():
                act_own(i).wait()

            @pl.when(turn > 0)
            def _():
                act_copy(turn - 1).wait()

            refs.act_stage[...] = refs.landed[side, i].astype(F32).T
            act_copy(turn).start()

    def step(t):
        @pl.when(t == 0)
        def _():
            settle_weights()

        @pl.when(jnp.logical_and(lax.rem(t, 2) == 0, t < 16))
        def _():
            products(lax.div(t, 2))

        @pl.when(t < CHUNKS)
        def _():
            @pl.when(t >= core_slots)
            def _():
                pl.semaphore_wait(refs.core_credit, 1)
                core_copy(t).wait_send()

            core_copy(t).start()

        k1 = t - CORE_LAG

        @pl.when(inside(k1))
        def _():
            core_copy(k1).wait_recv()
            for side in range(2):
                place = at(k1, side, everything, core)
                both = w[place].astype(F32) + core_buf[core_slot(k1), side].astype(F32)
                w[place] = both.astype(BF)

            @pl.when(k1 + core_slots < CHUNKS)
            def _():
                signal(refs.core_credit, c_dev)

        @pl.when(direct(k1))
        def _():
            @pl.when(order(k1) >= slots)
            def _():
                pl.semaphore_wait(refs.x_credit, 1)
                x_copy(k1).wait_send()

            x_copy(k1).start()

        small_step(t)
        act_step(t)
        k2 = t - X_LAG

        @pl.when(direct(k2))
        def _():
            x_copy(k2).wait_recv()
            place = at(k2, part, everything, core)
            both = w[place].astype(F32) + x_buf[slot(k2)].astype(F32)
            w[place] = both.astype(BF)

            @pl.when(order(k2) + slots < directs)
            def _():
                signal(refs.x_credit, x_dev)

        k3 = t - X_LAG - Z_LAG * z
        k4 = t - X_LAG - Z_LAG * (ends - z)
        k5 = jnp.minimum(k3, k4)

        @pl.when(direct(k3))
        def _():
            main.right_step(k3)

        @pl.when(direct(k4))
        def _():
            main.left_step(k4)

        @pl.when(direct(k5))
        def _():
            put_grads(k5, w[main.place(k5, z)].astype(F32))

        def listed(turn):
            even = lax.rem(turn + 64, 2) == 0
            return jnp.logical_and(even, jnp.logical_and(turn >= 0, turn < 2 * side_jobs))

        j3 = t - LINE_START - Z_LAG * z
        j4 = t - LINE_START - Z_LAG * (ends - z)

        @pl.when(listed(j3))
        def _():
            beside.right_step(lax.div(j3, 2))

        @pl.when(listed(j4))
        def _():
            beside.left_step(lax.div(j4, 2))

        @pl.when(t == LINE_LAST)
        def _():
            for index in range(len(LINE_FIRST)):
                last_copy(index).start()

        @pl.when(t == CHUNKS + X_LAG + Z_LAG * ends - 1)
        def _():
            for index in range(len(LINE_FIRST)):
                put_last(index)
            finish()

    def finish():
        def settle_core(k, _):
            core_copy(k).wait_send()
            return 0

        def settle_x(k, _):
            x_copy(k).wait_send()
            return 0

        def settle_main(k, _):
            main.settle(k)
            return 0

        def settle_beside(job, _):
            beside.settle(job)
            return 0

        lax.fori_loop(CHUNKS - core_slots, CHUNKS, settle_core, 0)
        lax.fori_loop(CHUNKS - slots, CHUNKS, settle_x, 0)
        lax.fori_loop(CHUNKS - line_slots, CHUNKS, settle_main, 0)
        lax.fori_loop(side_jobs - side_slots, side_jobs, settle_beside, 0)
        for index in range(len(LINE_FIRST)):
            last_copy(index).wait_send()
        grads_copy(0).wait()
        act_copy(2 * seqs - 1).wait()
        sends = [core_sums()] + x_sums() + last_sums(False)
        for bit in range(zbits):
            sends += z_sums(bit, False)
        for copy in sends:
            copy.wait_send()

        @pl.when(stage == 0)
        def _():
            for copy in final_copies():
                copy.wait_send()

        @pl.when(stage == 1)
        def _():
            arrive(final_copies())

    return step


def run_layers(weights, singles, ids, table, times, cot, replicas, fused):
    rows, length = ids.shape
    width = cot.shape[2]
    half = width // 2
    seqs = rows // 2
    tokens = seqs * length
    padded = -(-table.shape[0] // 16) * 16
    count = 16 + padded
    nz = replicas // 2
    lane = width + 128
    cut = half // 8
    dma = pltpu.SemaphoreType.DMA
    credit = pltpu.SemaphoreType.REGULAR
    anywhere = pl.BlockSpec(memory_space=pl.ANY)
    local = pl.BlockSpec(memory_space=pltpu.VMEM)
    vm = pltpu.VMEM
    shape = jax.ShapeDtypeStruct
    if fused:
        outs = {
            "act_out": (shape((2 * seqs, width // 4, length), F32), anywhere),
            "grads_out": (shape((CHUNKS, cut, half), F32), anywhere),
            "small_out": (shape((2, count // 2, width), F32), local),
            "token_out": (shape((2, count // 2, width), F32), local),
            "stamp_out": (shape((rows * replicas, lane), F32), local),
        }
    else:
        outs = {
            "act_out": (shape((2, seqs, length, width // 4), BF), anywhere),
            "sums_out": (shape((count + rows, lane), F32), local),
            "fixed_out": (shape((4, tokens, width), BF), anywhere),
            "moving_out": (shape((12, tokens, width), BF), anywhere),
        }
    scratch = {
        "w": vm((TILES, 2, 4, 2, cut, width), BF),
        "vecs": vm((2, 16, half), F32),
        "table": vm((padded, width), BF),
        "par": vm((16, width), F32),
        "xs": vm((length, width), F32),
        "acc": vm((length, width), F32),
        "n_a": vm((seqs, length, width), BF),
        "n_f": vm((seqs, length, width), BF),
        "r_a": vm((seqs, length, 128), F32),
        "r_f": vm((seqs, length, 128), F32),
        "qkv": vm((seqs, length, 3 * width), BF),
        "probs": vm((seqs, HEADS, length, length), BF),
        "y1": vm((seqs, length, width), BF),
        "slope": vm((seqs, 4, length, width), BF),
        "gate": vm((seqs, 4, length, width), BF),
        "h_s": vm((seqs, length, width), BF),
        "o_s": vm((seqs, length, width), BF),
        "hf_s": vm((seqs, length, width), BF),
        "go_s": vm((length, width), BF),
        "ybuf": vm((seqs, length, width), BF),
        "ysend": vm((seqs, length, width), BF),
        "act": vm((2, 4, length, width // 4), BF),
        "landed": vm((2, seqs, length, width // 4), BF),
        "gsum": vm((count + rows, lane), F32),
        "own_sem": dma((2 * TILES,)),
        "vec_sem": dma((2,)),
        "cot_sem": dma((seqs,)),
        "y_send": dma((seqs,)),
        "y_recv": dma((seqs,)),
        "act_send": dma((seqs, 4)),
        "act_recv": dma((2, seqs)),
    }
    for name in ("wx", "wz", "c1", "c2"):
        scratch[name + "_send"] = dma((TILES,))
        scratch[name + "_recv"] = dma((TILES,))
    if fused:
        zbits = nz.bit_length() - 1
        scratch |= {
            "core_buf": vm((4, 2, nz, cut, half), BF),
            "x_buf": vm((X_LAG, nz, cut, half), BF),
            "right_buf": vm((4, nz, cut, half), BF),
            "left_buf": vm((4, nz, cut, half), BF),
            "b_right_buf": vm((2, nz, cut, half), BF),
            "b_left_buf": vm((2, nz, cut, half), BF),
            "last_buf": vm((len(LINE_FIRST), cut, half), BF),
            "last_send": dma((len(LINE_FIRST),)),
            "last_recv": dma((len(LINE_FIRST),)),
            "sums_buf": vm((count, lane), F32),
            "adds": vm((1 + zbits, count // 2, width), F32),
            "adds_buf": vm((1 + zbits, count // 2, width), F32),
            "whole": vm((2, count // 2, width), F32),
            "stamp_buf": vm((rows, lane), F32),
            "stamps": vm((rows * replicas, lane), F32),
            "grad_stage": vm((cut, half), F32),
            "act_stage": vm((width // 4, length), F32),
            "out_sem": dma((2,)),
            "sums_sem": dma((4,)),
            "adds_send": dma((1 + zbits,)),
            "adds_recv": dma((1 + zbits,)),
            "stamp_send": dma((2 + zbits,)),
            "stamp_recv": dma((2 + zbits,)),
            "final_send": dma((2,)),
            "final_recv": dma((2,)),
            "core_credit": credit,
            "x_credit": credit,
            "right_credit": credit,
            "left_credit": credit,
            "b_right_credit": credit,
            "b_left_credit": credit,
        }
        for name in ("core", "x"):
            slots = scratch[name + "_buf"].shape[0]
            scratch[name + "_send"] = dma((slots,))
            scratch[name + "_recv"] = dma((slots,))
        for name in ("right", "left", "b_right", "b_left"):
            slots = scratch[name + "_buf"].shape[0]
            scratch[name + "_send"] = dma((slots, nz))
            scratch[name + "_recv"] = dma((slots, nz))
    else:
        scratch["keep_sem"] = dma((16 * seqs + 1,))
    names = INPUTS + list(outs) + list(scratch)
    return pl.pallas_call(
        functools.partial(layer_kernel, seqs, length, width, fused, names),
        out_shape=tuple(out[0] for out in outs.values()),
        in_specs=[anywhere] * 4 + [local] * 12 + [anywhere],
        out_specs=tuple(out[1] for out in outs.values()),
        scratch_shapes=list(scratch.values()),
        compiler_params=pltpu.CompilerParams(
            collective_id=0, has_side_effects=True, vmem_limit_bytes=64 * 2**20 - 2**17
        ),
    )(*weights, *singles, ids, table, times, cot)


def three_parts(value):
    first = value.astype(BF)
    rest = value - first.astype(F32)
    second = rest.astype(BF)
    return first, second, (rest - second.astype(F32)).astype(BF)


def finish_kernel(
    act,
    grads,
    small,
    token,
    stamp,
    act_out,
    token_out,
    time_out,
    ga_out,
    sa_out,
    qkv_out,
    bq_out,
    bv_out,
    proj_out,
    bo_out,
    gm_out,
    sm_out,
    up_out,
    bup_out,
    down_out,
    bdown_out,
    act_s,
    grads_s,
    sem,
):
    s = lax.axis_index("section")
    d = lax.axis_index("dp")
    part = lax.rem(s, 2)
    rows, half = grads.shape[1:]
    width = 2 * half
    quarter = width // 4
    loads = [
        pltpu.make_async_copy(src, dst, sem.at[25 + index])
        for index, (src, dst) in enumerate(((act, act_s), (grads, grads_s)))
    ]
    for copy in loads:
        copy.start()
    pairs = [(act_s, act_out)]
    for side in range(2):
        for j in range(4):
            columns = pl.ds(side * 4 * half + j * half, half)
            pairs.append((grads_s.at[2 * j + side], up_out.at[0, :, columns]))
        for j in range(3):
            columns = pl.ds(j * width + side * half, half)
            pairs.append((grads_s.at[8 + 2 * j + side], qkv_out.at[0, :, columns]))
        columns = pl.ds(side * half, half)
        pairs.append((grads_s.at[14 + side], proj_out.at[0, :, columns]))
        for j in range(4):
            pairs.append((grads_s.at[16 + 2 * j + side], down_out.at[0, pl.ds(j * rows, rows), columns]))
    copies = [pltpu.make_async_copy(src, dst, sem.at[index]) for index, (src, dst) in enumerate(pairs)]
    for copy in loads:
        copy.wait()
    for copy in copies:
        copy.start()
    vectors = small[0, :16, :]
    lower = jnp.where(part == 0, vectors[:, :half], vectors[:, half:])
    turned = pltpu.roll(lower, lax.rem(half - d * rows, half), 1)
    outs = (ga_out, sa_out, bq_out, bv_out, bo_out, gm_out, sm_out, bdown_out)
    for index, out in enumerate(outs):
        out[...] = turned[index : index + 1, :rows]
    per_row = half // (4 * rows)
    shifted = pltpu.roll(lower, lax.rem(half - lax.rem(d, per_row) * 4 * rows, half), 1)
    for j in range(4):

        @pl.when(lax.div(d, per_row) == j)
        def _():
            bup_out[...] = shifted[8 + j : 9 + j, : 4 * rows]

    times_count = time_out.shape[1]
    spread = -(-times_count // 128) * 128
    place = lax.broadcasted_iota(jnp.int32, (stamp.shape[0], spread), 1).astype(F32)
    hot = (place == stamp[:, width : width + 1]).astype(F32).astype(BF)
    letters = token_out.shape[0]
    split = token.shape[1]
    for q in range(4):

        @pl.when(s == q)
        def _():
            at = slice(q * quarter, (q + 1) * quarter)
            token_out[: split - 16, :] = token[0, 16:, at]
            token_out[split - 16 :, :] = token[1, : letters + 16 - split, at]
            sums = jnp.zeros((quarter, spread), F32)
            for piece in three_parts(stamp[:, at]):
                sums = sums + mul_tn(piece, hot)
            time_out[...] = sums[:, :times_count]

    for copy in copies:
        copy.wait()


def run_finish(act, grads, small, token, stamp, letters_count, times_count):
    rows, half = grads.shape[1:]
    width = 2 * half
    quarter = width // 4
    local = pl.BlockSpec(memory_space=pltpu.VMEM)
    anywhere = pl.BlockSpec(memory_space=pl.ANY)
    single = (1, rows)
    shapes = [
        (act.shape, anywhere),
        ((letters_count, quarter), local),
        ((quarter, times_count), local),
        (single, local),
        (single, local),
        ((1, rows, 3 * width), anywhere),
        (single, local),
        (single, local),
        ((1, rows, width), anywhere),
        (single, local),
        (single, local),
        (single, local),
        ((1, rows, 4 * width), anywhere),
        ((1, 4 * rows), local),
        ((1, 4 * rows, width), anywhere),
        (single, local),
    ]
    outs = pl.pallas_call(
        finish_kernel,
        out_shape=tuple(jax.ShapeDtypeStruct(shape, F32) for shape, _ in shapes),
        in_specs=[anywhere] * 2 + [local] * 3,
        out_specs=tuple(spec for _, spec in shapes),
        scratch_shapes=[
            pltpu.VMEM(act.shape, F32),
            pltpu.VMEM(grads.shape, F32),
            pltpu.SemaphoreType.DMA((27,)),
        ],
        compiler_params=pltpu.CompilerParams(vmem_limit_bytes=62 * 2**20),
    )(act, grads, small, token, stamp)
    return (jnp.swapaxes(outs[0], 1, 2), outs[1], jnp.swapaxes(outs[2], 0, 1)) + tuple(outs[3:])


def plain_reduce(fixed, moving, lower):
    def grad(left, right):
        return jnp.einsum("tk,tn->kn", left, right, preferred_element_type=F32)

    width = fixed.shape[2]
    half = width // 2
    hf, h, o, gz = (fixed[index] for index in range(4))
    ups = jnp.stack([grad(hf, moving[j]) for j in range(4)])
    up = ups.reshape(4, width, 2, half).transpose(1, 2, 0, 3).reshape(width, 4 * width)
    joint = jnp.concatenate([grad(h, moving[4 + j]) for j in range(3)], axis=1)
    proj = grad(o, moving[7])
    downs = jnp.stack([grad(moving[8 + j], gz) for j in range(4)])
    down = downs.reshape(4, 2, half, width).transpose(1, 0, 2, 3).reshape(4 * width, width)
    results = []
    for total in (joint, proj, up, down):
        halves = total.reshape((2, total.shape[0] // 2) + total.shape[1:])
        summed = lax.psum_scatter(halves, "dp", scatter_dimension=1, tiled=True)
        ours = jnp.where(lower, summed[0], summed[1])
        theirs = jnp.where(lower, summed[1], summed[0]).astype(BF)
        pairs = [(i, i ^ 1) for i in range(lax.axis_size("section"))]
        results.append((ours + lax.ppermute(theirs, "section", pairs).astype(F32))[None])
    return results


def per_device(
    token_ids,
    timesteps,
    token_table,
    time_table,
    attn_gain,
    attn_shift,
    qkv_weight,
    query_bias,
    value_bias,
    proj_weight,
    proj_bias,
    mlp_gain,
    mlp_shift,
    up_weight,
    up_bias,
    down_weight,
    down_bias,
    cotangent,
):
    section = lax.axis_index("section")
    replica = lax.axis_index("dp")
    replicas = lax.axis_size("dp")
    rows, length = token_ids.shape
    width = cotangent.shape[2]
    half = width // 2
    layer = section // 2
    part = section % 2
    letters_count = token_table.shape[0]
    times_count = time_table.shape[0]
    padded = -(-letters_count // 16) * 16
    singles = (
        attn_gain,
        attn_shift,
        query_bias,
        value_bias,
        proj_bias,
        mlp_gain,
        mlp_shift,
        down_bias,
        up_bias,
    )
    marks = jnp.broadcast_to(timesteps.astype(F32)[:, None], (rows, 128))
    times = time_table.at[timesteps].get(mode="promise_in_bounds").astype(F32)
    times = jnp.concatenate([times, marks], axis=1)
    cut = half // 8
    weights = (
        qkv_weight.reshape(4, 2, cut, 3 * width),
        proj_weight.reshape(4, 2, cut, width),
        up_weight.reshape(4, 2, cut, 4 * width),
        down_weight.reshape(4, 4, 2, cut, width),
    )
    vectors = 16
    fused = replicas == 8
    layers = run_layers(weights, singles, token_ids, token_table, times, cotangent, replicas, fused)
    if fused:
        return run_finish(*layers, letters_count, times_count)
    act, sums, fixed, moving = layers
    qkv_grad, proj_grad, up_grad, down_grad = plain_reduce(fixed, moving, part == 0)
    activations = act.reshape(rows, length, width // 4).astype(F32)
    mine = jnp.zeros((2, vectors, width + 128), F32)
    mine = lax.dynamic_update_slice_in_dim(mine, sums[None, :vectors], layer, 0)
    placed = jnp.zeros((rows * replicas, width + 128), F32)
    placed = lax.dynamic_update_slice_in_dim(placed, sums[vectors + padded :], replica * rows, 0)
    joined = jnp.concatenate(
        [sums[vectors : vectors + padded], mine.reshape(2 * vectors, width + 128), placed], axis=0
    )
    joined = lax.psum(joined, ("section", "dp"))
    quarter = width // 4
    columns = lax.dynamic_slice_in_dim(joined, section * quarter, quarter, axis=1)
    token_grad = columns[:letters_count]
    first = padded + 2 * vectors
    steps = jnp.arange(times_count, dtype=jnp.int32).astype(F32)
    hot = (steps[:, None] == joined[first:, width][None, :]).astype(F32)
    time_grad = jnp.einsum("tb,bd->td", hot, columns[first:], precision=HIGHEST)
    ours = lax.dynamic_slice(joined, (padded + vectors * layer, part * half), (vectors, half))
    each = half // replicas
    flat = lax.dynamic_slice_in_dim(ours[:8], replica * each, each, axis=1)
    ups = lax.dynamic_slice_in_dim(ours[8:12].reshape(1, 4 * half), replica * 4 * each, 4 * each, axis=1)
    return (
        activations,
        token_grad,
        time_grad,
        flat[0:1],
        flat[1:2],
        qkv_grad,
        flat[2:3],
        flat[3:4],
        proj_grad,
        flat[4:5],
        flat[5:6],
        flat[6:7],
        up_grad,
        ups,
        down_grad,
        flat[7:8],
    )


def solution(mesh):
    return jax.shard_map(
        per_device,
        mesh=mesh,
        in_specs=(
            P("dp", None),
            P("dp"),
            P(),
            P(),
            P("section", None),
            P("section", None),
            P("section", None, None),
            P("section", None),
            P("section", None),
            P("section", None, None),
            P("section", None),
            P("section", None),
            P("section", None),
            P("section", None, None),
            P("section", None),
            P("section", None, None),
            P("section", None),
            P("dp", None, None),
        ),
        out_specs=(
            P("dp", None, "section"),
            P(None, "section"),
            P(None, "section"),
            P("section", "dp"),
            P("section", "dp"),
            P("section", "dp", None),
            P("section", "dp"),
            P("section", "dp"),
            P("section", "dp", None),
            P("section", "dp"),
            P("section", "dp"),
            P("section", "dp"),
            P("section", "dp", None),
            P("section", "dp"),
            P("section", "dp", None),
            P("section", "dp"),
        ),
        check_vma=False,
    )
```

```python
import functools
import math

import jax
import jax.numpy as jnp
from jax import lax
from jax.experimental import pallas as pl
from jax.experimental.pallas import tpu as pltpu
from jax.sharding import PartitionSpec as P

HEADS = 12
EPS = 1e-05
HIGHEST = lax.Precision.HIGHEST
MESH = pl.DeviceIdType.MESH
BF = jnp.bfloat16
F32 = jnp.float32
TILES = 12
QKV, PROJ, UP, DOWN = 0, 3, 4, 8
CHUNKS = 2 * TILES
LINE_FIRST = (1, 4, 7, 11)
CORE_LAG, X_LAG, Z_LAG, LINE_START, LINE_LAST = 2, 6, 2, 3, 28
BOTH_BY_X = 1
GELU_A = math.sqrt(2.0 / math.pi)
GELU_B = 0.044715


def flipped(value, bit):
    mask = 2**bit
    return value + mask - 2 * mask * lax.rem(lax.div(value, mask), 2)


def mul(a, b):
    return lax.dot_general(a, b, (((1,), (0,)), ((), ())), preferred_element_type=F32)


def mul_nt(a, b):
    return lax.dot_general(a, b, (((1,), (1,)), ((), ())), preferred_element_type=F32)


def mul_tn(a, b):
    return lax.dot_general(a, b, (((0,), (0,)), ((), ())), preferred_element_type=F32)


def normalize(x):
    mean = jnp.mean(x, axis=-1, keepdims=True)
    centered = x - mean
    spread = jnp.mean(centered * centered, axis=-1, keepdims=True)
    rate = lax.rsqrt(spread + EPS)
    return centered * rate, rate


def scaled_back(gh, gain, n, rate):
    gn = gh * gain
    inner = jnp.mean(gn * n, axis=-1, keepdims=True)
    return (gn - jnp.mean(gn, axis=-1, keepdims=True) - n * inner) * rate


def column(values):
    return jnp.sum(values, axis=0, keepdims=True)


class Refs:
    def __init__(self, names, refs):
        for name, ref in zip(names, refs, strict=True):
            setattr(self, name, ref)


INPUTS = (
    "qkv_in proj_in up_in down_in ga_in sa_in bq_in bv_in bo_in gm_in sm_in bdown_in bup_in "
    "ids_in table_in steps_in time_in cot_in"
).split()


def layer_kernel(seqs, length, width, fused, names, *all_refs):
    refs = Refs(names, all_refs)
    w, par, qkv, probs = refs.w, refs.par, refs.qkv, refs.probs
    acc, ybuf, ysend, y1 = refs.acc, refs.ybuf, refs.ysend, refs.y1
    xs = acc
    slope, gate, h_s, o_s, hf_s, go_s = refs.slope, refs.gate, refs.h_s, refs.o_s, refs.hf_s, refs.go_s
    act, landed, gsum = refs.act, refs.landed, refs.gsum
    s = lax.axis_index("section")
    d = lax.axis_index("dp")
    stage = lax.div(s, 2)
    part = lax.rem(s, 2)
    other = 1 - part
    core = lax.rem(d, 2)
    z = lax.div(d, 2)
    x_dev = (flipped(s, 0), d)
    y_dev = (flipped(s, 1), d)
    far_dev = (flipped(flipped(s, 0), 1), d)
    z_dev = (s, flipped(d, 1))
    c_dev = (s, flipped(d, 0))
    half = width // 2
    wide = width // 4
    hidden_half = 4 * half
    rows = w.shape[4]
    mine = lax.rem(d, 4)
    across = flipped(mine, 1)
    scale = 1.0 / math.sqrt(width // HEADS)
    letters_count = refs.table_in.shape[0]
    padded = refs.table.shape[0]
    vectors = 16
    count = vectors + padded
    nz = lax.axis_size("dp") // 2
    zbits = nz.bit_length() - 1
    ends = nz - 1

    def send(src, dst, send_sem, recv_sem, device):
        return pltpu.make_async_remote_copy(
            src_ref=src,
            dst_ref=dst,
            send_sem=send_sem,
            recv_sem=recv_sem,
            device_id=device,
            device_id_type=MESH,
        )

    def start(copies):
        for copy in copies:
            copy.start()

    def wait(copies):
        for copy in copies:
            copy.wait()

    def signal(sem, device):
        pl.semaphore_signal(sem, inc=1, device_id=device, device_id_type=MESH)

    barrier = pltpu.get_barrier_semaphore()
    greeted = [x_dev, y_dev, far_dev, c_dev, z_dev]
    if fused:
        greeted += [(s, flipped(d, 1 + bit)) for bit in range(1, zbits)]
    for device in greeted:
        signal(barrier, device)
    expected = len(greeted)
    if fused:
        middle_left = jnp.logical_and(z > 0, lax.rem(z, 2) == 0)
        middle_right = jnp.logical_and(z < ends, lax.rem(z, 2) == 1)

        @pl.when(middle_left)
        def _():
            signal(barrier, (s, d - 2))

        @pl.when(middle_right)
        def _():
            signal(barrier, (s, d + 2))

        expected = expected + middle_left.astype(jnp.int32) + middle_right.astype(jnp.int32)

    def tile(index):
        return w[index].reshape(width, width)

    def own_copies(index):
        if index < PROJ:
            pairs = [(refs.qkv_in.at[:, :, :, pl.ds(index * width, width)], w.at[index, part])]
        elif index < UP:
            pairs = [(refs.proj_in, w.at[index, part])]
        elif index < DOWN:
            pairs = [
                (
                    refs.up_in.at[:, :, :, pl.ds(side * hidden_half + (index - UP) * half, half)],
                    w.at[index, part, :, :, :, pl.ds(side * half, half)],
                )
                for side in range(2)
            ]
        else:
            pairs = [(refs.down_in.at[index - DOWN], w.at[index, part])]
        return [
            pltpu.make_async_copy(src, dst, refs.own_sem.at[2 * index + k])
            for k, (src, dst) in enumerate(pairs)
        ]

    def x_weight(index):
        place = w.at[index, part, mine]
        return send(place, place, refs.wx_send.at[index], refs.wx_recv.at[index], x_dev)

    def x_second(index):
        place = w.at[index, part, across]
        return send(place, place, refs.wz_send.at[index], refs.wz_recv.at[index], x_dev)

    def by_z(index):
        return index < TILES - BOTH_BY_X

    def relay(index, which, send_sem, recv_sem, device):
        place = w.at[index, other, which]
        return send(place, place, send_sem.at[index], recv_sem.at[index], device)

    def z_weight(index):
        return relay(index, mine, refs.wz_send, refs.wz_recv, z_dev)

    def c1_weight(index):
        return relay(index, mine, refs.c1_send, refs.c1_recv, c_dev)

    def c2_weight(index):
        return relay(index, across, refs.c2_send, refs.c2_recv, c_dev)

    def pass_first(index):
        relay(index, mine, refs.wx_send, refs.wx_recv, x_dev).wait_recv()

        @pl.when(by_z(index))
        def _():
            z_weight(index).start()

        c1_weight(index).start()

    def pass_second(index):
        relay(index, across, refs.wz_send, refs.wz_recv, z_dev).wait_recv()
        c2_weight(index).start()

    def ready(index):
        relay(index, flipped(mine, 0), refs.c1_send, refs.c1_recv, c_dev).wait_recv()
        relay(index, flipped(across, 0), refs.c2_send, refs.c2_recv, c_dev).wait_recv()

    def settle_weights():
        def settle(index, _):
            x_weight(index).wait_send()
            z_weight(index).wait_send()
            c1_weight(index).wait_send()
            c2_weight(index).wait_send()
            return 0

        lax.fori_loop(0, TILES, settle, 0)

    def vec_copy(which):
        place = refs.vecs.at[which]
        return send(place, place, refs.vec_sem.at[0], refs.vec_sem.at[1], x_dev)

    for index in range(TILES):
        start(own_copies(index))
    singles = ("ga", "sa", "bq", "bv", "bo", "gm", "sm", "bdown")
    for index, name in enumerate(singles):
        refs.vecs[part, index : index + 1, :] = getattr(refs, name + "_in")[...].astype(F32)
    for j in range(4):
        refs.vecs[part, 8 + j : 9 + j, :] = refs.bup_in[:, j * half : (j + 1) * half].astype(F32)
    refs.vecs[part, 12:16, :] = jnp.zeros((4, half), F32)
    refs.table[...] = jnp.zeros_like(refs.table)
    refs.table[:letters_count, :] = refs.table_in[...]
    gsum[...] = jnp.zeros_like(gsum)
    pl.semaphore_wait(barrier, expected)
    for index in range(TILES):
        wait(own_copies(index))
        x_weight(index).start()
        if not by_z(index):
            x_second(index).start()
        if index == 3:
            vec_copy(part).start()

    seats, times_count = refs.ids_in.shape[0], refs.time_in.shape[0]
    line = lax.broadcasted_iota(jnp.int32, (seats, times_count), 0)
    moment = jnp.zeros((seats, times_count), jnp.int32)
    for index in range(seats):
        moment = jnp.where(line == index, refs.steps_in[index], moment)
    hot = lax.broadcasted_iota(jnp.int32, (seats, times_count), 1) == moment
    refs.times[:, :width] = mul(hot.astype(F32).astype(BF), refs.time_in[...])
    refs.times[:, width:] = moment[:, :128].astype(F32)

    pass_first(0)
    pass_first(1)
    pass_second(0)
    pass_first(2)
    pass_second(1)
    pass_first(3)
    pass_second(2)
    pass_first(4)
    pass_second(3)
    pass_first(5)

    @pl.when(stage == 1)
    def _():
        def step(index, _):
            pass_second(index - 2)
            pass_first(index)
            return 0

        lax.fori_loop(6, TILES, step, 0)
        pass_second(TILES - 2)
        pass_second(TILES - 1)

    vec_copy(other).wait_recv()
    par[:, :half] = refs.vecs[0]
    par[:, half:] = refs.vecs[1]
    for index in range(UP):
        ready(index)

    def act_copies(i):
        slot = lax.rem(i, 2)
        return [
            send(
                act.at[slot, device[0]],
                landed.at[part, i],
                refs.act_send.at[i, index],
                refs.act_recv.at[part, i],
                device,
            )
            for index, device in enumerate((y_dev, x_dev, far_dev))
        ]

    def act_own(i):
        return pltpu.make_async_copy(act.at[lax.rem(i, 2), s], landed.at[part, i], refs.act_send.at[i, 3])

    def act_arrival(side, i):
        return send(act.at[0, 0], landed.at[side, i], refs.act_send.at[i, 0], refs.act_recv.at[side, i], y_dev)

    def act_settle(i):
        for copy in act_copies(i):
            copy.wait_send()

    def cot_copy(i):
        return pltpu.make_async_copy(refs.cot_in.at[part * seqs + i], ybuf.at[i], refs.cot_sem.at[i])

    def y_copy(i):
        return send(ysend.at[i], ybuf.at[i], refs.y_send.at[i], refs.y_recv.at[i], y_dev)

    def row(index):
        return par[index : index + 1, :]

    def add_row(index, values):
        gsum[index : index + 1, :width] += column(values)

    lane = lax.broadcasted_iota(jnp.int32, (length, 128), 1)
    low = lane < 64
    side_ones = [(lane < 64).astype(F32).astype(BF), (lane >= 64).astype(F32).astype(BF)]
    side_scaled = [
        ((lane < 64).astype(F32) * scale).astype(BF),
        ((lane >= 64).astype(F32) * scale).astype(BF),
    ]
    pairs = HEADS // 2

    def letters(i):
        ids = refs.ids_in[pl.ds(part * seqs + i, 1), :]
        place = lax.broadcasted_iota(jnp.int32, (padded, length), 0)
        return (place == ids).astype(F32).astype(BF)

    def attn_fwd(i):
        @pl.when(stage == 0)
        def _():
            xs[...] = mul_tn(letters(i), refs.table[...]) + refs.times[pl.ds(part * seqs + i, 1), :width]

        @pl.when(stage == 1)
        def _():
            y_copy(i).wait_recv()
            xs[...] = ybuf[i].astype(F32)
            cot_copy(i).start()

        n, rate = normalize(xs[...])
        refs.n_a[i] = n.astype(BF)
        refs.rates[i] = jnp.broadcast_to(rate, (length, 128))
        h_s[i] = (n * row(0) + row(1)).astype(BF)
        for j in range(3):
            joint = mul(h_s[i], tile(QKV + j))
            if j == 0:
                joint = joint + row(2)
            if j == 2:
                joint = joint + row(3)
            qkv[i, :, j * width : (j + 1) * width] = joint.astype(BF)

        for hp in range(pairs):
            at = hp * 128
            q2 = qkv[i, :, at : at + 128]
            k2 = qkv[i, :, width + at : width + at + 128]
            for side in range(2):
                scores = mul_nt(q2 * side_scaled[side], k2)
                expo = jnp.exp(scores - jnp.max(scores, axis=-1, keepdims=True))
                total = jnp.sum(expo, axis=-1, keepdims=True)
                probs[i, 2 * hp + side] = (expo * (1.0 / total)).astype(BF)
        for hp in range(pairs):
            at = hp * 128
            v2 = qkv[i, :, 2 * width + at : 2 * width + at + 128]
            outs = [mul(probs[i, 2 * hp + side], v2) for side in range(2)]
            o_s[i, :, at : at + 128] = jnp.where(low, outs[0], outs[1]).astype(BF)
        y1[i] = (xs[...] + (mul(o_s[i], tile(PROJ)) + row(4))).astype(BF)

    def feed_fwd(i):
        def arrived(first, last):
            @pl.when(i == 0)
            def _():
                def one(index, _):
                    ready(index)
                    return 0

                lax.fori_loop(first, last, one, 0)

        arrived(UP, DOWN)
        x = y1[i].astype(F32)
        n, rate = normalize(x)
        refs.n_f[i] = n.astype(BF)
        refs.rates[i] = jnp.where(low, refs.rates[i], jnp.broadcast_to(rate, (length, 128)))
        hf_s[i] = (n * row(5) + row(6)).astype(BF)
        acc[...] = x + row(7)
        for j in range(4):
            u = mul(hf_s[i], tile(UP + j)) + row(8 + j)
            square = u * u
            t = jnp.tanh(u * (GELU_A + GELU_A * GELU_B * square))
            both = 0.5 + 0.5 * t
            gate[i, j] = (u * both).astype(BF)
            bend = (0.5 * GELU_A + 1.5 * GELU_A * GELU_B * square) * u
            slope[i, j] = (both + bend * (1.0 - t * t)).astype(BF)
        arrived(DOWN, TILES)
        down = mul(gate[i, 0], tile(DOWN))
        for j in range(1, 4):
            down = down + mul(gate[i, j], tile(DOWN + j))
        acc[...] += down

        @pl.when(stage == 0)
        def _():
            ysend[i] = acc[...].astype(BF)
            y_copy(i).start()

        @pl.when(stage == 1)
        def _():
            @pl.when(i >= 2)
            def _():
                act_settle(i - 2)
                act_own(i - 2).wait()

            for q in range(4):
                act[lax.rem(i, 2), q] = acc[:, q * wide : (q + 1) * wide].astype(BF)
            start(act_copies(i))
            act_own(i).start()

    def feed_bwd(i):
        @pl.when(stage == 0)
        def _():
            y_copy(i).wait_recv()

        @pl.when(stage == 1)
        def _():
            cot_copy(i).wait()

        add_row(7, ybuf[i].astype(F32))
        for j in range(4):
            ga = mul_nt(ybuf[i], tile(DOWN + j))
            gu = (ga * slope[i, j].astype(F32)).astype(BF)
            slope[i, j] = gu
            add_row(8 + j, gu.astype(F32))
        gh = mul_nt(slope[i, 0], tile(UP))
        for j in range(1, 4):
            gh = gh + mul_nt(slope[i, j], tile(UP + j))
        n = refs.n_f[i].astype(F32)
        add_row(5, gh * n)
        add_row(6, gh)
        gx = ybuf[i].astype(F32) + scaled_back(gh, row(5), n, refs.rates[i][:, 64:65])
        y1[i] = gx.astype(BF)

    def attn_bwd(i):
        add_row(4, y1[i].astype(F32))
        go_s[...] = mul_nt(y1[i], tile(PROJ)).astype(BF)
        for hp in range(pairs):
            at = hp * 128
            v2 = qkv[i, :, 2 * width + at : 2 * width + at + 128]
            go2 = go_s[:, at : at + 128]
            gv = []
            for side in range(2):
                pb = probs[i, 2 * hp + side]
                gp = mul_nt(go2 * side_ones[side], v2)
                p = pb.astype(F32)
                pg = p * gp
                gs = (pg - p * jnp.sum(pg, axis=-1, keepdims=True)).astype(BF)
                gv.append(mul_tn(pb, go2))
                probs[i, 2 * hp + side] = gs
            qkv[i, :, 2 * width + at : 2 * width + at + 128] = jnp.where(low, gv[0], gv[1]).astype(BF)
        for hp in range(pairs):
            at = hp * 128
            q2 = qkv[i, :, at : at + 128]
            k2 = qkv[i, :, width + at : width + at + 128]
            gq, gk = [], []
            for side in range(2):
                gs = probs[i, 2 * hp + side]
                gq.append(mul(gs, k2))
                gk.append(mul_tn(gs, q2))
            qkv[i, :, at : at + 128] = (jnp.where(low, gq[0], gq[1]) * scale).astype(BF)
            qkv[i, :, width + at : width + at + 128] = (jnp.where(low, gk[0], gk[1]) * scale).astype(BF)
        pieces = [qkv[i, :, j * width : (j + 1) * width] for j in range(3)]
        add_row(2, pieces[0].astype(F32))
        add_row(3, pieces[2].astype(F32))
        gh = mul_nt(pieces[0], tile(QKV)) + mul_nt(pieces[1], tile(QKV + 1)) + mul_nt(pieces[2], tile(QKV + 2))
        n = refs.n_a[i].astype(F32)
        add_row(0, gh * n)
        add_row(1, gh)
        acc[...] = y1[i].astype(F32) + scaled_back(gh, row(0), n, refs.rates[i][:, 0:1])

        @pl.when(stage == 1)
        def _():
            ysend[i] = acc[...].astype(BF)
            y_copy(i).start()

        @pl.when(stage == 0)
        def _():
            high = acc[...].astype(BF)
            rest = (acc[...] - high.astype(F32)).astype(BF)
            hot = letters(i)
            gsum[vectors:count, :width] += mul(hot, high) + mul(hot, rest)
            mark = part * seqs + i
            stamp = refs.times[pl.ds(mark, 1), :]
            gsum[pl.ds(count + mark, 1), :] = jnp.concatenate([column(acc[...]), stamp[:, width:]], axis=1)

    units = (attn_fwd, feed_fwd, feed_bwd, attn_bwd)
    steps = 0
    if fused:
        step = reduce_steps(refs, seqs, length, width, send, signal, act_arrival, act_own, settle_weights)
        units = units + (step,)
        steps = CHUNKS + X_LAG + Z_LAG * ends

    def unit(u, _):
        early = u < 2 * seqs
        kind0 = jnp.where(early, lax.div(u, seqs), 2 + lax.rem(u, 2))
        index0 = jnp.where(early, lax.rem(u, seqs), lax.div(u, 2) - seqs)
        kind1 = lax.rem(u, 4)
        index1 = lax.div(u, 4)
        if fused:
            last = 4 * seqs - 1
            ahead = 4
            kind0 = jnp.where(u >= last, 4, kind0)
            index0 = jnp.where(u >= last, jnp.where(u < last + ahead, u - last, u - last - 1), index0)
            kind0 = jnp.where(u == last + ahead, 3, kind0)
            index0 = jnp.where(u == last + ahead, seqs - 1, index0)
            kind1 = jnp.where(u > last, 4, kind1)
            index1 = jnp.where(u > last, u - last - 1, index1)
        kind = jnp.where(stage == 0, kind0, kind1)
        i = jnp.where(stage == 0, index0, index1)

        @pl.when(jnp.logical_and(stage == 0, jnp.logical_and(u >= 1, u <= 4)))
        def _():
            pass_second(2 + 2 * u)
            pass_second(3 + 2 * u)

        @pl.when(jnp.logical_and(stage == 0, jnp.logical_and(u >= 1, u <= 3)))
        def _():
            pass_first(4 + 2 * u)
            pass_first(5 + 2 * u)

        for index, run in enumerate(units):

            @pl.when(kind == index)
            def _():
                run(i)

        return 0

    lax.fori_loop(0, 4 * seqs + steps, unit, 0)

    vec_copy(part).wait_send()
    if not fused:
        settle_weights()

    def finish(i, _):
        y_copy(i).wait_send()

        @pl.when(jnp.logical_and(stage == 1, i >= 2))
        def _():
            act_settle(i)

        return 0

    lax.fori_loop(0, seqs, finish, 0)
    if not fused:

        @pl.when(stage == 1)
        def _():
            for i in range(2, seqs):
                act_own(i).wait()

        for i in range(seqs):
            for side in range(2):

                @pl.when(jnp.logical_or(stage == 0, part != side))
                def _():
                    act_arrival(side, i).wait_recv()

        refs.sums_out[...] = gsum[...]
        copies = []
        for i in range(seqs):
            place = pl.ds(i * length, length)
            for index, ref in enumerate((hf_s, h_s, o_s, ybuf)):
                copies.append((ref.at[i], refs.fixed_out.at[index, place]))
            for j in range(4):
                copies.append((slope.at[i, j], refs.moving_out.at[j, place]))
                copies.append((gate.at[i, j], refs.moving_out.at[8 + j, place]))
            for j in range(3):
                copies.append((qkv.at[i, :, pl.ds(j * width, width)], refs.moving_out.at[4 + j, place]))
            copies.append((y1.at[i], refs.moving_out.at[7, place]))
        copies.append((landed, refs.act_out))
        copies = [
            pltpu.make_async_copy(src, dst, refs.keep_sem.at[index]) for index, (src, dst) in enumerate(copies)
        ]
        start(copies)
        wait(copies)


def reduce_steps(refs, seqs, length, width, send, signal, act_arrival, act_own, settle_weights):
    s = lax.axis_index("section")
    d = lax.axis_index("dp")
    stage = lax.div(s, 2)
    part = lax.rem(s, 2)
    other = 1 - part
    core = lax.rem(d, 2)
    z = lax.div(d, 2)
    x_dev = (flipped(s, 0), d)
    y_dev = (flipped(s, 1), d)
    c_dev = (s, flipped(d, 0))
    right_dev = (s, d + 2)
    left_dev = (s, d - 2)
    w, gsum = refs.w, refs.gsum
    nz = w.shape[2]
    rows = w.shape[4]
    ends = nz - 1
    slots = refs.x_buf.shape[0]
    core_slots = refs.core_buf.shape[0]
    directs = CHUNKS - len(LINE_FIRST)
    half = width // 2
    tokens = seqs * length
    core_buf, x_buf, right_buf, left_buf = refs.core_buf, refs.x_buf, refs.right_buf, refs.left_buf
    vectors = 16
    count = vectors + refs.table.shape[0]
    split = count // 2
    zbits = nz.bit_length() - 1
    own = gsum.shape[0] - count

    def where(tile):
        return jnp.where(tile < 4, tile + 4, jnp.where(tile < 8, tile - 4, tile))

    def at(k, *index):
        columns = pl.ds(pl.multiple_of(lax.rem(k, 2) * half, 128), half)
        return (where(lax.div(k, 2)),) + index + (slice(None), columns)

    everything = slice(None)

    def turned(k):
        return functools.reduce(jnp.logical_or, [k == chunk for chunk in LINE_FIRST])

    def direct(k):
        return jnp.logical_and(jnp.logical_and(k >= 0, k < CHUNKS), jnp.logical_not(turned(k)))

    def order(k):
        return k - sum((k > chunk).astype(jnp.int32) for chunk in LINE_FIRST)

    def slot(k):
        return lax.rem(order(k), slots)

    def core_slot(k):
        return lax.rem(k, core_slots)

    def core_copy(k):
        return send(
            w.at[at(k, everything, everything, 1 - core)],
            core_buf.at[core_slot(k)],
            refs.core_send.at[core_slot(k)],
            refs.core_recv.at[core_slot(k)],
            c_dev,
        )

    def x_copy(k):
        return send(
            w.at[at(k, other, everything, core)],
            x_buf.at[slot(k)],
            refs.x_send.at[slot(k)],
            refs.x_recv.at[slot(k)],
            x_dev,
        )

    class Line:
        def __init__(self, name, slot, side, spend_from, grant_to):
            self.right_buf = getattr(refs, name + "right_buf")
            self.left_buf = getattr(refs, name + "left_buf")
            self.right_sems = getattr(refs, name + "right_send"), getattr(refs, name + "right_recv")
            self.left_sems = getattr(refs, name + "left_send"), getattr(refs, name + "left_recv")
            self.right_credit = getattr(refs, name + "right_credit")
            self.left_credit = getattr(refs, name + "left_credit")
            self.slots = self.right_buf.shape[0]
            self.slot = lambda job: lax.rem(slot(job), self.slots)
            self.side = side
            self.spend_from = spend_from
            self.grant_to = grant_to

        def place(self, job, j):
            k, side = self.side(job)
            return at(k, side, j, core)

        def right_copy(self, job, j):
            sends, recvs = self.right_sems
            slot = self.slot(job)
            target = self.right_buf.at[slot, j]
            return send(w.at[self.place(job, j)], target, sends.at[slot, j], recvs.at[slot, j], right_dev)

        def left_copy(self, job, j):
            sends, recvs = self.left_sems
            slot = self.slot(job)
            target = self.left_buf.at[slot, j]
            return send(w.at[self.place(job, j)], target, sends.at[slot, j], recvs.at[slot, j], left_dev)

        def add(self, job, j, buffer):
            both = w[self.place(job, j)].astype(F32) + buffer[self.slot(job), j].astype(F32)
            w[self.place(job, j)] = both.astype(BF)

        def right_step(self, job):
            @pl.when(jnp.logical_and(z < ends, self.spend_from(job)))
            def _():
                pl.semaphore_wait(self.right_credit, 1)

            for j in range(ends, -1, -1):

                @pl.when(jnp.logical_and(z > 0, j >= z))
                def _():
                    self.right_copy(job, j).wait_recv()
                    self.add(job, j, self.right_buf)

                @pl.when(jnp.logical_and(j > z, self.spend_from(job)))
                def _():
                    self.right_copy(job, j).wait_send()

                @pl.when(j > z)
                def _():
                    self.right_copy(job, j).start()

            @pl.when(jnp.logical_and(z > 0, self.grant_to(job)))
            def _():
                signal(self.right_credit, left_dev)

        def left_step(self, job):
            @pl.when(jnp.logical_and(z > 0, self.spend_from(job)))
            def _():
                pl.semaphore_wait(self.left_credit, 1)

            for j in range(nz):

                @pl.when(jnp.logical_and(z < ends, j <= z))
                def _():
                    self.left_copy(job, j).wait_recv()
                    self.add(job, j, self.left_buf)

                @pl.when(jnp.logical_and(j < z, self.spend_from(job)))
                def _():
                    self.left_copy(job, j).wait_send()

                @pl.when(j < z)
                def _():
                    self.left_copy(job, j).start()

            @pl.when(jnp.logical_and(z < ends, self.grant_to(job)))
            def _():
                signal(self.left_credit, right_dev)

        def settle(self, job):
            for j in range(nz):

                @pl.when(j > z)
                def _():
                    self.right_copy(job, j).wait_send()

                @pl.when(j < z)
                def _():
                    self.left_copy(job, j).wait_send()

    line_slots = refs.right_buf.shape[0]
    main = Line(
        "",
        order,
        lambda k: (k, part),
        lambda k: order(k) >= line_slots,
        lambda k: order(k) + line_slots < directs,
    )
    side_jobs = 2 * len(LINE_FIRST)
    side_slots = refs.b_right_buf.shape[0]

    def side_place(job):
        chunk = jnp.int32(LINE_FIRST[-1])
        for index in range(len(LINE_FIRST) - 1, -1, -1):
            chunk = jnp.where(job < 2 * (index + 1), LINE_FIRST[index], chunk)
        return chunk, lax.rem(job, 2)

    beside = Line(
        "b_",
        lambda job: job,
        side_place,
        lambda job: job >= side_slots,
        lambda job: job + side_slots < side_jobs,
    )

    def grads_copy(k):
        return pltpu.make_async_copy(refs.grad_stage, refs.grads_out.at[k], refs.out_sem.at[0])

    def act_copy(turn):
        return pltpu.make_async_copy(refs.act_stage, refs.act_out.at[turn], refs.out_sem.at[1])

    def put_grads(k, value):
        @pl.when(k > 0)
        def _():
            grads_copy(k).wait()

        refs.grad_stage[...] = value
        grads_copy(k).start()

    def last_copy(index):
        k = jnp.int32(LINE_FIRST[index])
        return send(
            w.at[at(k, other, z, core)],
            refs.last_buf.at[index],
            refs.last_send.at[index],
            refs.last_recv.at[index],
            x_dev,
        )

    def put_last(index):
        k = jnp.int32(LINE_FIRST[index])
        last_copy(index).wait_recv()
        put_grads(k, w[at(k, part, z, core)].astype(F32) + refs.last_buf[index].astype(F32))

    def flat(value):
        return value.reshape(tokens, width)

    def store(k, value):
        w[where(k)] = value.astype(BF).reshape(2, nz, 2, rows, width)

    def products(tile):
        @pl.when(tile < 4)
        def _():
            store(tile, mul_tn(flat(refs.hf_s[...]), flat(refs.slope[:, tile])))

        for j in range(3):

            @pl.when(tile == 4 + j)
            def _():
                store(tile, mul_tn(flat(refs.h_s[...]), flat(refs.qkv[:, :, j * width : (j + 1) * width])))

        @pl.when(tile == 7)
        def _():
            store(tile, mul_tn(flat(refs.o_s[...]), flat(refs.y1[...])))

        @pl.when(jnp.logical_and(tile >= 4, tile < 8))
        def _():
            value = mul_tn(flat(refs.gate[:, tile - 4]), flat(refs.ybuf[...])).astype(BF)
            value = value.reshape(2, 2, 4, rows, width)
            for block in range(4):
                w[8 + block, :, tile - 4] = value[:, :, block]

    def inside(k):
        return jnp.logical_and(k >= 0, k < CHUNKS)

    def core_sums():
        return send(
            gsum.at[pl.ds(0, count)], refs.sums_buf, refs.sums_sem.at[0], refs.sums_sem.at[1], c_dev
        )

    def x_sums():
        return [
            send(refs.adds.at[0], refs.adds_buf.at[0], refs.adds_send.at[0], refs.adds_recv.at[0], x_dev),
            send(
                gsum.at[pl.ds(count, own)],
                refs.stamp_buf,
                refs.stamp_send.at[0],
                refs.stamp_recv.at[0],
                x_dev,
            ),
        ]

    def block(bit, place_core, place_z):
        size = own * 2**bit
        first = place_core * nz * own + lax.div(place_z, 2**bit) * size
        return pl.ds(pl.multiple_of(first, 8), size)

    def z_sums(bit, arriving):
        there = flipped(z, bit)
        place = refs.stamps.at[block(bit, core, there if arriving else z)]
        device = (s, flipped(d, 1 + bit))
        return [
            send(
                refs.adds.at[1 + bit],
                refs.adds_buf.at[1 + bit],
                refs.adds_send.at[1 + bit],
                refs.adds_recv.at[1 + bit],
                device,
            ),
            send(place, place, refs.stamp_send.at[1 + bit], refs.stamp_recv.at[1 + bit], device),
        ]

    def last_sums(arriving):
        side = 1 - core if arriving else core
        place = refs.stamps.at[block(zbits, side, z)]
        half_sums = refs.whole.at[side]
        return [
            send(half_sums, half_sums, refs.sums_sem.at[2], refs.sums_sem.at[3], c_dev),
            send(place, place, refs.stamp_send.at[1 + zbits], refs.stamp_recv.at[1 + zbits], c_dev),
        ]

    def final_copies():
        return [
            send(src, dst, refs.final_send.at[index], refs.final_recv.at[index], y_dev)
            for index, (src, dst) in enumerate(((refs.whole, refs.token_out), (refs.stamps, refs.stamp_out)))
        ]

    def arrive(copies):
        for copy in copies:
            copy.wait_recv()

    def begin(copies):
        for copy in copies:
            copy.start()

    def small_step(t):
        @pl.when(t == 5)
        def _():
            core_sums().start()

        @pl.when(t == 8)
        def _():
            core_sums().wait_recv()
            sums = gsum[:count, :width] + refs.sums_buf[:, :width]

            @pl.when(core == 0)
            def _():
                refs.adds[0] = sums[:split]

            @pl.when(core == 1)
            def _():
                refs.adds[0] = sums[split:]

            begin(x_sums())

        @pl.when(t == 12)
        def _():
            arrive(x_sums())
            refs.adds[1] = refs.adds[0] + refs.adds_buf[0]
            refs.stamps[block(0, core, z), :] = gsum[count:, :] + refs.stamp_buf[...]
            begin(z_sums(0, False))

        for bit in range(zbits):

            @pl.when(t == 16 + 4 * bit)
            def _():
                arrive(z_sums(bit, True))
                total = refs.adds[1 + bit] + refs.adds_buf[1 + bit]
                if bit + 1 < zbits:
                    refs.adds[2 + bit] = total
                    begin(z_sums(bit + 1, False))
                else:
                    refs.whole[core] = total
                    begin(last_sums(False))

        @pl.when(t == 16 + 4 * zbits)
        def _():
            arrive(last_sums(True))
            refs.small_out[...] = refs.whole[...]

            @pl.when(stage == 0)
            def _():
                begin(final_copies())
                refs.token_out[...] = refs.whole[...]
                refs.stamp_out[...] = refs.stamps[...]

    def act_step(t):
        turn = t - 6

        @pl.when(jnp.logical_and(turn >= 0, turn < 2 * seqs))
        def _():
            side = lax.div(turn, seqs)
            i = lax.rem(turn, seqs)
            ours = jnp.logical_and(stage == 1, side == part)

            @pl.when(jnp.logical_not(ours))
            def _():
                act_arrival(side, i).wait_recv()

            @pl.when(jnp.logical_and(ours, i >= 2))
            def _():
                act_own(i).wait()

            @pl.when(turn > 0)
            def _():
                act_copy(turn - 1).wait()

            refs.act_stage[...] = refs.landed[side, i].astype(F32).T
            act_copy(turn).start()

    def step(t):
        @pl.when(t == 0)
        def _():
            settle_weights()

        @pl.when(jnp.logical_and(lax.rem(t, 2) == 0, t < 16))
        def _():
            products(lax.div(t, 2))

        @pl.when(t < CHUNKS)
        def _():
            @pl.when(t >= core_slots)
            def _():
                pl.semaphore_wait(refs.core_credit, 1)
                core_copy(t).wait_send()

            core_copy(t).start()

        k1 = t - CORE_LAG

        @pl.when(inside(k1))
        def _():
            core_copy(k1).wait_recv()
            for side in range(2):
                place = at(k1, side, everything, core)
                both = w[place].astype(F32) + core_buf[core_slot(k1), side].astype(F32)
                w[place] = both.astype(BF)

            @pl.when(k1 + core_slots < CHUNKS)
            def _():
                signal(refs.core_credit, c_dev)

        @pl.when(direct(k1))
        def _():
            @pl.when(order(k1) >= slots)
            def _():
                pl.semaphore_wait(refs.x_credit, 1)
                x_copy(k1).wait_send()

            x_copy(k1).start()

        small_step(t)
        act_step(t)
        k2 = t - X_LAG

        @pl.when(direct(k2))
        def _():
            x_copy(k2).wait_recv()
            place = at(k2, part, everything, core)
            both = w[place].astype(F32) + x_buf[slot(k2)].astype(F32)
            w[place] = both.astype(BF)

            @pl.when(order(k2) + slots < directs)
            def _():
                signal(refs.x_credit, x_dev)

        k3 = t - X_LAG - Z_LAG * z
        k4 = t - X_LAG - Z_LAG * (ends - z)
        k5 = jnp.minimum(k3, k4)

        @pl.when(direct(k3))
        def _():
            main.right_step(k3)

        @pl.when(direct(k4))
        def _():
            main.left_step(k4)

        @pl.when(direct(k5))
        def _():
            put_grads(k5, w[main.place(k5, z)].astype(F32))

        def listed(turn):
            even = lax.rem(turn + 64, 2) == 0
            return jnp.logical_and(even, jnp.logical_and(turn >= 0, turn < 2 * side_jobs))

        j3 = t - LINE_START - Z_LAG * z
        j4 = t - LINE_START - Z_LAG * (ends - z)

        @pl.when(listed(j3))
        def _():
            beside.right_step(lax.div(j3, 2))

        @pl.when(listed(j4))
        def _():
            beside.left_step(lax.div(j4, 2))

        @pl.when(t == LINE_LAST)
        def _():
            for index in range(len(LINE_FIRST)):
                last_copy(index).start()

        @pl.when(t == CHUNKS + X_LAG + Z_LAG * ends - 1)
        def _():
            for index in range(len(LINE_FIRST)):
                put_last(index)
            finish()

    def finish():
        def settle_core(k, _):
            core_copy(k).wait_send()
            return 0

        def settle_x(k, _):
            x_copy(k).wait_send()
            return 0

        def settle_main(k, _):
            main.settle(k)
            return 0

        def settle_beside(job, _):
            beside.settle(job)
            return 0

        lax.fori_loop(CHUNKS - core_slots, CHUNKS, settle_core, 0)
        lax.fori_loop(CHUNKS - slots, CHUNKS, settle_x, 0)
        lax.fori_loop(CHUNKS - line_slots, CHUNKS, settle_main, 0)
        lax.fori_loop(side_jobs - side_slots, side_jobs, settle_beside, 0)
        for index in range(len(LINE_FIRST)):
            last_copy(index).wait_send()
        grads_copy(0).wait()
        act_copy(2 * seqs - 1).wait()
        sends = [core_sums()] + x_sums() + last_sums(False)
        for bit in range(zbits):
            sends += z_sums(bit, False)
        for copy in sends:
            copy.wait_send()

        @pl.when(stage == 0)
        def _():
            for copy in final_copies():
                copy.wait_send()

        @pl.when(stage == 1)
        def _():
            arrive(final_copies())

    return step


def run_layers(weights, singles, ids, table, steps, times, cot, replicas, fused):
    rows, length = ids.shape
    width = cot.shape[2]
    half = width // 2
    seqs = rows // 2
    tokens = seqs * length
    padded = -(-table.shape[0] // 16) * 16
    count = 16 + padded
    nz = replicas // 2
    lane = width + 128
    cut = half // 8
    dma = pltpu.SemaphoreType.DMA
    credit = pltpu.SemaphoreType.REGULAR
    anywhere = pl.BlockSpec(memory_space=pl.ANY)
    local = pl.BlockSpec(memory_space=pltpu.VMEM)
    vm = pltpu.VMEM
    shape = jax.ShapeDtypeStruct
    if fused:
        outs = {
            "act_out": (shape((2 * seqs, width // 4, length), F32), anywhere),
            "grads_out": (shape((CHUNKS, cut, half), F32), anywhere),
            "small_out": (shape((2, count // 2, width), F32), local),
            "token_out": (shape((2, count // 2, width), F32), local),
            "stamp_out": (shape((rows * replicas, lane), F32), local),
        }
    else:
        outs = {
            "act_out": (shape((2, seqs, length, width // 4), BF), anywhere),
            "sums_out": (shape((count + rows, lane), F32), local),
            "fixed_out": (shape((4, tokens, width), BF), anywhere),
            "moving_out": (shape((12, tokens, width), BF), anywhere),
        }
    scratch = {
        "w": vm((TILES, 2, 4, 2, cut, width), BF),
        "vecs": vm((2, 16, half), F32),
        "table": vm((padded, width), BF),
        "par": vm((16, width), F32),
        "times": vm((rows, lane), F32),
        "acc": vm((length, width), F32),
        "n_a": vm((seqs, length, width), BF),
        "n_f": vm((seqs, length, width), BF),
        "rates": vm((seqs, length, 128), F32),
        "qkv": vm((seqs, length, 3 * width), BF),
        "probs": vm((seqs, HEADS, length, length), BF),
        "y1": vm((seqs, length, width), BF),
        "slope": vm((seqs, 4, length, width), BF),
        "gate": vm((seqs, 4, length, width), BF),
        "h_s": vm((seqs, length, width), BF),
        "o_s": vm((seqs, length, width), BF),
        "hf_s": vm((seqs, length, width), BF),
        "go_s": vm((length, width), BF),
        "ybuf": vm((seqs, length, width), BF),
        "ysend": vm((seqs, length, width), BF),
        "act": vm((2, 4, length, width // 4), BF),
        "landed": vm((2, seqs, length, width // 4), BF),
        "gsum": vm((count + rows, lane), F32),
        "own_sem": dma((2 * TILES,)),
        "vec_sem": dma((2,)),
        "cot_sem": dma((seqs,)),
        "y_send": dma((seqs,)),
        "y_recv": dma((seqs,)),
        "act_send": dma((seqs, 4)),
        "act_recv": dma((2, seqs)),
    }
    for name in ("wx", "wz", "c1", "c2"):
        scratch[name + "_send"] = dma((TILES,))
        scratch[name + "_recv"] = dma((TILES,))
    if fused:
        zbits = nz.bit_length() - 1
        scratch |= {
            "core_buf": vm((3, 2, nz, cut, half), BF),
            "x_buf": vm((X_LAG, nz, cut, half), BF),
            "right_buf": vm((4, nz, cut, half), BF),
            "left_buf": vm((4, nz, cut, half), BF),
            "b_right_buf": vm((2, nz, cut, half), BF),
            "b_left_buf": vm((2, nz, cut, half), BF),
            "last_buf": vm((len(LINE_FIRST), cut, half), BF),
            "last_send": dma((len(LINE_FIRST),)),
            "last_recv": dma((len(LINE_FIRST),)),
            "sums_buf": vm((count, lane), F32),
            "adds": vm((1 + zbits, count // 2, width), F32),
            "adds_buf": vm((1 + zbits, count // 2, width), F32),
            "whole": vm((2, count // 2, width), F32),
            "stamp_buf": vm((rows, lane), F32),
            "stamps": vm((rows * replicas, lane), F32),
            "grad_stage": vm((cut, half), F32),
            "act_stage": vm((width // 4, length), F32),
            "out_sem": dma((2,)),
            "sums_sem": dma((4,)),
            "adds_send": dma((1 + zbits,)),
            "adds_recv": dma((1 + zbits,)),
            "stamp_send": dma((2 + zbits,)),
            "stamp_recv": dma((2 + zbits,)),
            "final_send": dma((2,)),
            "final_recv": dma((2,)),
            "core_credit": credit,
            "x_credit": credit,
            "right_credit": credit,
            "left_credit": credit,
            "b_right_credit": credit,
            "b_left_credit": credit,
        }
        for name in ("core", "x"):
            slots = scratch[name + "_buf"].shape[0]
            scratch[name + "_send"] = dma((slots,))
            scratch[name + "_recv"] = dma((slots,))
        for name in ("right", "left", "b_right", "b_left"):
            slots = scratch[name + "_buf"].shape[0]
            scratch[name + "_send"] = dma((slots, nz))
            scratch[name + "_recv"] = dma((slots, nz))
    else:
        scratch["keep_sem"] = dma((16 * seqs + 1,))
    names = INPUTS + list(outs) + list(scratch)
    return pl.pallas_call(
        functools.partial(layer_kernel, seqs, length, width, fused, names),
        out_shape=tuple(out[0] for out in outs.values()),
        in_specs=[anywhere] * 4
        + [local] * 11
        + [pl.BlockSpec(memory_space=pltpu.SMEM), local, anywhere],
        out_specs=tuple(out[1] for out in outs.values()),
        scratch_shapes=list(scratch.values()),
        compiler_params=pltpu.CompilerParams(
            collective_id=0, has_side_effects=True, vmem_limit_bytes=64 * 2**20 - 2**17
        ),
    )(*weights, *singles, ids, table, steps, times, cot)


def three_parts(value):
    first = value.astype(BF)
    rest = value - first.astype(F32)
    second = rest.astype(BF)
    return first, second, (rest - second.astype(F32)).astype(BF)


def finish_kernel(
    act,
    grads,
    small,
    token,
    stamp,
    act_out,
    token_out,
    time_out,
    ga_out,
    sa_out,
    qkv_out,
    bq_out,
    bv_out,
    proj_out,
    bo_out,
    gm_out,
    sm_out,
    up_out,
    bup_out,
    down_out,
    bdown_out,
    act_s,
    grads_s,
    sem,
):
    s = lax.axis_index("section")
    d = lax.axis_index("dp")
    part = lax.rem(s, 2)
    rows, half = grads.shape[1:]
    width = 2 * half
    quarter = width // 4
    loads = [
        pltpu.make_async_copy(src, dst, sem.at[25 + index])
        for index, (src, dst) in enumerate(((act, act_s), (grads, grads_s)))
    ]
    for copy in loads:
        copy.start()
    pairs = [(act_s, act_out)]
    for side in range(2):
        for j in range(4):
            columns = pl.ds(side * 4 * half + j * half, half)
            pairs.append((grads_s.at[2 * j + side], up_out.at[0, :, columns]))
        for j in range(3):
            columns = pl.ds(j * width + side * half, half)
            pairs.append((grads_s.at[8 + 2 * j + side], qkv_out.at[0, :, columns]))
        columns = pl.ds(side * half, half)
        pairs.append((grads_s.at[14 + side], proj_out.at[0, :, columns]))
        for j in range(4):
            pairs.append((grads_s.at[16 + 2 * j + side], down_out.at[0, pl.ds(j * rows, rows), columns]))
    copies = [pltpu.make_async_copy(src, dst, sem.at[index]) for index, (src, dst) in enumerate(pairs)]
    for copy in loads:
        copy.wait()
    for copy in copies:
        copy.start()
    vectors = small[0, :16, :]
    lower = jnp.where(part == 0, vectors[:, :half], vectors[:, half:])
    turned = pltpu.roll(lower, lax.rem(half - d * rows, half), 1)
    outs = (ga_out, sa_out, bq_out, bv_out, bo_out, gm_out, sm_out, bdown_out)
    for index, out in enumerate(outs):
        out[...] = turned[index : index + 1, :rows]
    per_row = half // (4 * rows)
    shifted = pltpu.roll(lower, lax.rem(half - lax.rem(d, per_row) * 4 * rows, half), 1)
    for j in range(4):

        @pl.when(lax.div(d, per_row) == j)
        def _():
            bup_out[...] = shifted[8 + j : 9 + j, : 4 * rows]

    times_count = time_out.shape[1]
    spread = -(-times_count // 128) * 128
    place = lax.broadcasted_iota(jnp.int32, (stamp.shape[0], spread), 1).astype(F32)
    hot = (place == stamp[:, width : width + 1]).astype(F32).astype(BF)
    letters = token_out.shape[0]
    split = token.shape[1]
    for q in range(4):

        @pl.when(s == q)
        def _():
            at = slice(q * quarter, (q + 1) * quarter)
            token_out[: split - 16, :] = token[0, 16:, at]
            token_out[split - 16 :, :] = token[1, : letters + 16 - split, at]
            sums = jnp.zeros((quarter, spread), F32)
            for piece in three_parts(stamp[:, at]):
                sums = sums + mul_tn(piece, hot)
            time_out[...] = sums[:, :times_count]

    for copy in copies:
        copy.wait()


def run_finish(act, grads, small, token, stamp, letters_count, times_count):
    rows, half = grads.shape[1:]
    width = 2 * half
    quarter = width // 4
    local = pl.BlockSpec(memory_space=pltpu.VMEM)
    anywhere = pl.BlockSpec(memory_space=pl.ANY)
    single = (1, rows)
    shapes = [
        (act.shape, anywhere),
        ((letters_count, quarter), local),
        ((quarter, times_count), local),
        (single, local),
        (single, local),
        ((1, rows, 3 * width), anywhere),
        (single, local),
        (single, local),
        ((1, rows, width), anywhere),
        (single, local),
        (single, local),
        (single, local),
        ((1, rows, 4 * width), anywhere),
        ((1, 4 * rows), local),
        ((1, 4 * rows, width), anywhere),
        (single, local),
    ]
    outs = pl.pallas_call(
        finish_kernel,
        out_shape=tuple(jax.ShapeDtypeStruct(shape, F32) for shape, _ in shapes),
        in_specs=[anywhere] * 2 + [local] * 3,
        out_specs=tuple(spec for _, spec in shapes),
        scratch_shapes=[
            pltpu.VMEM(act.shape, F32),
            pltpu.VMEM(grads.shape, F32),
            pltpu.SemaphoreType.DMA((27,)),
        ],
        compiler_params=pltpu.CompilerParams(vmem_limit_bytes=62 * 2**20),
    )(act, grads, small, token, stamp)
    return (jnp.swapaxes(outs[0], 1, 2), outs[1], jnp.swapaxes(outs[2], 0, 1)) + tuple(outs[3:])


def plain_reduce(fixed, moving, lower):
    def grad(left, right):
        return jnp.einsum("tk,tn->kn", left, right, preferred_element_type=F32)

    width = fixed.shape[2]
    half = width // 2
    hf, h, o, gz = (fixed[index] for index in range(4))
    ups = jnp.stack([grad(hf, moving[j]) for j in range(4)])
    up = ups.reshape(4, width, 2, half).transpose(1, 2, 0, 3).reshape(width, 4 * width)
    joint = jnp.concatenate([grad(h, moving[4 + j]) for j in range(3)], axis=1)
    proj = grad(o, moving[7])
    downs = jnp.stack([grad(moving[8 + j], gz) for j in range(4)])
    down = downs.reshape(4, 2, half, width).transpose(1, 0, 2, 3).reshape(4 * width, width)
    results = []
    for total in (joint, proj, up, down):
        halves = total.reshape((2, total.shape[0] // 2) + total.shape[1:])
        summed = lax.psum_scatter(halves, "dp", scatter_dimension=1, tiled=True)
        ours = jnp.where(lower, summed[0], summed[1])
        theirs = jnp.where(lower, summed[1], summed[0]).astype(BF)
        pairs = [(i, i ^ 1) for i in range(lax.axis_size("section"))]
        results.append((ours + lax.ppermute(theirs, "section", pairs).astype(F32))[None])
    return results


def per_device(
    token_ids,
    timesteps,
    token_table,
    time_table,
    attn_gain,
    attn_shift,
    qkv_weight,
    query_bias,
    value_bias,
    proj_weight,
    proj_bias,
    mlp_gain,
    mlp_shift,
    up_weight,
    up_bias,
    down_weight,
    down_bias,
    cotangent,
):
    section = lax.axis_index("section")
    replica = lax.axis_index("dp")
    replicas = lax.axis_size("dp")
    rows, length = token_ids.shape
    width = cotangent.shape[2]
    half = width // 2
    layer = section // 2
    part = section % 2
    letters_count = token_table.shape[0]
    times_count = time_table.shape[0]
    padded = -(-letters_count // 16) * 16
    singles = (
        attn_gain,
        attn_shift,
        query_bias,
        value_bias,
        proj_bias,
        mlp_gain,
        mlp_shift,
        down_bias,
        up_bias,
    )
    cut = half // 8
    weights = (
        qkv_weight.reshape(4, 2, cut, 3 * width),
        proj_weight.reshape(4, 2, cut, width),
        up_weight.reshape(4, 2, cut, 4 * width),
        down_weight.reshape(4, 4, 2, cut, width),
    )
    vectors = 16
    fused = replicas == 8
    layers = run_layers(
        weights, singles, token_ids, token_table, timesteps, time_table, cotangent, replicas, fused
    )
    if fused:
        return run_finish(*layers, letters_count, times_count)
    act, sums, fixed, moving = layers
    qkv_grad, proj_grad, up_grad, down_grad = plain_reduce(fixed, moving, part == 0)
    activations = act.reshape(rows, length, width // 4).astype(F32)
    mine = jnp.zeros((2, vectors, width + 128), F32)
    mine = lax.dynamic_update_slice_in_dim(mine, sums[None, :vectors], layer, 0)
    placed = jnp.zeros((rows * replicas, width + 128), F32)
    placed = lax.dynamic_update_slice_in_dim(placed, sums[vectors + padded :], replica * rows, 0)
    joined = jnp.concatenate(
        [sums[vectors : vectors + padded], mine.reshape(2 * vectors, width + 128), placed], axis=0
    )
    joined = lax.psum(joined, ("section", "dp"))
    quarter = width // 4
    columns = lax.dynamic_slice_in_dim(joined, section * quarter, quarter, axis=1)
    token_grad = columns[:letters_count]
    first = padded + 2 * vectors
    steps = jnp.arange(times_count, dtype=jnp.int32).astype(F32)
    hot = (steps[:, None] == joined[first:, width][None, :]).astype(F32)
    time_grad = jnp.einsum("tb,bd->td", hot, columns[first:], precision=HIGHEST)
    ours = lax.dynamic_slice(joined, (padded + vectors * layer, part * half), (vectors, half))
    each = half // replicas
    flat = lax.dynamic_slice_in_dim(ours[:8], replica * each, each, axis=1)
    ups = lax.dynamic_slice_in_dim(ours[8:12].reshape(1, 4 * half), replica * 4 * each, 4 * each, axis=1)
    return (
        activations,
        token_grad,
        time_grad,
        flat[0:1],
        flat[1:2],
        qkv_grad,
        flat[2:3],
        flat[3:4],
        proj_grad,
        flat[4:5],
        flat[5:6],
        flat[6:7],
        up_grad,
        ups,
        down_grad,
        flat[7:8],
    )


def solution(mesh):
    return jax.shard_map(
        per_device,
        mesh=mesh,
        in_specs=(
            P("dp", None),
            P("dp"),
            P(),
            P(),
            P("section", None),
            P("section", None),
            P("section", None, None),
            P("section", None),
            P("section", None),
            P("section", None, None),
            P("section", None),
            P("section", None),
            P("section", None),
            P("section", None, None),
            P("section", None),
            P("section", None, None),
            P("section", None),
            P("dp", None, None),
        ),
        out_specs=(
            P("dp", None, "section"),
            P(None, "section"),
            P(None, "section"),
            P("section", "dp"),
            P("section", "dp"),
            P("section", "dp", None),
            P("section", "dp"),
            P("section", "dp"),
            P("section", "dp", None),
            P("section", "dp"),
            P("section", "dp"),
            P("section", "dp"),
            P("section", "dp", None),
            P("section", "dp"),
            P("section", "dp", None),
            P("section", "dp"),
        ),
        check_vma=False,
    )
```

```python
import functools
import math

import jax
import jax.numpy as jnp
from jax import lax
from jax.experimental import pallas as pl
from jax.experimental.pallas import tpu as pltpu
from jax.sharding import PartitionSpec as P

HEADS = 12
EPS = 1e-05
HIGHEST = lax.Precision.HIGHEST
MESH = pl.DeviceIdType.MESH
BF = jnp.bfloat16
F32 = jnp.float32
TILES = 12
QKV, PROJ, UP, DOWN = 0, 3, 4, 8
CHUNKS = 2 * TILES
LINE_FIRST = (1, 4, 7, 11)
CORE_LAG, X_LAG, Z_LAG, LINE_START, LINE_LAST = 2, 6, 2, 3, 28
BOTH_BY_X = 1
GELU_A = math.sqrt(2.0 / math.pi)
GELU_B = 0.044715


def flipped(value, bit):
    mask = 2**bit
    return value + mask - 2 * mask * lax.rem(lax.div(value, mask), 2)


def mul(a, b):
    return lax.dot_general(a, b, (((1,), (0,)), ((), ())), preferred_element_type=F32)


def mul_nt(a, b):
    return lax.dot_general(a, b, (((1,), (1,)), ((), ())), preferred_element_type=F32)


def mul_tn(a, b):
    return lax.dot_general(a, b, (((0,), (0,)), ((), ())), preferred_element_type=F32)


def normalize(x):
    mean = jnp.mean(x, axis=-1, keepdims=True)
    centered = x - mean
    spread = jnp.mean(centered * centered, axis=-1, keepdims=True)
    rate = lax.rsqrt(spread + EPS)
    return centered * rate, rate


def scaled_back(gh, gain, n, rate):
    gn = gh * gain
    inner = jnp.mean(gn * n, axis=-1, keepdims=True)
    return (gn - jnp.mean(gn, axis=-1, keepdims=True) - n * inner) * rate


def column(values):
    return jnp.sum(values, axis=0, keepdims=True)


class Refs:
    def __init__(self, names, refs):
        for name, ref in zip(names, refs, strict=True):
            setattr(self, name, ref)


INPUTS = (
    "qkv_in proj_in up_in down_in ga_in sa_in bq_in bv_in bo_in gm_in sm_in bdown_in bup_in "
    "ids_in table_in steps_in time_in cot_in"
).split()


def layer_kernel(seqs, length, width, fused, names, *all_refs):
    refs = Refs(names, all_refs)
    w, par, qkv, probs = refs.w, refs.par, refs.qkv, refs.probs
    acc, ybuf, ysend, y1 = refs.acc, refs.ybuf, refs.ysend, refs.y1
    xs = acc
    slope, gate, h_s, o_s, hf_s, go_s = refs.slope, refs.gate, refs.h_s, refs.o_s, refs.hf_s, refs.go_s
    act, landed, gsum = refs.act, refs.landed, refs.gsum
    s = lax.axis_index("section")
    d = lax.axis_index("dp")
    stage = lax.div(s, 2)
    part = lax.rem(s, 2)
    other = 1 - part
    core = lax.rem(d, 2)
    z = lax.div(d, 2)
    x_dev = (flipped(s, 0), d)
    y_dev = (flipped(s, 1), d)
    far_dev = (flipped(flipped(s, 0), 1), d)
    z_dev = (s, flipped(d, 1))
    c_dev = (s, flipped(d, 0))
    half = width // 2
    wide = width // 4
    hidden_half = 4 * half
    rows = w.shape[4]
    mine = lax.rem(d, 4)
    across = flipped(mine, 1)
    scale = 1.0 / math.sqrt(width // HEADS)
    letters_count = refs.table_in.shape[0]
    padded = refs.table.shape[0]
    vectors = 16
    count = vectors + padded
    nz = lax.axis_size("dp") // 2
    zbits = nz.bit_length() - 1
    ends = nz - 1

    def send(src, dst, send_sem, recv_sem, device):
        return pltpu.make_async_remote_copy(
            src_ref=src,
            dst_ref=dst,
            send_sem=send_sem,
            recv_sem=recv_sem,
            device_id=device,
            device_id_type=MESH,
        )

    def start(copies):
        for copy in copies:
            copy.start()

    def wait(copies):
        for copy in copies:
            copy.wait()

    def signal(sem, device):
        pl.semaphore_signal(sem, inc=1, device_id=device, device_id_type=MESH)

    barrier = pltpu.get_barrier_semaphore()
    greeted = [x_dev, y_dev, far_dev, c_dev, z_dev]
    if fused:
        greeted += [(s, flipped(d, 1 + bit)) for bit in range(1, zbits)]
    for device in greeted:
        signal(barrier, device)
    expected = len(greeted)
    if fused:
        middle_left = jnp.logical_and(z > 0, lax.rem(z, 2) == 0)
        middle_right = jnp.logical_and(z < ends, lax.rem(z, 2) == 1)

        @pl.when(middle_left)
        def _():
            signal(barrier, (s, d - 2))

        @pl.when(middle_right)
        def _():
            signal(barrier, (s, d + 2))

        expected = expected + middle_left.astype(jnp.int32) + middle_right.astype(jnp.int32)

    def tile(index):
        return w[index].reshape(width, width)

    def own_copies(index):
        if index < PROJ:
            pairs = [(refs.qkv_in.at[:, :, :, pl.ds(index * width, width)], w.at[index, part])]
        elif index < UP:
            pairs = [(refs.proj_in, w.at[index, part])]
        elif index < DOWN:
            pairs = [
                (
                    refs.up_in.at[:, :, :, pl.ds(side * hidden_half + (index - UP) * half, half)],
                    w.at[index, part, :, :, :, pl.ds(side * half, half)],
                )
                for side in range(2)
            ]
        else:
            pairs = [(refs.down_in.at[index - DOWN], w.at[index, part])]
        return [
            pltpu.make_async_copy(src, dst, refs.own_sem.at[2 * index + k])
            for k, (src, dst) in enumerate(pairs)
        ]

    def x_weight(index):
        place = w.at[index, part, mine]
        return send(place, place, refs.wx_send.at[index], refs.wx_recv.at[index], x_dev)

    def x_second(index):
        place = w.at[index, part, across]
        return send(place, place, refs.wz_send.at[index], refs.wz_recv.at[index], x_dev)

    def by_z(index):
        return index < TILES - BOTH_BY_X

    def relay(index, which, send_sem, recv_sem, device):
        place = w.at[index, other, which]
        return send(place, place, send_sem.at[index], recv_sem.at[index], device)

    def z_weight(index):
        return relay(index, mine, refs.wz_send, refs.wz_recv, z_dev)

    def c1_weight(index):
        return relay(index, mine, refs.c1_send, refs.c1_recv, c_dev)

    def c2_weight(index):
        return relay(index, across, refs.c2_send, refs.c2_recv, c_dev)

    def pass_first(index):
        relay(index, mine, refs.wx_send, refs.wx_recv, x_dev).wait_recv()

        @pl.when(by_z(index))
        def _():
            z_weight(index).start()

        c1_weight(index).start()

    def pass_second(index):
        relay(index, across, refs.wz_send, refs.wz_recv, z_dev).wait_recv()
        c2_weight(index).start()

    def ready(index):
        relay(index, flipped(mine, 0), refs.c1_send, refs.c1_recv, c_dev).wait_recv()
        relay(index, flipped(across, 0), refs.c2_send, refs.c2_recv, c_dev).wait_recv()

    def settle_weights():
        def settle(index, _):
            x_weight(index).wait_send()
            z_weight(index).wait_send()
            c1_weight(index).wait_send()
            c2_weight(index).wait_send()
            return 0

        lax.fori_loop(0, TILES, settle, 0)

    def vec_copy(which):
        place = refs.vecs.at[which]
        return send(place, place, refs.vec_sem.at[0], refs.vec_sem.at[1], x_dev)

    for index in range(TILES):
        start(own_copies(index))
    singles = ("ga", "sa", "bq", "bv", "bo", "gm", "sm", "bdown")
    for index, name in enumerate(singles):
        refs.vecs[part, index : index + 1, :] = getattr(refs, name + "_in")[...].astype(F32)
    for j in range(4):
        refs.vecs[part, 8 + j : 9 + j, :] = refs.bup_in[:, j * half : (j + 1) * half].astype(F32)
    refs.vecs[part, 12:16, :] = jnp.zeros((4, half), F32)
    refs.table[...] = jnp.zeros_like(refs.table)
    refs.table[:letters_count, :] = refs.table_in[...]
    gsum[...] = jnp.zeros_like(gsum)
    pl.semaphore_wait(barrier, expected)
    for index in range(TILES):
        wait(own_copies(index))
        x_weight(index).start()
        if not by_z(index):
            x_second(index).start()
        if index == 3:
            vec_copy(part).start()

    seats, times_count = refs.ids_in.shape[0], refs.time_in.shape[0]
    line = lax.broadcasted_iota(jnp.int32, (seats, times_count), 0)
    moment = jnp.zeros((seats, times_count), jnp.int32)
    for index in range(seats):
        moment = jnp.where(line == index, refs.steps_in[index], moment)
    hot = lax.broadcasted_iota(jnp.int32, (seats, times_count), 1) == moment
    refs.times[:, :width] = mul(hot.astype(F32).astype(BF), refs.time_in[...])
    refs.times[:, width:] = moment[:, :128].astype(F32)

    pass_first(0)
    pass_first(1)
    pass_second(0)
    pass_first(2)
    pass_second(1)
    pass_first(3)
    pass_second(2)
    pass_first(4)
    pass_second(3)
    pass_first(5)

    @pl.when(stage == 1)
    def _():
        def step(index, _):
            pass_second(index - 2)
            pass_first(index)
            return 0

        lax.fori_loop(6, TILES, step, 0)
        pass_second(TILES - 2)
        pass_second(TILES - 1)

    vec_copy(other).wait_recv()
    par[:, :half] = refs.vecs[0]
    par[:, half:] = refs.vecs[1]
    for index in range(UP):
        ready(index)

    def act_copies(i):
        slot = lax.rem(i, 2)
        return [
            send(
                act.at[slot, device[0]],
                landed.at[part, i],
                refs.act_send.at[i, index],
                refs.act_recv.at[part, i],
                device,
            )
            for index, device in enumerate((y_dev, x_dev, far_dev))
        ]

    def act_own(i):
        return pltpu.make_async_copy(act.at[lax.rem(i, 2), s], landed.at[part, i], refs.act_send.at[i, 3])

    def act_arrival(side, i):
        return send(act.at[0, 0], landed.at[side, i], refs.act_send.at[i, 0], refs.act_recv.at[side, i], y_dev)

    def act_settle(i):
        for copy in act_copies(i):
            copy.wait_send()

    def cot_copy(i):
        return pltpu.make_async_copy(refs.cot_in.at[part * seqs + i], ybuf.at[i], refs.cot_sem.at[i])

    def y_copy(i):
        return send(ysend.at[i], ybuf.at[i], refs.y_send.at[i], refs.y_recv.at[i], y_dev)

    def row(index):
        return par[index : index + 1, :]

    def add_row(index, values):
        gsum[index : index + 1, :width] += column(values)

    lane = lax.broadcasted_iota(jnp.int32, (length, 128), 1)
    low = lane < 64
    side_ones = [(lane < 64).astype(F32).astype(BF), (lane >= 64).astype(F32).astype(BF)]
    side_scaled = [
        ((lane < 64).astype(F32) * scale).astype(BF),
        ((lane >= 64).astype(F32) * scale).astype(BF),
    ]
    pairs = HEADS // 2

    def letters(i):
        ids = refs.ids_in[pl.ds(part * seqs + i, 1), :]
        place = lax.broadcasted_iota(jnp.int32, (padded, length), 0)
        return (place == ids).astype(F32).astype(BF)

    def attn_fwd(i):
        @pl.when(stage == 0)
        def _():
            xs[...] = mul_tn(letters(i), refs.table[...]) + refs.times[pl.ds(part * seqs + i, 1), :width]

        @pl.when(stage == 1)
        def _():
            y_copy(i).wait_recv()
            xs[...] = ybuf[i].astype(F32)
            cot_copy(i).start()

        n, rate = normalize(xs[...])
        refs.n_a[i] = n.astype(BF)
        refs.rates[i] = jnp.broadcast_to(rate, (length, 128))
        h_s[i] = (n * row(0) + row(1)).astype(BF)
        for j in range(3):
            joint = mul(h_s[i], tile(QKV + j))
            if j == 0:
                joint = joint + row(2)
            if j == 2:
                joint = joint + row(3)
            qkv[i, :, j * width : (j + 1) * width] = joint.astype(BF)

        for hp in range(pairs):
            at = hp * 128
            q2 = qkv[i, :, at : at + 128]
            k2 = qkv[i, :, width + at : width + at + 128]
            for side in range(2):
                scores = mul_nt(q2 * side_scaled[side], k2)
                expo = jnp.exp(scores - jnp.max(scores, axis=-1, keepdims=True))
                total = jnp.sum(expo, axis=-1, keepdims=True)
                probs[i, 2 * hp + side] = (expo * (1.0 / total)).astype(BF)
        for hp in range(pairs):
            at = hp * 128
            v2 = qkv[i, :, 2 * width + at : 2 * width + at + 128]
            outs = [mul(probs[i, 2 * hp + side], v2) for side in range(2)]
            o_s[i, :, at : at + 128] = jnp.where(low, outs[0], outs[1]).astype(BF)
        y1[i] = (xs[...] + (mul(o_s[i], tile(PROJ)) + row(4))).astype(BF)

    def feed_fwd(i):
        def arrived(first, last):
            @pl.when(i == 0)
            def _():
                def one(index, _):
                    ready(index)
                    return 0

                lax.fori_loop(first, last, one, 0)

        arrived(UP, TILES)
        x = y1[i].astype(F32)
        n, rate = normalize(x)
        refs.n_f[i] = n.astype(BF)
        refs.rates[i] = jnp.where(low, refs.rates[i], jnp.broadcast_to(rate, (length, 128)))
        hf_s[i] = (n * row(5) + row(6)).astype(BF)
        acc[...] = x + row(7)
        for j in range(4):
            u = mul(hf_s[i], tile(UP + j)) + row(8 + j)
            square = u * u
            t = jnp.tanh(u * (GELU_A + GELU_A * GELU_B * square))
            both = 0.5 + 0.5 * t
            gate[i, j] = (u * both).astype(BF)
            bend = (0.5 * GELU_A + 1.5 * GELU_A * GELU_B * square) * u
            slope[i, j] = (both + bend * (1.0 - t * t)).astype(BF)
        down = mul(gate[i, 0], tile(DOWN))
        for j in range(1, 4):
            down = down + mul(gate[i, j], tile(DOWN + j))
        acc[...] += down

        @pl.when(stage == 0)
        def _():
            ysend[i] = acc[...].astype(BF)
            y_copy(i).start()

        @pl.when(stage == 1)
        def _():
            @pl.when(i >= 2)
            def _():
                act_settle(i - 2)
                act_own(i - 2).wait()

            for q in range(4):
                act[lax.rem(i, 2), q] = acc[:, q * wide : (q + 1) * wide].astype(BF)
            start(act_copies(i))
            act_own(i).start()

    def feed_bwd(i):
        @pl.when(stage == 0)
        def _():
            y_copy(i).wait_recv()

        @pl.when(stage == 1)
        def _():
            cot_copy(i).wait()

        add_row(7, ybuf[i].astype(F32))
        for j in range(4):
            ga = mul_nt(ybuf[i], tile(DOWN + j))
            gu = (ga * slope[i, j].astype(F32)).astype(BF)
            slope[i, j] = gu
            add_row(8 + j, gu.astype(F32))
        gh = mul_nt(slope[i, 0], tile(UP))
        for j in range(1, 4):
            gh = gh + mul_nt(slope[i, j], tile(UP + j))
        n = refs.n_f[i].astype(F32)
        add_row(5, gh * n)
        add_row(6, gh)
        gx = ybuf[i].astype(F32) + scaled_back(gh, row(5), n, refs.rates[i][:, 64:65])
        y1[i] = gx.astype(BF)

    def attn_bwd(i):
        add_row(4, y1[i].astype(F32))
        go_s[...] = mul_nt(y1[i], tile(PROJ)).astype(BF)
        for hp in range(pairs):
            at = hp * 128
            v2 = qkv[i, :, 2 * width + at : 2 * width + at + 128]
            go2 = go_s[:, at : at + 128]
            gv = []
            for side in range(2):
                pb = probs[i, 2 * hp + side]
                gp = mul_nt(go2 * side_ones[side], v2)
                p = pb.astype(F32)
                pg = p * gp
                gs = (pg - p * jnp.sum(pg, axis=-1, keepdims=True)).astype(BF)
                gv.append(mul_tn(pb, go2))
                probs[i, 2 * hp + side] = gs
            qkv[i, :, 2 * width + at : 2 * width + at + 128] = jnp.where(low, gv[0], gv[1]).astype(BF)
        for hp in range(pairs):
            at = hp * 128
            q2 = qkv[i, :, at : at + 128]
            k2 = qkv[i, :, width + at : width + at + 128]
            gq, gk = [], []
            for side in range(2):
                gs = probs[i, 2 * hp + side]
                gq.append(mul(gs, k2))
                gk.append(mul_tn(gs, q2))
            qkv[i, :, at : at + 128] = (jnp.where(low, gq[0], gq[1]) * scale).astype(BF)
            qkv[i, :, width + at : width + at + 128] = (jnp.where(low, gk[0], gk[1]) * scale).astype(BF)
        pieces = [qkv[i, :, j * width : (j + 1) * width] for j in range(3)]
        add_row(2, pieces[0].astype(F32))
        add_row(3, pieces[2].astype(F32))
        gh = mul_nt(pieces[0], tile(QKV)) + mul_nt(pieces[1], tile(QKV + 1)) + mul_nt(pieces[2], tile(QKV + 2))
        n = refs.n_a[i].astype(F32)
        add_row(0, gh * n)
        add_row(1, gh)
        acc[...] = y1[i].astype(F32) + scaled_back(gh, row(0), n, refs.rates[i][:, 0:1])

        @pl.when(stage == 1)
        def _():
            ysend[i] = acc[...].astype(BF)
            y_copy(i).start()

        @pl.when(stage == 0)
        def _():
            high = acc[...].astype(BF)
            rest = (acc[...] - high.astype(F32)).astype(BF)
            hot = letters(i)
            gsum[vectors:count, :width] += mul(hot, high) + mul(hot, rest)
            mark = part * seqs + i
            stamp = refs.times[pl.ds(mark, 1), :]
            gsum[pl.ds(count + mark, 1), :] = jnp.concatenate([column(acc[...]), stamp[:, width:]], axis=1)

    units = (attn_fwd, feed_fwd, feed_bwd, attn_bwd)
    steps = 0
    if fused:
        step = reduce_steps(refs, seqs, length, width, send, signal, act_arrival, act_own, settle_weights)
        units = units + (step,)
        steps = CHUNKS + X_LAG + Z_LAG * ends

    def unit(u, _):
        early = u < 2 * seqs
        kind0 = jnp.where(early, lax.div(u, seqs), 2 + lax.rem(u, 2))
        index0 = jnp.where(early, lax.rem(u, seqs), lax.div(u, 2) - seqs)
        kind1 = lax.rem(u, 4)
        index1 = lax.div(u, 4)
        if fused:
            last = 4 * seqs - 1
            ahead = 4
            kind0 = jnp.where(u >= last, 4, kind0)
            index0 = jnp.where(u >= last, jnp.where(u < last + ahead, u - last, u - last - 1), index0)
            kind0 = jnp.where(u == last + ahead, 3, kind0)
            index0 = jnp.where(u == last + ahead, seqs - 1, index0)
            kind1 = jnp.where(u > last, 4, kind1)
            index1 = jnp.where(u > last, u - last - 1, index1)
        kind = jnp.where(stage == 0, kind0, kind1)
        i = jnp.where(stage == 0, index0, index1)

        @pl.when(jnp.logical_and(stage == 0, jnp.logical_and(u >= 1, u <= 4)))
        def _():
            pass_second(2 + 2 * u)
            pass_second(3 + 2 * u)

        @pl.when(jnp.logical_and(stage == 0, jnp.logical_and(u >= 1, u <= 3)))
        def _():
            pass_first(4 + 2 * u)
            pass_first(5 + 2 * u)

        for index, run in enumerate(units):

            @pl.when(kind == index)
            def _():
                run(i)

        return 0

    lax.fori_loop(0, 4 * seqs + steps, unit, 0)

    vec_copy(part).wait_send()
    if not fused:
        settle_weights()

    def finish(i, _):
        y_copy(i).wait_send()

        @pl.when(jnp.logical_and(stage == 1, i >= 2))
        def _():
            act_settle(i)

        return 0

    lax.fori_loop(0, seqs, finish, 0)
    if not fused:

        @pl.when(stage == 1)
        def _():
            for i in range(2, seqs):
                act_own(i).wait()

        for i in range(seqs):
            for side in range(2):

                @pl.when(jnp.logical_or(stage == 0, part != side))
                def _():
                    act_arrival(side, i).wait_recv()

        refs.sums_out[...] = gsum[...]
        copies = []
        for i in range(seqs):
            place = pl.ds(i * length, length)
            for index, ref in enumerate((hf_s, h_s, o_s, ybuf)):
                copies.append((ref.at[i], refs.fixed_out.at[index, place]))
            for j in range(4):
                copies.append((slope.at[i, j], refs.moving_out.at[j, place]))
                copies.append((gate.at[i, j], refs.moving_out.at[8 + j, place]))
            for j in range(3):
                copies.append((qkv.at[i, :, pl.ds(j * width, width)], refs.moving_out.at[4 + j, place]))
            copies.append((y1.at[i], refs.moving_out.at[7, place]))
        copies.append((landed, refs.act_out))
        copies = [
            pltpu.make_async_copy(src, dst, refs.keep_sem.at[index]) for index, (src, dst) in enumerate(copies)
        ]
        start(copies)
        wait(copies)


def reduce_steps(refs, seqs, length, width, send, signal, act_arrival, act_own, settle_weights):
    s = lax.axis_index("section")
    d = lax.axis_index("dp")
    stage = lax.div(s, 2)
    part = lax.rem(s, 2)
    other = 1 - part
    core = lax.rem(d, 2)
    z = lax.div(d, 2)
    x_dev = (flipped(s, 0), d)
    y_dev = (flipped(s, 1), d)
    c_dev = (s, flipped(d, 0))
    right_dev = (s, d + 2)
    left_dev = (s, d - 2)
    w, gsum = refs.w, refs.gsum
    nz = w.shape[2]
    rows = w.shape[4]
    ends = nz - 1
    slots = refs.x_buf.shape[0]
    core_slots = refs.core_buf.shape[0]
    directs = CHUNKS - len(LINE_FIRST)
    half = width // 2
    tokens = seqs * length
    core_buf, x_buf, right_buf, left_buf = refs.core_buf, refs.x_buf, refs.right_buf, refs.left_buf
    vectors = 16
    count = vectors + refs.table.shape[0]
    split = count // 2
    zbits = nz.bit_length() - 1
    own = gsum.shape[0] - count

    def where(tile):
        return jnp.where(tile < 4, tile + 4, jnp.where(tile < 8, tile - 4, tile))

    def at(k, *index):
        columns = pl.ds(pl.multiple_of(lax.rem(k, 2) * half, 128), half)
        return (where(lax.div(k, 2)),) + index + (slice(None), columns)

    everything = slice(None)

    def turned(k):
        return functools.reduce(jnp.logical_or, [k == chunk for chunk in LINE_FIRST])

    def direct(k):
        return jnp.logical_and(jnp.logical_and(k >= 0, k < CHUNKS), jnp.logical_not(turned(k)))

    def order(k):
        return k - sum((k > chunk).astype(jnp.int32) for chunk in LINE_FIRST)

    def slot(k):
        return lax.rem(order(k), slots)

    def core_slot(k):
        return lax.rem(k, core_slots)

    def core_copy(k):
        return send(
            w.at[at(k, everything, everything, 1 - core)],
            core_buf.at[core_slot(k)],
            refs.core_send.at[core_slot(k)],
            refs.core_recv.at[core_slot(k)],
            c_dev,
        )

    def x_copy(k):
        return send(
            w.at[at(k, other, everything, core)],
            x_buf.at[slot(k)],
            refs.x_send.at[slot(k)],
            refs.x_recv.at[slot(k)],
            x_dev,
        )

    class Line:
        def __init__(self, name, slot, side, spend_from, grant_to):
            self.right_buf = getattr(refs, name + "right_buf")
            self.left_buf = getattr(refs, name + "left_buf")
            self.right_sems = getattr(refs, name + "right_send"), getattr(refs, name + "right_recv")
            self.left_sems = getattr(refs, name + "left_send"), getattr(refs, name + "left_recv")
            self.right_credit = getattr(refs, name + "right_credit")
            self.left_credit = getattr(refs, name + "left_credit")
            self.slots = self.right_buf.shape[0]
            self.slot = lambda job: lax.rem(slot(job), self.slots)
            self.side = side
            self.spend_from = spend_from
            self.grant_to = grant_to

        def place(self, job, j):
            k, side = self.side(job)
            return at(k, side, j, core)

        def right_copy(self, job, j):
            sends, recvs = self.right_sems
            slot = self.slot(job)
            target = self.right_buf.at[slot, j]
            return send(w.at[self.place(job, j)], target, sends.at[slot, j], recvs.at[slot, j], right_dev)

        def left_copy(self, job, j):
            sends, recvs = self.left_sems
            slot = self.slot(job)
            target = self.left_buf.at[slot, j]
            return send(w.at[self.place(job, j)], target, sends.at[slot, j], recvs.at[slot, j], left_dev)

        def add(self, job, j, buffer):
            both = w[self.place(job, j)].astype(F32) + buffer[self.slot(job), j].astype(F32)
            w[self.place(job, j)] = both.astype(BF)

        def right_step(self, job):
            @pl.when(jnp.logical_and(z < ends, self.spend_from(job)))
            def _():
                pl.semaphore_wait(self.right_credit, 1)

            for j in range(ends, -1, -1):

                @pl.when(jnp.logical_and(z > 0, j >= z))
                def _():
                    self.right_copy(job, j).wait_recv()
                    self.add(job, j, self.right_buf)

                @pl.when(jnp.logical_and(j > z, self.spend_from(job)))
                def _():
                    self.right_copy(job, j).wait_send()

                @pl.when(j > z)
                def _():
                    self.right_copy(job, j).start()

            @pl.when(jnp.logical_and(z > 0, self.grant_to(job)))
            def _():
                signal(self.right_credit, left_dev)

        def left_step(self, job):
            @pl.when(jnp.logical_and(z > 0, self.spend_from(job)))
            def _():
                pl.semaphore_wait(self.left_credit, 1)

            for j in range(nz):

                @pl.when(jnp.logical_and(z < ends, j <= z))
                def _():
                    self.left_copy(job, j).wait_recv()
                    self.add(job, j, self.left_buf)

                @pl.when(jnp.logical_and(j < z, self.spend_from(job)))
                def _():
                    self.left_copy(job, j).wait_send()

                @pl.when(j < z)
                def _():
                    self.left_copy(job, j).start()

            @pl.when(jnp.logical_and(z < ends, self.grant_to(job)))
            def _():
                signal(self.left_credit, right_dev)

        def settle(self, job):
            for j in range(nz):

                @pl.when(j > z)
                def _():
                    self.right_copy(job, j).wait_send()

                @pl.when(j < z)
                def _():
                    self.left_copy(job, j).wait_send()

    line_slots = refs.right_buf.shape[0]
    main = Line(
        "",
        order,
        lambda k: (k, part),
        lambda k: order(k) >= line_slots,
        lambda k: order(k) + line_slots < directs,
    )
    side_jobs = 2 * len(LINE_FIRST)
    side_slots = refs.b_right_buf.shape[0]

    def side_place(job):
        chunk = jnp.int32(LINE_FIRST[-1])
        for index in range(len(LINE_FIRST) - 1, -1, -1):
            chunk = jnp.where(job < 2 * (index + 1), LINE_FIRST[index], chunk)
        return chunk, lax.rem(job, 2)

    beside = Line(
        "b_",
        lambda job: job,
        side_place,
        lambda job: job >= side_slots,
        lambda job: job + side_slots < side_jobs,
    )

    def grads_copy(k):
        return pltpu.make_async_copy(refs.grad_stage, refs.grads_out.at[k], refs.out_sem.at[0])

    def act_copy(turn):
        return pltpu.make_async_copy(refs.act_stage, refs.act_out.at[turn], refs.out_sem.at[1])

    def put_grads(k, value):
        @pl.when(k > 0)
        def _():
            grads_copy(k).wait()

        refs.grad_stage[...] = value
        grads_copy(k).start()

    def last_copy(index):
        k = jnp.int32(LINE_FIRST[index])
        return send(
            w.at[at(k, other, z, core)],
            refs.last_buf.at[index],
            refs.last_send.at[index],
            refs.last_recv.at[index],
            x_dev,
        )

    def put_last(index):
        k = jnp.int32(LINE_FIRST[index])
        last_copy(index).wait_recv()
        put_grads(k, w[at(k, part, z, core)].astype(F32) + refs.last_buf[index].astype(F32))

    def flat(value):
        return value.reshape(tokens, width)

    def store(k, value):
        w[where(k)] = value.astype(BF).reshape(2, nz, 2, rows, width)

    def products(tile):
        @pl.when(tile < 4)
        def _():
            store(tile, mul_tn(flat(refs.hf_s[...]), flat(refs.slope[:, tile])))

        for j in range(3):

            @pl.when(tile == 4 + j)
            def _():
                store(tile, mul_tn(flat(refs.h_s[...]), flat(refs.qkv[:, :, j * width : (j + 1) * width])))

        @pl.when(tile == 7)
        def _():
            store(tile, mul_tn(flat(refs.o_s[...]), flat(refs.y1[...])))

        @pl.when(jnp.logical_and(tile >= 4, tile < 8))
        def _():
            value = mul_tn(flat(refs.gate[:, tile - 4]), flat(refs.ybuf[...])).astype(BF)
            value = value.reshape(2, 2, 4, rows, width)
            for block in range(4):
                w[8 + block, :, tile - 4] = value[:, :, block]

    def inside(k):
        return jnp.logical_and(k >= 0, k < CHUNKS)

    def core_sums():
        return send(
            gsum.at[pl.ds(0, count)], refs.sums_buf, refs.sums_sem.at[0], refs.sums_sem.at[1], c_dev
        )

    def x_sums():
        return [
            send(refs.adds.at[0], refs.adds_buf.at[0], refs.adds_send.at[0], refs.adds_recv.at[0], x_dev),
            send(
                gsum.at[pl.ds(count, own)],
                refs.stamp_buf,
                refs.stamp_send.at[0],
                refs.stamp_recv.at[0],
                x_dev,
            ),
        ]

    def block(bit, place_core, place_z):
        size = own * 2**bit
        first = place_core * nz * own + lax.div(place_z, 2**bit) * size
        return pl.ds(pl.multiple_of(first, 8), size)

    def z_sums(bit, arriving):
        there = flipped(z, bit)
        place = refs.stamps.at[block(bit, core, there if arriving else z)]
        device = (s, flipped(d, 1 + bit))
        return [
            send(
                refs.adds.at[1 + bit],
                refs.adds_buf.at[1 + bit],
                refs.adds_send.at[1 + bit],
                refs.adds_recv.at[1 + bit],
                device,
            ),
            send(place, place, refs.stamp_send.at[1 + bit], refs.stamp_recv.at[1 + bit], device),
        ]

    def last_sums(arriving):
        side = 1 - core if arriving else core
        place = refs.stamps.at[block(zbits, side, z)]
        half_sums = refs.whole.at[side]
        return [
            send(half_sums, half_sums, refs.sums_sem.at[2], refs.sums_sem.at[3], c_dev),
            send(place, place, refs.stamp_send.at[1 + zbits], refs.stamp_recv.at[1 + zbits], c_dev),
        ]

    def final_copies():
        return [
            send(src, dst, refs.final_send.at[index], refs.final_recv.at[index], y_dev)
            for index, (src, dst) in enumerate(((refs.whole, refs.token_out), (refs.stamps, refs.stamp_out)))
        ]

    def arrive(copies):
        for copy in copies:
            copy.wait_recv()

    def begin(copies):
        for copy in copies:
            copy.start()

    def small_step(t):
        @pl.when(t == 5)
        def _():
            core_sums().start()

        @pl.when(t == 8)
        def _():
            core_sums().wait_recv()
            sums = gsum[:count, :width] + refs.sums_buf[:, :width]

            @pl.when(core == 0)
            def _():
                refs.adds[0] = sums[:split]

            @pl.when(core == 1)
            def _():
                refs.adds[0] = sums[split:]

            begin(x_sums())

        @pl.when(t == 12)
        def _():
            arrive(x_sums())
            refs.adds[1] = refs.adds[0] + refs.adds_buf[0]
            refs.stamps[block(0, core, z), :] = gsum[count:, :] + refs.stamp_buf[...]
            begin(z_sums(0, False))

        for bit in range(zbits):

            @pl.when(t == 16 + 4 * bit)
            def _():
                arrive(z_sums(bit, True))
                total = refs.adds[1 + bit] + refs.adds_buf[1 + bit]
                if bit + 1 < zbits:
                    refs.adds[2 + bit] = total
                    begin(z_sums(bit + 1, False))
                else:
                    refs.whole[core] = total
                    begin(last_sums(False))

        @pl.when(t == 16 + 4 * zbits)
        def _():
            arrive(last_sums(True))
            refs.small_out[...] = refs.whole[...]

            @pl.when(stage == 0)
            def _():
                begin(final_copies())
                refs.token_out[...] = refs.whole[...]
                refs.stamp_out[...] = refs.stamps[...]

    def act_step(t):
        turn = t - 6

        @pl.when(jnp.logical_and(turn >= 0, turn < 2 * seqs))
        def _():
            side = lax.div(turn, seqs)
            i = lax.rem(turn, seqs)
            ours = jnp.logical_and(stage == 1, side == part)

            @pl.when(jnp.logical_not(ours))
            def _():
                act_arrival(side, i).wait_recv()

            @pl.when(jnp.logical_and(ours, i >= 2))
            def _():
                act_own(i).wait()

            @pl.when(turn > 0)
            def _():
                act_copy(turn - 1).wait()

            refs.act_stage[...] = refs.landed[side, i].astype(F32).T
            act_copy(turn).start()

    def step(t):
        @pl.when(t == 0)
        def _():
            settle_weights()

        @pl.when(jnp.logical_and(lax.rem(t, 2) == 0, t < 16))
        def _():
            products(lax.div(t, 2))

        @pl.when(t < CHUNKS)
        def _():
            @pl.when(t >= core_slots)
            def _():
                pl.semaphore_wait(refs.core_credit, 1)
                core_copy(t).wait_send()

            core_copy(t).start()

        k1 = t - CORE_LAG

        @pl.when(inside(k1))
        def _():
            core_copy(k1).wait_recv()
            for side in range(2):
                place = at(k1, side, everything, core)
                both = w[place].astype(F32) + core_buf[core_slot(k1), side].astype(F32)
                w[place] = both.astype(BF)

            @pl.when(k1 + core_slots < CHUNKS)
            def _():
                signal(refs.core_credit, c_dev)

        @pl.when(direct(k1))
        def _():
            @pl.when(order(k1) >= slots)
            def _():
                pl.semaphore_wait(refs.x_credit, 1)
                x_copy(k1).wait_send()

            x_copy(k1).start()

        small_step(t)
        act_step(t)
        k2 = t - X_LAG

        @pl.when(direct(k2))
        def _():
            x_copy(k2).wait_recv()
            place = at(k2, part, everything, core)
            both = w[place].astype(F32) + x_buf[slot(k2)].astype(F32)
            w[place] = both.astype(BF)

            @pl.when(order(k2) + slots < directs)
            def _():
                signal(refs.x_credit, x_dev)

        k3 = t - X_LAG - Z_LAG * z
        k4 = t - X_LAG - Z_LAG * (ends - z)
        k5 = jnp.minimum(k3, k4)

        @pl.when(direct(k3))
        def _():
            main.right_step(k3)

        @pl.when(direct(k4))
        def _():
            main.left_step(k4)

        @pl.when(direct(k5))
        def _():
            put_grads(k5, w[main.place(k5, z)].astype(F32))

        def listed(turn):
            even = lax.rem(turn + 64, 2) == 0
            return jnp.logical_and(even, jnp.logical_and(turn >= 0, turn < 2 * side_jobs))

        j3 = t - LINE_START - Z_LAG * z
        j4 = t - LINE_START - Z_LAG * (ends - z)

        @pl.when(listed(j3))
        def _():
            beside.right_step(lax.div(j3, 2))

        @pl.when(listed(j4))
        def _():
            beside.left_step(lax.div(j4, 2))

        @pl.when(t == LINE_LAST)
        def _():
            for index in range(len(LINE_FIRST)):
                last_copy(index).start()

        @pl.when(t == CHUNKS + X_LAG + Z_LAG * ends - 1)
        def _():
            for index in range(len(LINE_FIRST)):
                put_last(index)
            finish()

    def finish():
        def settle_core(k, _):
            core_copy(k).wait_send()
            return 0

        def settle_x(k, _):
            x_copy(k).wait_send()
            return 0

        def settle_main(k, _):
            main.settle(k)
            return 0

        def settle_beside(job, _):
            beside.settle(job)
            return 0

        lax.fori_loop(CHUNKS - core_slots, CHUNKS, settle_core, 0)
        lax.fori_loop(CHUNKS - slots, CHUNKS, settle_x, 0)
        lax.fori_loop(CHUNKS - line_slots, CHUNKS, settle_main, 0)
        lax.fori_loop(side_jobs - side_slots, side_jobs, settle_beside, 0)
        for index in range(len(LINE_FIRST)):
            last_copy(index).wait_send()
        grads_copy(0).wait()
        act_copy(2 * seqs - 1).wait()
        sends = [core_sums()] + x_sums() + last_sums(False)
        for bit in range(zbits):
            sends += z_sums(bit, False)
        for copy in sends:
            copy.wait_send()

        @pl.when(stage == 0)
        def _():
            for copy in final_copies():
                copy.wait_send()

        @pl.when(stage == 1)
        def _():
            arrive(final_copies())

    return step


def run_layers(weights, singles, ids, table, steps, times, cot, replicas, fused):
    rows, length = ids.shape
    width = cot.shape[2]
    half = width // 2
    seqs = rows // 2
    tokens = seqs * length
    padded = -(-table.shape[0] // 16) * 16
    count = 16 + padded
    nz = replicas // 2
    lane = width + 128
    cut = half // 8
    dma = pltpu.SemaphoreType.DMA
    credit = pltpu.SemaphoreType.REGULAR
    anywhere = pl.BlockSpec(memory_space=pl.ANY)
    local = pl.BlockSpec(memory_space=pltpu.VMEM)
    vm = pltpu.VMEM
    shape = jax.ShapeDtypeStruct
    if fused:
        outs = {
            "act_out": (shape((2 * seqs, width // 4, length), F32), anywhere),
            "grads_out": (shape((CHUNKS, cut, half), F32), anywhere),
            "small_out": (shape((2, count // 2, width), F32), local),
            "token_out": (shape((2, count // 2, width), F32), local),
            "stamp_out": (shape((rows * replicas, lane), F32), local),
        }
    else:
        outs = {
            "act_out": (shape((2, seqs, length, width // 4), BF), anywhere),
            "sums_out": (shape((count + rows, lane), F32), local),
            "fixed_out": (shape((4, tokens, width), BF), anywhere),
            "moving_out": (shape((12, tokens, width), BF), anywhere),
        }
    scratch = {
        "w": vm((TILES, 2, 4, 2, cut, width), BF),
        "vecs": vm((2, 16, half), F32),
        "table": vm((padded, width), BF),
        "par": vm((16, width), F32),
        "times": vm((rows, lane), F32),
        "acc": vm((length, width), F32),
        "n_a": vm((seqs, length, width), BF),
        "n_f": vm((seqs, length, width), BF),
        "rates": vm((seqs, length, 128), F32),
        "qkv": vm((seqs, length, 3 * width), BF),
        "probs": vm((seqs, HEADS, length, length), BF),
        "y1": vm((seqs, length, width), BF),
        "slope": vm((seqs, 4, length, width), BF),
        "gate": vm((seqs, 4, length, width), BF),
        "h_s": vm((seqs, length, width), BF),
        "o_s": vm((seqs, length, width), BF),
        "hf_s": vm((seqs, length, width), BF),
        "go_s": vm((length, width), BF),
        "ybuf": vm((seqs, length, width), BF),
        "ysend": vm((seqs, length, width), BF),
        "act": vm((2, 4, length, width // 4), BF),
        "landed": vm((2, seqs, length, width // 4), BF),
        "gsum": vm((count + rows, lane), F32),
        "own_sem": dma((2 * TILES,)),
        "vec_sem": dma((2,)),
        "cot_sem": dma((seqs,)),
        "y_send": dma((seqs,)),
        "y_recv": dma((seqs,)),
        "act_send": dma((seqs, 4)),
        "act_recv": dma((2, seqs)),
    }
    for name in ("wx", "wz", "c1", "c2"):
        scratch[name + "_send"] = dma((TILES,))
        scratch[name + "_recv"] = dma((TILES,))
    if fused:
        zbits = nz.bit_length() - 1
        scratch |= {
            "core_buf": vm((3, 2, nz, cut, half), BF),
            "x_buf": vm((X_LAG, nz, cut, half), BF),
            "right_buf": vm((4, nz, cut, half), BF),
            "left_buf": vm((4, nz, cut, half), BF),
            "b_right_buf": vm((2, nz, cut, half), BF),
            "b_left_buf": vm((2, nz, cut, half), BF),
            "last_buf": vm((len(LINE_FIRST), cut, half), BF),
            "last_send": dma((len(LINE_FIRST),)),
            "last_recv": dma((len(LINE_FIRST),)),
            "sums_buf": vm((count, lane), F32),
            "adds": vm((1 + zbits, count // 2, width), F32),
            "adds_buf": vm((1 + zbits, count // 2, width), F32),
            "whole": vm((2, count // 2, width), F32),
            "stamp_buf": vm((rows, lane), F32),
            "stamps": vm((rows * replicas, lane), F32),
            "grad_stage": vm((cut, half), F32),
            "act_stage": vm((width // 4, length), F32),
            "out_sem": dma((2,)),
            "sums_sem": dma((4,)),
            "adds_send": dma((1 + zbits,)),
            "adds_recv": dma((1 + zbits,)),
            "stamp_send": dma((2 + zbits,)),
            "stamp_recv": dma((2 + zbits,)),
            "final_send": dma((2,)),
            "final_recv": dma((2,)),
            "core_credit": credit,
            "x_credit": credit,
            "right_credit": credit,
            "left_credit": credit,
            "b_right_credit": credit,
            "b_left_credit": credit,
        }
        for name in ("core", "x"):
            slots = scratch[name + "_buf"].shape[0]
            scratch[name + "_send"] = dma((slots,))
            scratch[name + "_recv"] = dma((slots,))
        for name in ("right", "left", "b_right", "b_left"):
            slots = scratch[name + "_buf"].shape[0]
            scratch[name + "_send"] = dma((slots, nz))
            scratch[name + "_recv"] = dma((slots, nz))
    else:
        scratch["keep_sem"] = dma((16 * seqs + 1,))
    names = INPUTS + list(outs) + list(scratch)
    return pl.pallas_call(
        functools.partial(layer_kernel, seqs, length, width, fused, names),
        out_shape=tuple(out[0] for out in outs.values()),
        in_specs=[anywhere] * 4
        + [local] * 11
        + [pl.BlockSpec(memory_space=pltpu.SMEM), local, anywhere],
        out_specs=tuple(out[1] for out in outs.values()),
        scratch_shapes=list(scratch.values()),
        compiler_params=pltpu.CompilerParams(
            collective_id=0, has_side_effects=True, vmem_limit_bytes=64 * 2**20 - 2**17
        ),
    )(*weights, *singles, ids, table, steps, times, cot)


def three_parts(value):
    first = value.astype(BF)
    rest = value - first.astype(F32)
    second = rest.astype(BF)
    return first, second, (rest - second.astype(F32)).astype(BF)


def finish_kernel(
    act,
    grads,
    small,
    token,
    stamp,
    act_out,
    token_out,
    time_out,
    ga_out,
    sa_out,
    qkv_out,
    bq_out,
    bv_out,
    proj_out,
    bo_out,
    gm_out,
    sm_out,
    up_out,
    bup_out,
    down_out,
    bdown_out,
    act_s,
    grads_s,
    sem,
):
    s = lax.axis_index("section")
    d = lax.axis_index("dp")
    part = lax.rem(s, 2)
    rows, half = grads.shape[1:]
    width = 2 * half
    quarter = width // 4
    thirds = [pl.ds(8 * index, 8) for index in range(3)]
    loads = [
        pltpu.make_async_copy(src, dst, sem.at[25 + index])
        for index, (src, dst) in enumerate(
            [(grads.at[third], grads_s.at[third]) for third in thirds] + [(act, act_s)]
        )
    ]
    for copy in loads:
        copy.start()
    pairs = [[], [], [], [(act_s, act_out)]]
    for side in range(2):
        for j in range(4):
            columns = pl.ds(side * 4 * half + j * half, half)
            pairs[0].append((grads_s.at[2 * j + side], up_out.at[0, :, columns]))
        for j in range(3):
            columns = pl.ds(j * width + side * half, half)
            pairs[1].append((grads_s.at[8 + 2 * j + side], qkv_out.at[0, :, columns]))
        columns = pl.ds(side * half, half)
        pairs[1].append((grads_s.at[14 + side], proj_out.at[0, :, columns]))
        for j in range(4):
            pairs[2].append((grads_s.at[16 + 2 * j + side], down_out.at[0, pl.ds(j * rows, rows), columns]))
    copies = []
    for load, group in zip(loads, pairs):
        load.wait()
        for src, dst in group:
            copies.append(pltpu.make_async_copy(src, dst, sem.at[len(copies)]))
            copies[-1].start()
    vectors = small[0, :16, :]
    lower = jnp.where(part == 0, vectors[:, :half], vectors[:, half:])
    turned = pltpu.roll(lower, lax.rem(half - d * rows, half), 1)
    outs = (ga_out, sa_out, bq_out, bv_out, bo_out, gm_out, sm_out, bdown_out)
    for index, out in enumerate(outs):
        out[...] = turned[index : index + 1, :rows]
    per_row = half // (4 * rows)
    shifted = pltpu.roll(lower, lax.rem(half - lax.rem(d, per_row) * 4 * rows, half), 1)
    for j in range(4):

        @pl.when(lax.div(d, per_row) == j)
        def _():
            bup_out[...] = shifted[8 + j : 9 + j, : 4 * rows]

    times_count = time_out.shape[1]
    spread = -(-times_count // 128) * 128
    place = lax.broadcasted_iota(jnp.int32, (stamp.shape[0], spread), 1).astype(F32)
    hot = (place == stamp[:, width : width + 1]).astype(F32).astype(BF)
    letters = token_out.shape[0]
    split = token.shape[1]
    for q in range(4):

        @pl.when(s == q)
        def _():
            at = slice(q * quarter, (q + 1) * quarter)
            token_out[: split - 16, :] = token[0, 16:, at]
            token_out[split - 16 :, :] = token[1, : letters + 16 - split, at]
            sums = jnp.zeros((quarter, spread), F32)
            for piece in three_parts(stamp[:, at]):
                sums = sums + mul_tn(piece, hot)
            time_out[...] = sums[:, :times_count]

    for copy in copies:
        copy.wait()


def run_finish(act, grads, small, token, stamp, letters_count, times_count):
    rows, half = grads.shape[1:]
    width = 2 * half
    quarter = width // 4
    local = pl.BlockSpec(memory_space=pltpu.VMEM)
    anywhere = pl.BlockSpec(memory_space=pl.ANY)
    single = (1, rows)
    shapes = [
        (act.shape, anywhere),
        ((letters_count, quarter), local),
        ((quarter, times_count), local),
        (single, local),
        (single, local),
        ((1, rows, 3 * width), anywhere),
        (single, local),
        (single, local),
        ((1, rows, width), anywhere),
        (single, local),
        (single, local),
        (single, local),
        ((1, rows, 4 * width), anywhere),
        ((1, 4 * rows), local),
        ((1, 4 * rows, width), anywhere),
        (single, local),
    ]
    outs = pl.pallas_call(
        finish_kernel,
        out_shape=tuple(jax.ShapeDtypeStruct(shape, F32) for shape, _ in shapes),
        in_specs=[anywhere] * 2 + [local] * 3,
        out_specs=tuple(spec for _, spec in shapes),
        scratch_shapes=[
            pltpu.VMEM(act.shape, F32),
            pltpu.VMEM(grads.shape, F32),
            pltpu.SemaphoreType.DMA((29,)),
        ],
        compiler_params=pltpu.CompilerParams(vmem_limit_bytes=62 * 2**20),
    )(act, grads, small, token, stamp)
    return (jnp.swapaxes(outs[0], 1, 2), outs[1], jnp.swapaxes(outs[2], 0, 1)) + tuple(outs[3:])


def plain_reduce(fixed, moving, lower):
    def grad(left, right):
        return jnp.einsum("tk,tn->kn", left, right, preferred_element_type=F32)

    width = fixed.shape[2]
    half = width // 2
    hf, h, o, gz = (fixed[index] for index in range(4))
    ups = jnp.stack([grad(hf, moving[j]) for j in range(4)])
    up = ups.reshape(4, width, 2, half).transpose(1, 2, 0, 3).reshape(width, 4 * width)
    joint = jnp.concatenate([grad(h, moving[4 + j]) for j in range(3)], axis=1)
    proj = grad(o, moving[7])
    downs = jnp.stack([grad(moving[8 + j], gz) for j in range(4)])
    down = downs.reshape(4, 2, half, width).transpose(1, 0, 2, 3).reshape(4 * width, width)
    results = []
    for total in (joint, proj, up, down):
        halves = total.reshape((2, total.shape[0] // 2) + total.shape[1:])
        summed = lax.psum_scatter(halves, "dp", scatter_dimension=1, tiled=True)
        ours = jnp.where(lower, summed[0], summed[1])
        theirs = jnp.where(lower, summed[1], summed[0]).astype(BF)
        pairs = [(i, i ^ 1) for i in range(lax.axis_size("section"))]
        results.append((ours + lax.ppermute(theirs, "section", pairs).astype(F32))[None])
    return results


def per_device(
    token_ids,
    timesteps,
    token_table,
    time_table,
    attn_gain,
    attn_shift,
    qkv_weight,
    query_bias,
    value_bias,
    proj_weight,
    proj_bias,
    mlp_gain,
    mlp_shift,
    up_weight,
    up_bias,
    down_weight,
    down_bias,
    cotangent,
):
    section = lax.axis_index("section")
    replica = lax.axis_index("dp")
    replicas = lax.axis_size("dp")
    rows, length = token_ids.shape
    width = cotangent.shape[2]
    half = width // 2
    layer = section // 2
    part = section % 2
    letters_count = token_table.shape[0]
    times_count = time_table.shape[0]
    padded = -(-letters_count // 16) * 16
    singles = (
        attn_gain,
        attn_shift,
        query_bias,
        value_bias,
        proj_bias,
        mlp_gain,
        mlp_shift,
        down_bias,
        up_bias,
    )
    cut = half // 8
    weights = (
        qkv_weight.reshape(4, 2, cut, 3 * width),
        proj_weight.reshape(4, 2, cut, width),
        up_weight.reshape(4, 2, cut, 4 * width),
        down_weight.reshape(4, 4, 2, cut, width),
    )
    vectors = 16
    fused = replicas == 8
    layers = run_layers(
        weights, singles, token_ids, token_table, timesteps, time_table, cotangent, replicas, fused
    )
    if fused:
        return run_finish(*layers, letters_count, times_count)
    act, sums, fixed, moving = layers
    qkv_grad, proj_grad, up_grad, down_grad = plain_reduce(fixed, moving, part == 0)
    activations = act.reshape(rows, length, width // 4).astype(F32)
    mine = jnp.zeros((2, vectors, width + 128), F32)
    mine = lax.dynamic_update_slice_in_dim(mine, sums[None, :vectors], layer, 0)
    placed = jnp.zeros((rows * replicas, width + 128), F32)
    placed = lax.dynamic_update_slice_in_dim(placed, sums[vectors + padded :], replica * rows, 0)
    joined = jnp.concatenate(
        [sums[vectors : vectors + padded], mine.reshape(2 * vectors, width + 128), placed], axis=0
    )
    joined = lax.psum(joined, ("section", "dp"))
    quarter = width // 4
    columns = lax.dynamic_slice_in_dim(joined, section * quarter, quarter, axis=1)
    token_grad = columns[:letters_count]
    first = padded + 2 * vectors
    steps = jnp.arange(times_count, dtype=jnp.int32).astype(F32)
    hot = (steps[:, None] == joined[first:, width][None, :]).astype(F32)
    time_grad = jnp.einsum("tb,bd->td", hot, columns[first:], precision=HIGHEST)
    ours = lax.dynamic_slice(joined, (padded + vectors * layer, part * half), (vectors, half))
    each = half // replicas
    flat = lax.dynamic_slice_in_dim(ours[:8], replica * each, each, axis=1)
    ups = lax.dynamic_slice_in_dim(ours[8:12].reshape(1, 4 * half), replica * 4 * each, 4 * each, axis=1)
    return (
        activations,
        token_grad,
        time_grad,
        flat[0:1],
        flat[1:2],
        qkv_grad,
        flat[2:3],
        flat[3:4],
        proj_grad,
        flat[4:5],
        flat[5:6],
        flat[6:7],
        up_grad,
        ups,
        down_grad,
        flat[7:8],
    )


def solution(mesh):
    return jax.shard_map(
        per_device,
        mesh=mesh,
        in_specs=(
            P("dp", None),
            P("dp"),
            P(),
            P(),
            P("section", None),
            P("section", None),
            P("section", None, None),
            P("section", None),
            P("section", None),
            P("section", None, None),
            P("section", None),
            P("section", None),
            P("section", None),
            P("section", None, None),
            P("section", None),
            P("section", None, None),
            P("section", None),
            P("dp", None, None),
        ),
        out_specs=(
            P("dp", None, "section"),
            P(None, "section"),
            P(None, "section"),
            P("section", "dp"),
            P("section", "dp"),
            P("section", "dp", None),
            P("section", "dp"),
            P("section", "dp"),
            P("section", "dp", None),
            P("section", "dp"),
            P("section", "dp"),
            P("section", "dp"),
            P("section", "dp", None),
            P("section", "dp"),
            P("section", "dp", None),
            P("section", "dp"),
        ),
        check_vma=False,
    )
```
